32 devices in a mesh: cell: 4 (over z), gene: 8 (over y, x, core).
Axes of the slice: x: 2, y: 2, z: 4, core: 2. Of those that a mesh axis runs over, the one named last changes fastest.
Arguments:
- genes: bfloat16 [4, 1024, 1120], P('cell', 'gene'), may hold values from -30 to 30
- prefix: bfloat16 [4, 64, 1120], P('cell'), may hold values from -30 to 30
- cot_genes: float32 [4, 1024, 1120], P('cell', 'gene'), may hold values from -6 to 6
- cot_prefix: float32 [4, 64, 1120], P('cell', 'gene'), may hold values from -6 to 6
- w_qkv: bfloat16 [2, 1120, 3360], P(None, 'gene'), may hold values from -0.25 to 0.25
- w_out: bfloat16 [2, 1120, 1120], P(None, 'gene'), may hold values from -0.75 to 0.75
- w_up: bfloat16 [2, 1120, 4480], P(None, 'gene'), may hold values from -0.1875 to 0.1875
- w_down: bfloat16 [2, 4480, 1120], P(None, 'gene'), may hold values from -0.09375 to 0.09375
- norm1_gain: float32 [2, 1120], replicated, may hold values from 0.5 to 1.5
- norm1_bias: float32 [2, 1120], replicated, may hold values from -3 to 3
- norm2_gain: float32 [2, 1120], replicated, may hold values from 0.5 to 1.5
- norm2_bias: float32 [2, 1120], replicated, may hold values from -3 to 3
- bias_q: float32 [2, 1120], replicated, may hold values from -3 to 3
- bias_v: float32 [2, 1120], replicated, may hold values from -3 to 3
- bias_out: float32 [2, 1120], replicated, may hold values from -3 to 3
- bias_up: float32 [2, 4480], replicated, may hold values from -3 to 3
- bias_down: float32 [2, 1120], replicated, may hold values from -3 to 3
Outputs:
- out_genes: float32 [4, 1024, 1120], P('cell', 'gene')
- out_prefix: float32 [4, 64, 1120], P('cell', 'gene')
- grad_genes: float32 [4, 1024, 1120], P('cell', 'gene')
- grad_prefix: float32 [4, 64, 1120], P('cell', 'gene')
- grad_w_qkv: float32 [2, 1120, 3360], P(None, 'gene')
- grad_w_out: float32 [2, 1120, 1120], P(None, 'gene')
- grad_w_up: float32 [2, 1120, 4480], P(None, 'gene')
- grad_w_down: float32 [2, 4480, 1120], P(None, 'gene')
- grad_norm1_gain: float32 [2, 1120], P(None, 'gene')
- grad_norm1_bias: float32 [2, 1120], P(None, 'gene')
- grad_norm2_gain: float32 [2, 1120], P(None, 'gene')
- grad_norm2_bias: float32 [2, 1120], P(None, 'gene')
- grad_bias_q: float32 [2, 1120], P(None, 'gene')
- grad_bias_v: float32 [2, 1120], P(None, 'gene')
- grad_bias_out: float32 [2, 1120], P(None, 'gene')
- grad_bias_up: float32 [2, 4480], P(None, 'gene')
- grad_bias_down: float32 [2, 1120], P(None, 'gene')
The draws below stay inside these ranges and needn't reach their ends.
All inputs are finite; a program needn't handle non-finite values.
Results may differ from the reference program's by a relative error of at most 0.03.
Values may be sent and summed in bfloat16 or wider, within the bound.
No kernel may reach another device: no remote copies, remote signals or barrier semaphores. Data moves between devices by JAX's collectives and lax.ppermute only.
A program may use at most 512 MiB of HBM per device.

```python
import math
import jax
import jax.numpy as jnp
from jax import lax

D = 1120
HEADS = 20
HEAD_DIM = 56
FF = 4480
PREFIX = 64
LAYERS = 2
GENES = 1024
CELLS = 4


def row_factor(factor_key, shape):
    return jnp.exp(jax.random.uniform(factor_key, shape, jnp.float32, math.log(0.5), math.log(5.0)))


def draw_genes(key, part):
    key = jax.random.fold_in(key, 11)
    noise_key, factor_key = jax.random.split(key)
    base_rows = jnp.clip(jax.random.normal(noise_key, (CELLS, GENES, D), jnp.float32), -6.0, 6.0)
    return (base_rows * row_factor(factor_key, (CELLS, GENES, 1))).astype(jnp.bfloat16)


def draw_prefix(key, part):
    key = jax.random.fold_in(key, 23)
    noise_key, factor_key = jax.random.split(key)
    base_rows = jnp.clip(jax.random.normal(noise_key, (CELLS, PREFIX, D), jnp.float32), -6.0, 6.0)
    return (base_rows * row_factor(factor_key, (CELLS, PREFIX, 1))).astype(jnp.bfloat16)


def block_levels(rng, dims, shards, smallest, largest):
    loudness = 1.0
    for axis_at, shards_of in shards:
        draws = jax.random.uniform(jax.random.fold_in(jax.random.fold_in(rng, 6), axis_at), (shards_of,), jnp.float32, smallest / len(shards), largest / len(shards))
        loudness = loudness * jnp.repeat(jnp.exp(draws), dims[axis_at] // shards_of).reshape((-1,) + (1,) * (len(dims) - 1 - axis_at))
    return loudness


def bell_draw(own_key, shape, width, limit, pieces=(), kind=jnp.bfloat16):
    values = width * jax.random.normal(own_key, shape, jnp.float32)
    if pieces:
        values = values * block_levels(own_key, shape, pieces, -0.22, 0.18)
    return jnp.clip(values, -limit, limit).astype(kind)


def setup_inputs(seed: int = 0) -> dict:
    key_of = jax.random.split(jax.random.key(seed), 18)
    genes = draw_genes(jax.random.fold_in(key_of[17], 71), 0)
    prefix = draw_prefix(jax.random.fold_in(key_of[17], 71), 0)
    cot_genes = bell_draw(key_of[2], (CELLS, GENES, D), 1.0, 6.0, ((0, 4), (1, 8)), jnp.float32)
    cot_prefix = bell_draw(key_of[3], (CELLS, PREFIX, D), 1.0, 6.0, ((0, 4), (1, 8)), jnp.float32)
    w_qkv = bell_draw(key_of[4], (LAYERS, D, 3 * D), (D // 2) ** -0.5, 0.25, ((1, 8),))
    w_out = bell_draw(key_of[5], (LAYERS, D, D), (D // 16) ** -0.5, 0.75, ((1, 8),))
    w_up = bell_draw(key_of[6], (LAYERS, D, FF), D ** -0.5, 0.1875, ((1, 8),))
    w_down = bell_draw(key_of[7], (LAYERS, FF, D), FF ** -0.5, 0.09375, ((1, 8),))
    norm1_gain = jnp.clip(1.0 + 0.1 * jax.random.normal(key_of[8], (LAYERS, D), jnp.float32), 0.5, 1.5)
    norm1_bias = bell_draw(key_of[9], (LAYERS, D), 0.5, 3.0, (), jnp.float32)
    norm2_gain = jnp.clip(1.0 + 0.1 * jax.random.normal(key_of[10], (LAYERS, D), jnp.float32), 0.5, 1.5)
    norm2_bias = bell_draw(key_of[11], (LAYERS, D), 0.5, 3.0, (), jnp.float32)
    bias_q = bell_draw(key_of[12], (LAYERS, D), 0.5, 3.0, (), jnp.float32)
    bias_v = bell_draw(key_of[13], (LAYERS, D), 0.5, 3.0, (), jnp.float32)
    bias_out = bell_draw(key_of[14], (LAYERS, D), 0.5, 3.0, (), jnp.float32)
    bias_up = bell_draw(key_of[15], (LAYERS, FF), 0.5, 3.0, (), jnp.float32)
    bias_down = bell_draw(key_of[16], (LAYERS, D), 0.5, 3.0, (), jnp.float32)
    return {"genes": genes, "prefix": prefix, "cot_genes": cot_genes, "cot_prefix": cot_prefix, "w_qkv": w_qkv, "w_out": w_out, "w_up": w_up, "w_down": w_down, "norm1_gain": norm1_gain, "norm1_bias": norm1_bias, "norm2_gain": norm2_gain, "norm2_bias": norm2_bias, "bias_q": bias_q, "bias_v": bias_v, "bias_out": bias_out, "bias_up": bias_up, "bias_down": bias_down}


@jax.custom_vjp
def low(v):
    return lax.optimization_barrier(v.astype(jnp.bfloat16)).astype(jnp.float32)

@jax.custom_vjp
def low_back(v):
    return v

def low_keep(v):
    return (low(v), None)

def low_pass(kept, grad):
    return (grad,)

def back_keep(v):
    return (v, None)

def back_low(kept, grad):
    return (low(grad),)
low.defvjp(low_keep, low_pass)
low_back.defvjp(back_keep, back_low)

def normalize(values, scale_vec, shift_vec):
    centred = values - lax.optimization_barrier(jnp.mean(values, axis=-1, keepdims=True))
    variance = lax.optimization_barrier(jnp.mean(centred * centred, axis=-1, keepdims=True))
    return centred * lax.rsqrt(variance + 1e-05) * scale_vec + shift_vec

def attend_rows(query_rows, query_pos, key_rows, val_rows, key_pos):
    heads_q = query_rows.reshape(query_rows.shape[0], HEADS, HEAD_DIM)
    heads_k = key_rows.reshape(key_rows.shape[0], HEADS, HEAD_DIM)
    heads_v = val_rows.reshape(val_rows.shape[0], HEADS, HEAD_DIM)
    scores = jnp.einsum('qhd,khd->hqk', heads_q, heads_k, precision=lax.Precision.HIGHEST) * HEAD_DIM ** (-0.5)
    scores = low_back(scores)
    allowed = key_pos[None, None, :] <= query_pos[None, :, None]
    scores = jnp.where(allowed, scores, -jnp.inf)
    row_max = lax.optimization_barrier(jnp.max(scores, axis=-1, keepdims=True))
    weights = jnp.exp(scores - row_max)
    probs = low(weights / lax.optimization_barrier(jnp.sum(weights, axis=-1, keepdims=True)))
    mixed = jnp.einsum('hqk,khd->qhd', probs, heads_v, precision=lax.Precision.HIGHEST)
    return mixed.reshape(query_rows.shape[0], HEADS * HEAD_DIM)

def sequence_attention(queries, key_rows, val_rows):
    positions = jnp.arange(queries.shape[0], dtype=jnp.int32)
    head_part = attend_rows(queries[:PREFIX], positions[:PREFIX], key_rows, val_rows, positions)
    block_rows = min(GENES, 512)
    block_count = GENES // block_rows
    gene_q = queries[PREFIX:].reshape(block_count, block_rows, HEADS * HEAD_DIM)
    gene_pos = positions[PREFIX:].reshape(block_count, block_rows)

    def one_block(element):
        return attend_rows(element[0], element[1], key_rows, val_rows, positions)
    gene_part = lax.map(jax.checkpoint(one_block), (gene_q, gene_pos))
    return jnp.concatenate([head_part, gene_part.reshape(GENES, HEADS * HEAD_DIM)], 0)

def layer_block(rows, params):
    w_qkv, w_out, w_up, w_down, gain_one, shift_one, gain_two, shift_two, bias_q, bias_v, bias_out, bias_up, bias_down = params
    normed_one = low(normalize(rows, gain_one, shift_one))
    mixed = jnp.dot(normed_one, w_qkv, precision=lax.Precision.HIGHEST)
    queries = low(low_back(mixed[:, :D] + bias_q))
    key_rows = low(low_back(mixed[:, D:2 * D]))
    val_rows = low(low_back(mixed[:, 2 * D:] + bias_v))
    attended = low(low_back(sequence_attention(queries, key_rows, val_rows)))
    middle = rows + low_back(jnp.dot(attended, w_out, precision=lax.Precision.HIGHEST) + bias_out)
    normed_two = low(normalize(middle, gain_two, shift_two))
    pre_act = low_back(jnp.dot(normed_two, w_up, precision=lax.Precision.HIGHEST) + bias_up)
    active = low(jax.nn.gelu(pre_act, approximate=True))
    return middle + low_back(jnp.dot(active, w_down, precision=lax.Precision.HIGHEST) + bias_down)

def reference(genes, prefix, cot_genes, cot_prefix, w_qkv, w_out, w_up, w_down, norm1_gain, norm1_bias, norm2_gain, norm2_bias, bias_q, bias_v, bias_out, bias_up, bias_down):
    params = tuple((array_in.astype(jnp.float32) for array_in in (w_qkv, w_out, w_up, w_down, norm1_gain, norm1_bias, norm2_gain, norm2_bias, bias_q, bias_v, bias_out, bias_up, bias_down)))

    def forward(gene_rows, prefix_rows, *weights):

        def one_cell(element):
            sequence = jnp.concatenate([element[1], element[0]], 0)
            for level in range(LAYERS):
                sequence = layer_block(sequence, tuple((weight[level] for weight in weights)))
            return sequence
        result = lax.map(one_cell, (gene_rows, prefix_rows))
        return (result[:, PREFIX:], result[:, :PREFIX])
    outputs, pullback = jax.vjp(forward, genes.astype(jnp.float32), prefix.astype(jnp.float32), *params)
    grads = pullback((cot_genes.astype(jnp.float32), cot_prefix.astype(jnp.float32)))
    return (outputs[0], outputs[1], grads[0], grads[1], grads[2], grads[3], grads[4], grads[5], grads[6], grads[7], grads[8], grads[9], grads[10], grads[11], grads[12], grads[13], grads[14])
```

```python
import functools
import math

import jax
import jax.numpy as jnp
from jax import lax
from jax.experimental import pallas as pl
from jax.experimental.pallas import tpu as pltpu
from jax.sharding import PartitionSpec as P

D = 1120
HEADS = 20
HEAD_DIM = 56
FF = 4480
PREFIX = 64
LAYERS = 2
LANES = 128
HALF = 64
TILE = 2 * LANES
EXTRA = 8
SCALE = HEAD_DIM ** (-0.5)
SCALE2 = SCALE * math.log2(math.e)
BF = jnp.bfloat16
F32 = jnp.float32


def dot(left, right, left_dim=1, right_dim=0):
    return lax.dot_general(
        left, right, (((left_dim,), (right_dim,)), ((), ())), preferred_element_type=F32
    )


class Plan:
    def __init__(self, groups, gene_rows):
        self.groups = groups
        self.gene_rows = gene_rows
        self.pre_rows = PREFIX // groups
        self.pre_block = -(-self.pre_rows // 8) * 8
        self.own_rows = gene_rows + self.pre_block
        self.piece_rows = self.own_rows + EXTRA
        self.genes = groups * gene_rows
        self.prefix = groups * self.pre_block
        self.total = self.genes + self.prefix
        self.all_rows = groups * self.piece_rows
        self.cols = D // groups
        self.hidden = FF // groups
        self.chunk = 256
        spans = [
            (self.cols * at // HEAD_DIM, -(-self.cols * (at + 1) // HEAD_DIM))
            for at in range(groups)
        ]
        self.window = max(last - first for first, last in spans)
        self.first_heads = [min(first, HEADS - self.window) for first, _ in spans]
        self.offsets = sorted(
            {self.cols * at - HEAD_DIM * first for at, first in enumerate(self.first_heads)}
        )
        self.wide = self.window * HEAD_DIM
        self.by_pairs = groups == 8


SCALAR = pl.BlockSpec(memory_space=pltpu.SMEM)
WHOLE = pl.BlockSpec(memory_space=pltpu.VMEM)


def call(kernel, name, args, outs, scratch=(), specs=None, flops=0):
    specs = specs or {}
    in_specs = [specs.get(at, WHOLE) for at in range(len(args))]
    moved = sum(math.prod(a.shape) * a.dtype.itemsize for a in args)
    moved += sum(math.prod(o.shape) * o.dtype.itemsize for o in outs)
    return pl.pallas_call(
        kernel,
        in_specs=in_specs,
        out_specs=[WHOLE] * len(outs),
        out_shape=outs,
        scratch_shapes=list(scratch),
        compiler_params=pltpu.CompilerParams(vmem_limit_bytes=58 << 20),
        cost_estimate=pl.CostEstimate(flops=flops, bytes_accessed=moved, transcendentals=0),
        name=name,
    )(*args)


def shape_of(*dims, dtype=BF):
    return jax.ShapeDtypeStruct(dims, dtype)


def aligned(at, size):
    return pl.ds(pl.multiple_of(at * size, size), size)


def normed_of(values):
    centred = values - jnp.mean(values, axis=-1, keepdims=True)
    variance = jnp.mean(centred * centred, axis=-1, keepdims=True)
    inverse = lax.rsqrt(variance + 1e-05)
    return centred * inverse, inverse


def write_piece(plan, piece_ref, rows, tail):
    if plan.pre_rows < plan.pre_block:
        at = lax.broadcasted_iota(jnp.int32, rows.shape, 0)
        rows = jnp.where(at < plan.gene_rows + plan.pre_rows, rows, 0.0)
    whole = jnp.concatenate([rows, tail], 0)
    piece_ref[...] = whole.astype(BF)


def begin_kernel(plan, gene_ref, pre_ref, gain_ref, shift_ref, rows_ref, piece_ref):
    rows = jnp.concatenate([gene_ref[...].astype(F32), pre_ref[...].astype(F32)], 0)
    rows_ref[...] = rows
    unit, _ = normed_of(rows)
    normed = unit * gain_ref[0:1, :] + shift_ref[0:1, :]
    write_piece(plan, piece_ref, normed, jnp.zeros((EXTRA, D), F32))


def add_parts(refs):
    total = refs[0][...].astype(F32)
    for ref in refs[1:]:
        total = total + ref[...].astype(F32)
    return total


def middle_kernel(plan, parts, level, gain_level, *refs):
    part_refs, (base_ref, bias_ref, gain_ref, shift_ref, rows_ref, piece_ref) = (
        refs[:parts],
        refs[parts:],
    )
    rows = base_ref[...] + add_parts(part_refs) + bias_ref[level : level + 1, :]
    rows_ref[...] = rows
    unit, _ = normed_of(rows)
    at = slice(gain_level, gain_level + 1)
    write_piece(
        plan, piece_ref, unit * gain_ref[at, :] + shift_ref[at, :], jnp.zeros((EXTRA, D), F32)
    )


def finish_kernel(plan, parts, level, *refs):
    part_refs, (base_ref, bias_ref, gene_ref, pre_ref) = refs[:parts], refs[parts:]
    rows = base_ref[...] + add_parts(part_refs) + bias_ref[level : level + 1, :]
    gene_ref[...] = rows[: plan.gene_rows]
    pre_ref[...] = rows[plan.gene_rows :]


def norm_back(parts, level, refs):
    part_refs, (x_ref, gain_ref, base_ref) = refs[:parts], refs[parts : parts + 3]
    grad_norm = add_parts(part_refs)
    unit, inverse = normed_of(x_ref[...])
    scaled = grad_norm * gain_ref[level : level + 1, :]
    grad = base_ref[...] + inverse * (
        scaled
        - jnp.mean(scaled, axis=-1, keepdims=True)
        - unit * jnp.mean(scaled * unit, axis=-1, keepdims=True)
    )
    sums = (
        jnp.sum(grad_norm * unit, axis=0, keepdims=True),
        jnp.sum(grad_norm, axis=0, keepdims=True),
    )
    return grad, sums


def tail_of(sums):
    return jnp.concatenate([sums[0], sums[1], jnp.zeros((EXTRA - 2, D), F32)], 0)


def back_kernel(plan, parts, level, *refs):
    grad, sums = norm_back(parts, level, refs)
    grad_ref, piece_ref = refs[parts + 3 :]
    grad_ref[...] = grad
    write_piece(plan, piece_ref, grad, tail_of(sums))


def back_end_kernel(plan, parts, level, *refs):
    grad, sums = norm_back(parts, level, refs)
    gene_ref, pre_ref, sums_ref = refs[parts + 3 :]
    gene_ref[...] = grad[: plan.gene_rows]
    pre_ref[...] = grad[plan.gene_rows :]
    sums_ref[...] = tail_of(sums)


def cot_kernel(plan, gene_ref, pre_ref, rows_ref, piece_ref):
    rows = jnp.concatenate([gene_ref[...], pre_ref[...]], 0)
    rows_ref[...] = rows
    write_piece(plan, piece_ref, rows, jnp.zeros((EXTRA, D), F32))


def chunks_of(plan):
    genes, rows, prefix = plan.genes, plan.chunk, plan.prefix
    chunks = []
    for first in range(0, genes, rows):
        blocks = [(genes, prefix, False)]
        blocks += [(start, rows, start == first) for start in range(0, first + rows, rows)]
        chunks.append((first, rows, blocks))
    chunks.append((genes, prefix, [(genes, prefix, True)]))
    return chunks


def masked(plan, scores, start, diagonal):
    holes = start == plan.genes and plan.pre_rows < plan.pre_block
    if not (diagonal or holes):
        return scores
    key_at = lax.broadcasted_iota(jnp.int32, scores.shape, 0)
    query_at = lax.broadcasted_iota(jnp.int32, scores.shape, 1)
    keep = key_at <= query_at if diagonal else None
    if holes:
        real = lax.rem(key_at, plan.pre_block) < plan.pre_rows
        keep = real if keep is None else keep & real
    return jnp.where(keep, scores, -jnp.inf)


def collect(plan, me, piece_refs, whole_ref, pre_ref):
    sums = 0.0
    for at, ref in enumerate(piece_refs):
        owner = me ^ at
        whole_ref[aligned(owner, plan.gene_rows), :] = ref[: plan.gene_rows, :]
        pre_ref[aligned(owner, plan.pre_block), :] = ref[plan.gene_rows : plan.own_rows, :].astype(F32)
        sums = sums + ref[plan.own_rows :, :].astype(F32)
    whole_ref[plan.genes :, :] = pre_ref[...].astype(BF)
    return sums


def give_blocks(plan, me, block_refs, rows_ref, weight, weight_dim, pre_ref):
    pre_ref[...] = dot(rows_ref[plan.genes :, :], weight, 1, weight_dim)
    for at, ref in enumerate(block_refs):
        owner = me ^ at
        ref[: plan.gene_rows, :] = dot(
            rows_ref[aligned(owner, plan.gene_rows), :], weight, 1, weight_dim
        ).astype(BF)
        ref[plan.gene_rows :, :] = pre_ref[aligned(owner, plan.pre_block), :].astype(BF)


def attend_kernel(plan, level, me_ref, *refs):
    pieces, refs = refs[: plan.groups], refs[plan.groups :]
    weight_ref, bias_ref, select_ref, out_weight_ref = refs[:4]
    low_ref, qkv_ref, mixed_ref, lse_ref = refs[4:8]
    blocks, (pre_ref, turned_ref, score_ref, padded_ref) = (
        refs[8 : 8 + plan.groups],
        refs[8 + plan.groups :],
    )
    me = me_ref[0]
    collect(plan, me, pieces, low_ref, pre_ref)
    for first in range(0, plan.total, plan.chunk):
        rows = slice(first, min(first + plan.chunk, plan.total))
        qkv_ref[rows, :] = (dot(low_ref[rows, :], weight_ref[...]) + bias_ref[...]).astype(BF)
    for head in range(plan.window):
        query_at = slice(TILE * head, TILE * head + LANES)
        value_at = slice(TILE * head + LANES, TILE * (head + 1))
        turned_ref[...] = qkv_ref[:, value_at].astype(F32).T.astype(BF)
        for first, count, parts in chunks_of(plan):
            query = qkv_ref[first : first + count, query_at]
            top = None
            for start, size, diagonal in parts:
                scores = dot(qkv_ref[start : start + size, value_at], query, 1, 1)
                scores = masked(plan, scores, start, diagonal)
                score_ref[start : start + size, :count] = scores
                high = jnp.max(scores, axis=0, keepdims=True)
                top = high if top is None else jnp.maximum(top, high)
            top = top * SCALE2
            total, mixed = 0.0, 0.0
            for start, size, _ in parts:
                weights = jnp.exp2(score_ref[start : start + size, :count] * SCALE2 - top)
                total = total + jnp.sum(weights, axis=0, keepdims=True)
                mixed = mixed + dot(turned_ref[:, start : start + size], weights.astype(BF))
            padded_ref[first : first + count, LANES * head : LANES * (head + 1)] = (
                (mixed * (1.0 / total)).T.astype(BF)
            )
            lse_ref[head, :, first : first + count] = top + jnp.log2(total)
    mixed_ref[...] = dot(padded_ref[...], select_ref[...]).astype(BF)
    give_blocks(plan, me, blocks, mixed_ref, out_weight_ref[level], 0, pre_ref)


def attend_back_kernel(plan, me_ref, *refs):
    pieces, refs = refs[: plan.groups], refs[plan.groups :]
    out_weight_ref, qkv_ref, lse_ref, select_ref, weight_ref = refs[:5]
    low_ref, qkv_grad_ref, sums_ref, out_bias_ref, qkv_bias_ref = refs[5:10]
    blocks = refs[10 : 10 + plan.groups]
    pre_ref, grad_ref, turned_ref, prob_ref, pgrad_ref, pair_ref, padded_ref = refs[10 + plan.groups :]
    me = me_ref[0]
    sums_ref[...] = collect(plan, me, pieces, low_ref, pre_ref)
    out_bias_ref[...] = jnp.sum(low_ref[...].astype(F32), axis=0, keepdims=True)
    for first in range(0, plan.total, plan.chunk):
        rows = slice(first, min(first + plan.chunk, plan.total))
        grad_ref[rows, :] = dot(low_ref[rows, :], out_weight_ref[...], 1, 1).astype(BF)
    lane = lax.broadcasted_iota(jnp.int32, (1, LANES), 1)
    pair_scale = jnp.where(lane < HALF, SCALE, 1.0)
    for head in range(plan.window):
        query_at = slice(TILE * head, TILE * head + LANES)
        value_at = slice(TILE * head + LANES, TILE * (head + 1))
        grad_at = slice(LANES * head, LANES * (head + 1))
        turned_ref[...] = qkv_ref[:, value_at].astype(F32).T.astype(BF)
        pair_ref[...] = jnp.zeros_like(pair_ref)
        for first, count, parts in chunks_of(plan):
            query = qkv_ref[first : first + count, query_at]
            grad = grad_ref[first : first + count, grad_at]
            lse = lse_ref[head, :, first : first + count]
            delta = 0.0
            for start, size, diagonal in parts:
                pair = qkv_ref[start : start + size, value_at]
                scores = masked(plan, dot(pair, query, 1, 1), start, diagonal)
                probs = jnp.exp2(scores * SCALE2 - lse)
                prob_grad = dot(pair, grad, 1, 1)
                delta = delta + jnp.sum(probs * prob_grad, axis=0, keepdims=True)
                prob_ref[start : start + size, :count] = probs
                pgrad_ref[start : start + size, :count] = prob_grad
            query_grad = 0.0
            for start, size, _ in parts:
                probs = prob_ref[start : start + size, :count]
                score_grad = (probs * (pgrad_ref[start : start + size, :count] - delta)).astype(BF)
                pair_ref[start : start + size, :] += dot(probs.astype(BF), grad) + dot(score_grad, query)
                query_grad = query_grad + dot(turned_ref[:, start : start + size], score_grad)
            padded_ref[first : first + count, query_at] = (query_grad.T * SCALE).astype(BF)
        padded_ref[:, value_at] = (pair_ref[...] * pair_scale).astype(BF)
    qkv_grad_ref[...] = dot(padded_ref[...], select_ref[...]).astype(BF)
    qkv_bias_ref[...] = jnp.sum(qkv_grad_ref[...].astype(F32), axis=0, keepdims=True)
    give_blocks(plan, me, blocks, qkv_grad_ref, weight_ref[...], 1, pre_ref)


ROOT = math.sqrt(2.0 / math.pi)
CUBE = 0.044715


def lift_kernel(plan, level, *refs):
    pieces, refs = refs[: plan.groups], refs[plan.groups :]
    up_ref, bias_ref, down_ref, low_ref, pre_ref, active_ref = refs[:6]
    blocks = refs[6:]
    size = plan.piece_rows
    for at, ref in enumerate(pieces):
        low_ref[at * size : (at + 1) * size, :] = ref[...]
    step = 2 * size
    for first in range(0, plan.all_rows, step):
        rows = slice(first, first + step)
        pre = dot(low_ref[rows, :], up_ref[...]) + bias_ref[...]
        pre_ref[rows, :] = pre
        active = (0.5 * pre * (1.0 + jnp.tanh(ROOT * (pre + CUBE * pre * pre * pre)))).astype(BF)
        active_ref[rows, :] = active
        lifted = dot(active, down_ref[level])
        for at in range(2):
            blocks[first // size + at][...] = lifted[at * size : at * size + plan.own_rows].astype(BF)


def lift_back_kernel(plan, level, *refs):
    pieces, refs = refs[: plan.groups], refs[plan.groups :]
    up_ref, pre_ref, down_ref = refs[:3]
    low_ref, pre_grad_ref, sums_ref, down_bias_ref, up_bias_ref = refs[3:8]
    blocks = refs[8:]
    size = plan.piece_rows
    at_row = lax.broadcasted_iota(jnp.int32, (size, D), 0)
    sums, down_bias, up_bias = 0.0, 0.0, 0.0
    for at, ref in enumerate(pieces):
        rows = ref[...].astype(F32)
        sums = sums + rows[plan.own_rows :]
        rows = jnp.where(at_row < plan.own_rows, rows, 0.0)
        down_bias = down_bias + jnp.sum(rows, axis=0, keepdims=True)
        low_ref[at * size : (at + 1) * size, :] = rows.astype(BF)
    sums_ref[...] = sums
    down_bias_ref[...] = down_bias
    step = 2 * size
    for first in range(0, plan.all_rows, step):
        rows = slice(first, first + step)
        act_grad = dot(low_ref[rows, :], down_ref[level], 1, 1)
        pre = pre_ref[rows, :]
        square = pre * pre
        turn = jnp.tanh(ROOT * pre * (1.0 + CUBE * square))
        slope = 0.5 * (1.0 + turn) + (0.5 * ROOT) * pre * (1.0 - turn * turn) * (1.0 + 3.0 * CUBE * square)
        pre_grad = (act_grad * slope).astype(BF)
        pre_grad_ref[rows, :] = pre_grad
        up_bias = up_bias + jnp.sum(pre_grad.astype(F32), axis=0, keepdims=True)
        norm_grad = dot(pre_grad, up_ref[...], 1, 1)
        for at in range(2):
            blocks[first // size + at][...] = norm_grad[at * size : at * size + plan.own_rows].astype(BF)
    up_bias_ref[...] = up_bias


def send_qkv_kernel(plan, level, me_ref, weight_ref, *refs):
    outs, (stack_ref,) = refs[: plan.groups], refs[plan.groups :]
    wide = plan.wide
    for to, head in enumerate(plan.first_heads):
        for block in range(3):
            begin = block * D + head * HEAD_DIM
            stack_ref[to, :, block * wide : (block + 1) * wide] = weight_ref[
                level, :, begin : begin + wide
            ].astype(F32)
    for at, ref in enumerate(outs):
        ref[...] = stack_ref[me_ref[0] ^ at].astype(BF)


def take_qkv_kernel(plan, me_ref, *refs):
    pieces, (padded_ref, own_ref, stack_ref, wide_ref, cut_ref) = (
        refs[: plan.groups],
        refs[plan.groups :],
    )
    me = me_ref[0]
    offset = me_ref[1]
    cols, wide = plan.cols, plan.wide
    for at, ref in enumerate(pieces):
        stack_ref[at] = ref[...].astype(F32)
    wide_ref[...] = jnp.zeros_like(wide_ref)
    for source in range(plan.groups):
        rows = slice(cols * source, cols * (source + 1))
        value = stack_ref[me ^ source]
        for block, to in enumerate((0, LANES, LANES + HALF)):
            part = value[:, block * wide : (block + 1) * wide]
            for head in range(plan.window):
                wide_ref[rows, TILE * head + to : TILE * head + to + HEAD_DIM] = part[
                    :, head * HEAD_DIM : (head + 1) * HEAD_DIM
                ]
            own = part[:, plan.offsets[0] : plan.offsets[0] + cols]
            for choice in plan.offsets[1:]:
                own = jnp.where(offset == choice, part[:, choice : choice + cols], own)
            cut_ref[rows, block * cols : (block + 1) * cols] = own
    padded_ref[...] = wide_ref[...].astype(BF)
    own_ref[...] = cut_ref[...].astype(BF)


def send_up_kernel(plan, level, me_ref, weight_ref, *refs):
    outs, (stack_ref,) = refs[: plan.groups], refs[plan.groups :]
    for to in range(plan.groups):
        stack_ref[to] = weight_ref[level, :, to * plan.hidden : (to + 1) * plan.hidden].astype(F32)
    for at, ref in enumerate(outs):
        ref[...] = stack_ref[me_ref[0] ^ at].astype(BF)


def take_up_kernel(plan, me_ref, *refs):
    pieces, (up_ref, stack_ref, whole_ref) = refs[: plan.groups], refs[plan.groups :]
    for at, ref in enumerate(pieces):
        stack_ref[at] = ref[...].astype(F32)
    for source in range(plan.groups):
        whole_ref[plan.cols * source : plan.cols * (source + 1), :] = stack_ref[me_ref[0] ^ source]
    up_ref[...] = whole_ref[...].astype(BF)


def weight_grad_kernel(plan, me_ref, left_ref, right_ref, *refs):
    outs, (whole_ref, stack_ref) = refs[: plan.groups], refs[plan.groups :]
    for first in range(0, D, TILE):
        rows = slice(first, min(first + TILE, D))
        whole_ref[rows, :] = dot(left_ref[:, rows], right_ref[...], 0, 0)
    for to in range(plan.groups):
        stack_ref[to] = whole_ref[plan.cols * to : plan.cols * (to + 1), :]
    for at, ref in enumerate(outs):
        ref[...] = stack_ref[me_ref[0] ^ at].astype(BF)


def join_kernel(plan, blocks, me_ref, *refs):
    parts, out_ref = refs[:LAYERS], refs[LAYERS]
    each = parts[0].shape[2] // blocks
    for level, ref in enumerate(parts):
        for source in range(plan.groups):
            value = ref[me_ref[0] ^ source].astype(F32)
            for block in range(blocks):
                begin = (block * plan.groups + source) * each
                out_ref[level, :, begin : begin + each] = value[:, block * each : (block + 1) * each]


def body(
    genes,
    prefix,
    cot_genes,
    cot_prefix,
    w_qkv,
    w_out,
    w_up,
    w_down,
    norm1_gain,
    norm1_bias,
    norm2_gain,
    norm2_bias,
    bias_q,
    bias_v,
    bias_out,
    bias_up,
    bias_down,
):
    groups = lax.axis_size("gene")
    cells = lax.axis_size("cell")
    me = lax.axis_index("gene")
    cell = lax.axis_index("cell")
    plan = Plan(groups, genes.shape[1])
    cols, wide, window, hidden = plan.cols, plan.wide, plan.window, plan.hidden
    own_rows, piece_rows = plan.own_rows, plan.piece_rows
    first_head = jnp.asarray(plan.first_heads, jnp.int32)[me]
    offset = me * cols - first_head * HEAD_DIM
    turn = me if plan.by_pairs else jnp.zeros_like(me)
    where = jnp.stack([turn, offset]).astype(jnp.int32)
    here = functools.partial

    def swap(value, bits):
        return lax.ppermute(value, "gene", [(at, at ^ bits) for at in range(groups)])

    def gather(piece):
        if not plan.by_pairs:
            stack = lax.all_gather(piece, "gene", axis=0)
            return [stack[at] for at in range(groups)]
        near = [piece] + [swap(piece, bits) for bits in (2, 4, 6)]
        far = [swap(value, 1) for value in near]
        return [value for pair in zip(near, far) for value in pair]

    def scatter_sum(blocks):
        if not plan.by_pairs:
            return [lax.psum_scatter(jnp.stack(blocks), "gene", scatter_dimension=0)]
        parts = []
        for bits in (2, 4, 6):
            other = swap(blocks[bits ^ 1], 1)
            total = (blocks[bits].astype(F32) + other.astype(F32)).astype(BF)
            parts.append(swap(total, bits))
        return [blocks[0], swap(blocks[1], 1)] + parts

    def exchange(pieces):
        if not plan.by_pairs:
            stack = lax.all_to_all(jnp.stack(pieces), "gene", 0, 0)
            return [stack[at] for at in range(groups)]
        return [pieces[0]] + [swap(pieces[bits], bits) for bits in range(1, groups)]

    def sum_cells(value):
        if cells != 4:
            return lax.psum(value, "cell").astype(F32)
        outer = lax.ppermute(value, "cell", [(0, 1), (3, 2)])
        half = (value.astype(F32) + outer.astype(F32)).astype(BF)
        other = lax.ppermute(half, "cell", [(1, 2), (2, 1)])
        total = (half.astype(F32) + other.astype(F32)).astype(BF)
        back = lax.ppermute(total, "cell", [(1, 0), (2, 3)])
        return jnp.where((cell == 1) | (cell == 2), total, back).astype(F32)

    def reshard_qkv(level):
        pieces = call(
            here(send_qkv_kernel, plan, level),
            "send_qkv",
            [where, w_qkv],
            [shape_of(cols, 3 * wide)] * groups,
            [pltpu.VMEM((groups, cols, 3 * wide), F32)],
            {0: SCALAR},
        )
        return call(
            here(take_qkv_kernel, plan),
            "take_qkv",
            [where] + exchange(pieces),
            [shape_of(D, window * TILE), shape_of(D, 3 * cols)],
            [
                pltpu.VMEM((groups, cols, 3 * wide), F32),
                pltpu.VMEM((D, window * TILE), F32),
                pltpu.VMEM((D, 3 * cols), F32),
            ],
            {0: SCALAR},
        )

    def reshard_up(level):
        pieces = call(
            here(send_up_kernel, plan, level),
            "send_up",
            [where, w_up],
            [shape_of(cols, hidden)] * groups,
            [pltpu.VMEM((groups, cols, hidden), F32)],
            {0: SCALAR},
        )
        return call(
            here(take_up_kernel, plan),
            "take_up",
            [where] + exchange(pieces),
            [shape_of(D, hidden)],
            [pltpu.VMEM((groups, cols, hidden), F32), pltpu.VMEM((D, hidden), F32)],
            {0: SCALAR},
        )[0]

    at_row = jnp.arange(window * TILE)
    lane = at_row % TILE
    block = jnp.where(lane < LANES, 0, jnp.where(lane < LANES + HALF, 1, 2))
    inner = lane % HALF
    inner_ok = (inner < HEAD_DIM) & ((lane < HALF) | (lane >= LANES))
    source = jnp.where(inner_ok, block * cols + (at_row // TILE) * HEAD_DIM + inner - offset, -1)
    in_block = source - block * cols
    source = jnp.where((in_block >= 0) & (in_block < cols), source, -1)
    select = (source[:, None] == jnp.arange(3 * cols)[None, :]).astype(BF)
    at_out = jnp.arange(window * LANES)
    inner = at_out % LANES - HALF
    out_col = (at_out // LANES) * HEAD_DIM + inner
    out_ok = (inner >= 0) & (inner < HEAD_DIM)
    out_select = (
        jnp.where(out_ok, out_col - offset, -1)[:, None] == jnp.arange(cols)[None, :]
    ).astype(BF)

    def out_window(level):
        pairs = plan.by_pairs
        if pairs:
            other = swap(w_out[level], 1)
            rows = jnp.concatenate([w_out[level], other], 0)
            owner = jnp.concatenate([me * cols + jnp.arange(cols), (me ^ 1) * cols + jnp.arange(cols)])
        else:
            rows = lax.all_gather(w_out[level], "gene", axis=0, tiled=True)
            owner = jnp.arange(D)
        wanted = jnp.where(out_ok, first_head * HEAD_DIM + out_col, -1)
        pick = (wanted[:, None] == owner[None, :]).astype(BF)
        return dot(pick, rows).astype(BF)

    def padded_bias(level):
        def cut(vec):
            part = lax.dynamic_slice_in_dim(vec[level], first_head * HEAD_DIM, wide, 0)
            return jnp.pad(part.reshape(window, HEAD_DIM), ((0, 0), (0, HALF - HEAD_DIM)))

        nothing = jnp.zeros((window, HALF), F32)
        return jnp.stack([cut(bias_q), nothing, nothing, cut(bias_v)], 1).reshape(1, window * TILE)

    qkv_biases = [padded_bias(level) for level in range(LAYERS)]
    up_biases = [
        lax.dynamic_slice_in_dim(bias_up[level], me * hidden, hidden, 0)[None]
        for level in range(LAYERS)
    ]
    rows_f32 = shape_of(own_rows, D, dtype=F32)
    piece_like = shape_of(piece_rows, D)
    blocks_like = [shape_of(own_rows, D)] * groups
    vector = shape_of(1, D, dtype=F32)
    sums_like = shape_of(EXTRA, D, dtype=F32)

    own_prefix = lax.dynamic_slice_in_dim(prefix[0], me * plan.pre_rows, plan.pre_rows, 0)
    filler = ((0, plan.pre_block - plan.pre_rows), (0, 0))
    rows, piece = call(
        here(begin_kernel, plan),
        "begin",
        [genes[0], jnp.pad(own_prefix, filler), norm1_gain, norm1_bias],
        [rows_f32, piece_like],
    )
    saved = []
    qkv_weights, up_weights, out_windows = [None] * LAYERS, [None] * LAYERS, [None] * LAYERS
    result = None
    for level in range(LAYERS):
        qkv_weights[level] = reshard_qkv(level)
        up_weights[level] = reshard_up(level)
        out_windows[level] = out_window(level)
    for level in range(LAYERS):
        pieces = gather(piece)
        outs = call(
            here(attend_kernel, plan, level),
            "attend",
            [where] + pieces + [qkv_weights[level][0], qkv_biases[level], out_select, w_out],
            [
                shape_of(plan.total, D),
                shape_of(plan.total, window * TILE),
                shape_of(plan.total, cols),
                shape_of(window, 1, plan.total, dtype=F32),
            ]
            + blocks_like,
            [
                pltpu.VMEM((plan.prefix, D), F32),
                pltpu.VMEM((LANES, plan.total), BF),
                pltpu.VMEM((plan.total, plan.chunk), F32),
                pltpu.VMEM((plan.total, window * LANES), BF),
            ],
            {0: SCALAR},
            flops=4 * 10**9,
        )
        low_one, qkv, mixed, lse = outs[:4]
        parts = scatter_sum(outs[4:])
        middle, piece = call(
            here(middle_kernel, plan, len(parts), level, level),
            "middle",
            parts + [rows, bias_out, norm2_gain, norm2_bias],
            [rows_f32, piece_like],
        )
        outs = call(
            here(lift_kernel, plan, level),
            "lift",
            gather(piece) + [up_weights[level], up_biases[level], w_down],
            [
                shape_of(plan.all_rows, D),
                shape_of(plan.all_rows, hidden, dtype=F32),
                shape_of(plan.all_rows, hidden),
            ]
            + blocks_like,
            flops=3 * 10**9,
        )
        low_two, pre_act, active = outs[:3]
        saved.append((rows, low_one, qkv, mixed, lse, middle, low_two, pre_act, active))
        parts = scatter_sum(outs[3:])
        if level + 1 < LAYERS:
            rows, piece = call(
                here(middle_kernel, plan, len(parts), level, level + 1),
                "next_rows",
                parts + [middle, bias_down, norm1_gain, norm1_bias],
                [rows_f32, piece_like],
            )
        else:
            result = call(
                here(finish_kernel, plan, len(parts), level),
                "finish",
                parts + [middle, bias_down],
                [
                    shape_of(plan.gene_rows, D, dtype=F32),
                    shape_of(plan.pre_block, D, dtype=F32),
                ],
            )

    grad, piece = call(
        here(cot_kernel, plan),
        "cotangent",
        [cot_genes[0], jnp.pad(cot_prefix[0], filler)],
        [rows_f32, piece_like],
    )
    weight_sums = [[None] * LAYERS for _ in range(4)]
    small = [[None] * LAYERS for _ in range(9)]

    def own_slice(rows_in):
        return lax.dynamic_slice_in_dim(rows_in, me * cols, cols, 1)

    for level in reversed(range(LAYERS)):
        rows, low_one, qkv, mixed, lse, middle, low_two, pre_act, active = saved[level]
        outs = call(
            here(lift_back_kernel, plan, level),
            "lift_back",
            gather(piece) + [up_weights[level], pre_act, w_down],
            [
                shape_of(plan.all_rows, D),
                shape_of(plan.all_rows, hidden),
                sums_like,
                vector,
                shape_of(1, hidden, dtype=F32),
            ]
            + blocks_like,
            flops=3 * 10**9,
        )
        low_grad, pre_grad, sums, down_bias, up_bias = outs[:5]
        if level + 1 < LAYERS:
            small[0][level + 1], small[1][level + 1] = sums[0:1], sums[1:2]
        small[8][level], small[7][level] = down_bias, up_bias
        parts = scatter_sum(outs[5:])
        weight_sums[3][level] = sum_cells(dot(active, low_grad, 0, 0).astype(BF))
        up_parts = call(
            here(weight_grad_kernel, plan),
            "up_grad",
            [where, low_two, pre_grad],
            [shape_of(cols, hidden)] * groups,
            [pltpu.VMEM((D, hidden), F32), pltpu.VMEM((groups, cols, hidden), F32)],
            {0: SCALAR},
            flops=14 * 10**8,
        )
        weight_sums[2][level] = sum_cells(jnp.stack(exchange(up_parts)))
        middle_grad, piece = call(
            here(back_kernel, plan, len(parts), level),
            "middle_back",
            parts + [middle, norm2_gain, grad],
            [rows_f32, piece_like],
        )
        outs = call(
            here(attend_back_kernel, plan),
            "attend_back",
            [where]
            + gather(piece)
            + [out_windows[level], qkv, lse, select, qkv_weights[level][1]],
            [
                shape_of(plan.total, D),
                shape_of(plan.total, 3 * cols),
                sums_like,
                vector,
                shape_of(1, 3 * cols, dtype=F32),
            ]
            + blocks_like,
            [
                pltpu.VMEM((plan.prefix, D), F32),
                pltpu.VMEM((plan.total, window * LANES), BF),
                pltpu.VMEM((LANES, plan.total), BF),
                pltpu.VMEM((plan.total, plan.chunk), F32),
                pltpu.VMEM((plan.total, plan.chunk), F32),
                pltpu.VMEM((plan.total, LANES), F32),
                pltpu.VMEM((plan.total, window * TILE), BF),
            ],
            {0: SCALAR},
            flops=8 * 10**9,
        )
        low_grad, qkv_grad, sums, out_bias, qkv_bias = outs[:5]
        small[2][level], small[3][level] = sums[0:1], sums[1:2]
        small[6][level] = out_bias
        small[4][level], small[5][level] = qkv_bias[:, :cols], qkv_bias[:, 2 * cols :]
        parts = scatter_sum(outs[5:])
        weight_sums[1][level] = sum_cells(dot(mixed, low_grad, 0, 0).astype(BF))
        qkv_parts = call(
            here(weight_grad_kernel, plan),
            "qkv_grad",
            [where, low_one, qkv_grad],
            [shape_of(cols, 3 * cols)] * groups,
            [pltpu.VMEM((D, 3 * cols), F32), pltpu.VMEM((groups, cols, 3 * cols), F32)],
            {0: SCALAR},
            flops=10**9,
        )
        weight_sums[0][level] = sum_cells(jnp.stack(exchange(qkv_parts)))
        if level:
            grad, piece = call(
                here(back_kernel, plan, len(parts), level),
                "rows_back",
                parts + [rows, norm1_gain, middle_grad],
                [rows_f32, piece_like],
            )
        else:
            gene_grad, pre_grad, sums = call(
                here(back_end_kernel, plan, len(parts), level),
                "rows_back_end",
                parts + [rows, norm1_gain, middle_grad],
                [
                    shape_of(plan.gene_rows, D, dtype=F32),
                    shape_of(plan.pre_block, D, dtype=F32),
                    sums_like,
                ],
            )

    long_rows = [small[which][level] for which in (2, 3, 6, 8) for level in range(LAYERS)]
    long_rows += [small[which][level] for which in (0, 1) for level in range(1, LAYERS)]
    packed = own_slice(jnp.concatenate(long_rows, 0))
    short_rows = [small[which][level] for which in (4, 5) for level in range(LAYERS)]
    short_rows += [small[7][level].reshape(hidden // cols, cols) for level in range(LAYERS)]
    packed = sum_cells(jnp.concatenate([packed] + short_rows, 0).astype(BF))
    last = lax.psum(sums[:2].astype(BF), ("gene", "cell"))
    last = own_slice(last.astype(F32))
    base = 4 * LAYERS
    ends = base + 2 * (LAYERS - 1)
    per = LAYERS - 1
    vectors = [
        jnp.concatenate([last[0:1], packed[base : base + per]], 0),
        jnp.concatenate([last[1:2], packed[base + per : ends]], 0),
        packed[0:LAYERS],
        packed[LAYERS : 2 * LAYERS],
        packed[ends : ends + LAYERS],
        packed[ends + LAYERS : ends + 2 * LAYERS],
        packed[2 * LAYERS : 3 * LAYERS],
        packed[ends + 2 * LAYERS :].reshape(LAYERS, hidden),
        packed[3 * LAYERS : 4 * LAYERS],
    ]

    def join(parts, blocks, width):
        return call(
            here(join_kernel, plan, blocks),
            "join",
            [where] + [part.astype(BF) for part in parts],
            [shape_of(LAYERS, cols, width, dtype=F32)],
            specs={0: SCALAR},
        )[0]

    return (
        result[0][None],
        result[1][: plan.pre_rows][None],
        gene_grad[None],
        pre_grad[: plan.pre_rows][None],
        join(weight_sums[0], 3, 3 * D),
        jnp.stack(weight_sums[1]),
        join(weight_sums[2], 1, FF),
        jnp.stack(weight_sums[3]),
        *vectors,
    )


def solution(mesh):
    rows = P("cell", "gene", None)
    weight = P(None, "gene", None)
    vector = P(None, "gene")
    return jax.shard_map(
        body,
        mesh=mesh,
        in_specs=(rows, P("cell", None, None), rows, rows) + (weight,) * 4 + (P(),) * 9,
        out_specs=(rows,) * 4 + (weight,) * 4 + (vector,) * 9,
        check_vma=False,
    )
```

```python
import functools
import math

import jax
import jax.numpy as jnp
from jax import lax
from jax.experimental import pallas as pl
from jax.experimental.pallas import tpu as pltpu
from jax.sharding import PartitionSpec as P

D = 1120
HEADS = 20
HEAD_DIM = 56
FF = 4480
PREFIX = 64
LAYERS = 2
LANES = 128
HALF = 64
SCALE = HEAD_DIM ** (-0.5)
SCALE2 = SCALE * math.log2(math.e)
BF = jnp.bfloat16
F32 = jnp.float32
COST = 1000


def dot(left, right, left_dim=1, right_dim=0):
    return lax.dot_general(
        left, right, (((left_dim,), (right_dim,)), ((), ())), preferred_element_type=F32
    )


class Plan:
    def __init__(self, groups, gene_rows):
        self.groups = groups
        self.chips = groups // 2
        self.gene_rows = gene_rows
        self.pre_rows = PREFIX // groups
        self.pre_block = -(-self.pre_rows // 8) * 8
        self.own_rows = gene_rows + self.pre_block
        self.step_rows = -(-self.own_rows // 16) * 16
        self.genes = self.chips * gene_rows
        self.prefix = self.chips * self.pre_block
        self.rows = self.genes + self.prefix
        self.all_rows = self.chips * self.step_rows
        self.cols = D // groups
        self.chip_cols = D // self.chips
        self.hidden = FF // groups
        self.chip_hidden = FF // self.chips
        self.part = -(-self.cols // 16) * 16
        self.features = groups * self.part
        spans = [
            (self.chip_cols * at // HEAD_DIM, -(-self.chip_cols * (at + 1) // HEAD_DIM))
            for at in range(self.chips)
        ]
        self.window = max(last - first for first, last in spans)
        self.first_heads = [min(first, HEADS - self.window) for first, _ in spans]
        self.wide = self.window * HEAD_DIM
        self.lanes = self.window * LANES
        self.by_links = groups == 8

    def halves(self, total):
        step = -(-total // 32) * 16
        return [slice(first, min(first + step, total)) for first in range(0, total, step)]


SCALAR = pl.BlockSpec(memory_space=pltpu.SMEM)
WHOLE = pl.BlockSpec(memory_space=pltpu.VMEM)


def call(kernel, name, args, outs, scratch=(), scalar=False):
    got = pl.pallas_call(
        kernel,
        in_specs=[SCALAR if scalar and at == 0 else WHOLE for at in range(len(args))],
        out_specs=[WHOLE] * len(outs),
        out_shape=outs,
        scratch_shapes=list(scratch),
        compiler_params=pltpu.CompilerParams(vmem_limit_bytes=58 << 20),
        cost_estimate=pl.CostEstimate(flops=COST, bytes_accessed=COST, transcendentals=0),
        name=name,
    )(*args)
    return list(got)


def shape_of(*dims, dtype=BF):
    return jax.ShapeDtypeStruct(dims, dtype)


def aligned(at, size):
    return pl.ds(pl.multiple_of(at * size, size), size)


def normed_of(values):
    centred = values - jnp.mean(values, axis=-1, keepdims=True)
    variance = jnp.mean(centred * centred, axis=-1, keepdims=True)
    inverse = lax.rsqrt(variance + 1e-05)
    return centred * inverse, inverse


def spread(plan, rows):
    filler = jnp.zeros((rows.shape[0], plan.part - plan.cols), rows.dtype)
    parts = []
    for at in range(plan.groups):
        parts += [rows[:, at * plan.cols : (at + 1) * plan.cols], filler]
    return jnp.concatenate(parts, 1)


def unspread(plan, rows):
    return jnp.concatenate(
        [rows[:, at * plan.part : at * plan.part + plan.cols] for at in range(plan.groups)], 1
    )


def real_rows(plan, rows):
    if plan.pre_rows == plan.pre_block:
        return rows
    at = lax.broadcasted_iota(jnp.int32, rows.shape, 0)
    return jnp.where(at < plan.gene_rows + plan.pre_rows, rows, 0.0)


def normed_piece(plan, rows, gain_ref, shift_ref, level):
    unit, _ = normed_of(rows)
    normed = unit * gain_ref[level : level + 1, :] + shift_ref[level : level + 1, :]
    return spread(plan, real_rows(plan, normed)).astype(BF)


def begin_kernel(plan, gene_ref, pre_ref, gain_ref, shift_ref, rows_ref, piece_ref):
    rows = jnp.concatenate([gene_ref[...].astype(F32).T, pre_ref[...].astype(F32)], 0)
    rows_ref[...] = rows
    piece_ref[...] = normed_piece(plan, rows, gain_ref, shift_ref, 0)


def add_parts(refs):
    total = refs[0][...].astype(F32)
    for ref in refs[1:]:
        total = total + ref[...].astype(F32)
    return total


def middle_kernel(plan, parts, level, gain_level, *refs):
    part_refs, (base_ref, bias_ref, gain_ref, shift_ref, rows_ref, piece_ref) = (
        refs[:parts],
        refs[parts:],
    )
    rows = base_ref[...] + add_parts(part_refs) + bias_ref[level : level + 1, :]
    rows_ref[...] = rows
    piece_ref[...] = normed_piece(plan, rows, gain_ref, shift_ref, gain_level)


def finish_kernel(plan, parts, level, *refs):
    part_refs, (base_ref, bias_ref, gene_ref, pre_ref) = refs[:parts], refs[parts:]
    rows = base_ref[...] + add_parts(part_refs) + bias_ref[level : level + 1, :]
    gene_ref[...] = rows[: plan.gene_rows].T
    pre_ref[...] = rows[plan.gene_rows :]


def norm_back(plan, parts, level, refs):
    part_refs, (x_ref, gain_ref, base_ref) = refs[:parts], refs[parts : parts + 3]
    grad_norm = unspread(plan, add_parts(part_refs))
    unit, inverse = normed_of(x_ref[...])
    scaled = grad_norm * gain_ref[level : level + 1, :]
    return base_ref[...] + inverse * (
        scaled
        - jnp.mean(scaled, axis=-1, keepdims=True)
        - unit * jnp.mean(scaled * unit, axis=-1, keepdims=True)
    )


def back_kernel(plan, parts, level, *refs):
    grad = norm_back(plan, parts, level, refs)
    grad_ref, piece_ref = refs[parts + 3 :]
    grad_ref[...] = grad
    piece_ref[...] = real_rows(plan, grad).astype(BF)


def back_end_kernel(plan, parts, level, *refs):
    grad = norm_back(plan, parts, level, refs)
    gene_ref, pre_ref = refs[parts + 3 :]
    gene_ref[...] = grad[: plan.gene_rows].T
    pre_ref[...] = grad[plan.gene_rows :]


def cot_kernel(plan, gene_ref, pre_ref, rows_ref, piece_ref):
    rows = jnp.concatenate([gene_ref[...].T, pre_ref[...]], 0)
    rows_ref[...] = rows
    piece_ref[...] = real_rows(plan, rows).astype(BF)


def query_chunks(plan):
    both, genes = 2 * plan.gene_rows, 2 * plan.genes
    chunks = []
    for chip in range(plan.chips):
        blocks = [(genes, 2 * plan.prefix, False)]
        blocks += [(start, both, start == chip * both) for start in range(0, (chip + 1) * both, both)]
        chunks.append((chip * plan.gene_rows, plan.gene_rows, blocks))
    chunks.append((plan.genes, plan.prefix, [(genes, 2 * plan.prefix, True)]))
    return chunks


def masked(plan, scores, start, diagonal, core):
    in_prefix = start == 2 * plan.genes
    holes = in_prefix and plan.pre_rows < plan.pre_block
    if not (diagonal or holes):
        return scores
    key_at = lax.broadcasted_iota(jnp.int32, scores.shape, 0)
    query_at = lax.broadcasted_iota(jnp.int32, scores.shape, 1)
    keep = None
    if diagonal:
        block = plan.pre_block if in_prefix else plan.gene_rows
        inner = lax.rem(query_at, block)
        keep = key_at <= 2 * query_at - inner + core * block
    if holes:
        real = lax.rem(key_at, plan.pre_block) < plan.pre_rows
        keep = real if keep is None else keep & real
    return jnp.where(keep, scores, -jnp.inf)


def collect(plan, chip, piece_refs, whole_ref, pre_ref):
    for at, ref in enumerate(piece_refs):
        owner = chip ^ at
        whole_ref[aligned(owner, plan.gene_rows), :] = ref[: plan.gene_rows, :]
        pre_ref[aligned(owner, plan.pre_block), :] = ref[plan.gene_rows :, :].astype(F32)
    whole_ref[plan.genes :, :] = pre_ref[...].astype(BF)


def collect_weight(plan, me, part_refs, weight_ref):
    for at, ref in enumerate(part_refs):
        weight_ref[aligned(me ^ at, plan.part), :] = ref[...]


def give_blocks(plan, chip, block_refs, rows_ref, weight, weight_dim, pre_ref):
    pre_ref[...] = dot(rows_ref[plan.genes :, :], weight, 1, weight_dim)
    for at, ref in enumerate(block_refs):
        owner = chip ^ at
        ref[: plan.gene_rows, :] = dot(
            rows_ref[aligned(owner, plan.gene_rows), :], weight, 1, weight_dim
        ).astype(BF)
        ref[plan.gene_rows :, :] = pre_ref[aligned(owner, plan.pre_block), :].astype(BF)


def project_kernel(plan, me_ref, *refs):
    chips, groups = plan.chips, plan.groups
    pieces, parts, refs = refs[:chips], refs[chips : chips + groups], refs[chips + groups :]
    bias_ref, widen_ref, low_ref, query_ref, pair_ref, weight_ref, pre_ref = refs
    me = me_ref[0]
    collect(plan, me_ref[1], pieces, low_ref, pre_ref)
    collect_weight(plan, me, parts, weight_ref)
    for rows in plan.halves(plan.rows):
        narrow = (dot(low_ref[rows, :], weight_ref[...]) + bias_ref[...]).astype(BF)
        wide = dot(narrow, widen_ref[...]).astype(BF)
        query_ref[rows, :] = wide[:, : plan.lanes]
        pair_ref[rows, :] = wide[:, plan.lanes :]


def order_pairs(plan, core, mine_ref, other_ref, keys_ref, pre_ref):
    for chip in range(plan.chips):
        for ref, place in ((mine_ref, 2 * chip + core), (other_ref, 2 * chip + 1 - core)):
            genes = slice(chip * plan.gene_rows, (chip + 1) * plan.gene_rows)
            keys_ref[aligned(place, plan.gene_rows), :] = ref[genes, :]
            prefix = slice(
                plan.genes + chip * plan.pre_block, plan.genes + (chip + 1) * plan.pre_block
            )
            pre_ref[aligned(place, plan.pre_block), :] = ref[prefix, :].astype(F32)
    keys_ref[2 * plan.genes :, :] = pre_ref[...].astype(BF)


def attend_kernel(plan, me_ref, *refs):
    query_ref, mine_ref, other_ref, select_ref, out_weight_ref = refs[:5]
    keys_ref, mixed_ref, lse_ref = refs[5:8]
    blocks = refs[8 : 8 + plan.chips]
    key_pre_ref, out_pre_ref, turned_ref, score_ref, padded_ref = refs[8 + plan.chips :]
    core = me_ref[2]
    order_pairs(plan, core, mine_ref, other_ref, keys_ref, key_pre_ref)
    for head in range(plan.window):
        at = slice(LANES * head, LANES * (head + 1))
        turned_ref[...] = keys_ref[:, at].astype(F32).T.astype(BF)
        for first, count, key_parts in query_chunks(plan):
            query = query_ref[first : first + count, at]
            top = None
            for start, size, diagonal in key_parts:
                scores = dot(keys_ref[start : start + size, at], query, 1, 1)
                scores = masked(plan, scores, start, diagonal, core)
                score_ref[start : start + size, :count] = scores
                high = jnp.max(scores, axis=0, keepdims=True)
                top = high if top is None else jnp.maximum(top, high)
            top = top * SCALE2
            total, mixed = 0.0, 0.0
            for start, size, _ in key_parts:
                weights = jnp.exp2(score_ref[start : start + size, :count] * SCALE2 - top)
                total = total + jnp.sum(weights, axis=0, keepdims=True)
                mixed = mixed + dot(turned_ref[:, start : start + size], weights.astype(BF))
            padded_ref[first : first + count, at] = (mixed * (1.0 / total)).T.astype(BF)
            lse_ref[head, :, first : first + count] = top + jnp.log2(total)
    mixed_ref[...] = dot(padded_ref[...], select_ref[...]).astype(BF)
    give_blocks(plan, me_ref[1], blocks, mixed_ref, out_weight_ref[...], 0, out_pre_ref)


def attend_back_kernel(plan, me_ref, *refs):
    pieces, refs = refs[: plan.chips], refs[plan.chips :]
    out_weight_ref, query_ref, keys_ref, lse_ref = refs[:4]
    low_ref, query_grad_ref, mine_ref, other_ref, out_bias_ref = refs[4:9]
    pre_ref, grad_ref, turned_ref, prob_ref, pgrad_ref, pair_ref = refs[9:]
    core = me_ref[2]
    collect(plan, me_ref[1], pieces, low_ref, pre_ref)
    out_bias_ref[...] = jnp.sum(low_ref[...].astype(F32), axis=0, keepdims=True)
    for rows in plan.halves(plan.rows):
        grad_ref[rows, :] = dot(low_ref[rows, :], out_weight_ref[...], 1, 1).astype(BF)
    lane = lax.broadcasted_iota(jnp.int32, (1, LANES), 1)
    pair_scale = jnp.where(lane < HALF, SCALE, 1.0)
    for head in range(plan.window):
        at = slice(LANES * head, LANES * (head + 1))
        turned_ref[...] = keys_ref[:, at].astype(F32).T.astype(BF)
        pair_ref[...] = jnp.zeros_like(pair_ref)
        for first, count, key_parts in query_chunks(plan):
            query = query_ref[first : first + count, at]
            grad = grad_ref[first : first + count, at]
            lse = lse_ref[head, :, first : first + count]
            delta = 0.0
            for start, size, diagonal in key_parts:
                pair = keys_ref[start : start + size, at]
                scores = masked(plan, dot(pair, query, 1, 1), start, diagonal, core)
                probs = jnp.exp2(scores * SCALE2 - lse)
                prob_grad = dot(pair, grad, 1, 1)
                delta = delta + jnp.sum(probs * prob_grad, axis=0, keepdims=True)
                prob_ref[start : start + size, :count] = probs
                pgrad_ref[start : start + size, :count] = prob_grad
            query_grad = 0.0
            for start, size, _ in key_parts:
                probs = prob_ref[start : start + size, :count]
                score_grad = (probs * (pgrad_ref[start : start + size, :count] - delta)).astype(BF)
                pair_ref[start : start + size, :] += dot(probs.astype(BF), grad) + dot(score_grad, query)
                query_grad = query_grad + dot(turned_ref[:, start : start + size], score_grad)
            query_grad_ref[first : first + count, at] = (query_grad.T * SCALE).astype(BF)
        for chip in range(plan.chips):
            for ref, place in ((mine_ref, 2 * chip + core), (other_ref, 2 * chip + 1 - core)):
                genes = slice(chip * plan.gene_rows, (chip + 1) * plan.gene_rows)
                ref[genes, at] = (pair_ref[aligned(place, plan.gene_rows), :] * pair_scale).astype(ref.dtype)
                prefix = slice(
                    plan.genes + chip * plan.pre_block, plan.genes + (chip + 1) * plan.pre_block
                )
                place = pl.ds(
                    pl.multiple_of(2 * plan.genes + place * plan.pre_block, plan.pre_block), plan.pre_block
                )
                ref[prefix, at] = (pair_ref[place, :] * pair_scale).astype(ref.dtype)


def project_back_kernel(plan, me_ref, *refs):
    query_grad_ref, mine_ref, other_ref, select_ref, weight_ref, qkv_grad_ref, bias_ref = refs[:7]
    blocks, (pre_ref,) = refs[7 : 7 + plan.chips], refs[7 + plan.chips :]
    for rows in plan.halves(plan.rows):
        pairs = (mine_ref[rows, :] + other_ref[rows, :].astype(F32)).astype(BF)
        qkv_grad_ref[rows, :] = (
            dot(query_grad_ref[rows, :], select_ref[: plan.lanes, :])
            + dot(pairs, select_ref[plan.lanes :, :])
        ).astype(BF)
    bias_ref[...] = jnp.sum(qkv_grad_ref[...].astype(F32), axis=0, keepdims=True)
    give_blocks(plan, me_ref[1], blocks, qkv_grad_ref, weight_ref[...], 1, pre_ref)


ROOT = math.sqrt(2.0 / math.pi)
CUBE = 0.044715


def stack_pieces(plan, pieces, low_ref):
    size = plan.step_rows
    for at, ref in enumerate(pieces):
        low_ref[at * size : at * size + plan.own_rows, :] = ref[...]
        if plan.own_rows < size:
            low_ref[at * size + plan.own_rows : (at + 1) * size, :] = jnp.zeros(
                (size - plan.own_rows, low_ref.shape[1]), BF
            )


def collect_down(plan, level, core, mine_ref, other_ref, down_ref):
    if plan.hidden % 16 == 0:
        down_ref[aligned(core, plan.hidden), :] = mine_ref[level]
        down_ref[aligned(1 - core, plan.hidden), :] = other_ref[level]
        return
    mine, other = mine_ref[level].astype(F32), other_ref[level].astype(F32)
    halves = [jnp.where(core == 0, mine, other), jnp.where(core == 0, other, mine)]
    down_ref[...] = jnp.concatenate(halves, 0).astype(BF)


def lift_kernel(plan, level, me_ref, *refs):
    chips, groups = plan.chips, plan.groups
    pieces, parts, refs = refs[:chips], refs[chips : chips + groups], refs[chips + groups :]
    bias_ref, mine_ref, other_ref, low_ref, pre_ref, active_ref, up_ref = refs[:7]
    blocks, (down_ref,) = refs[7:-1], refs[-1:]
    collect_weight(plan, me_ref[0], parts, up_ref)
    collect_down(plan, level, me_ref[2], mine_ref, other_ref, down_ref)
    stack_pieces(plan, pieces, low_ref)
    size = plan.step_rows
    for first in range(0, plan.all_rows, 2 * size):
        rows = slice(first, first + 2 * size)
        pre = dot(low_ref[rows, :], up_ref[...]) + bias_ref[...]
        pre_ref[rows, :] = pre
        active = (0.5 * pre * (1.0 + jnp.tanh(ROOT * (pre + CUBE * pre * pre * pre)))).astype(BF)
        active_ref[rows, :] = active
        lifted = dot(active, down_ref[...])
        for at in range(2):
            blocks[first // size + at][...] = lifted[at * size : at * size + plan.own_rows].astype(BF)


def lift_back_kernel(plan, level, me_ref, *refs):
    pieces, refs = refs[: plan.chips], refs[plan.chips :]
    up_ref, pre_ref, mine_ref, other_ref, low_ref, pre_grad_ref, down_bias_ref, up_bias_ref = refs[:8]
    blocks, (down_ref,) = refs[8:-1], refs[-1:]
    collect_down(plan, level, me_ref[2], mine_ref, other_ref, down_ref)
    stack_pieces(plan, pieces, low_ref)
    size = plan.step_rows
    down_bias_ref[...] = jnp.sum(low_ref[...].astype(F32), axis=0, keepdims=True)
    up_bias = 0.0
    for first in range(0, plan.all_rows, 2 * size):
        rows = slice(first, first + 2 * size)
        act_grad = dot(low_ref[rows, :], down_ref[...], 1, 1)
        pre = pre_ref[rows, :]
        square = pre * pre
        turn = jnp.tanh(ROOT * pre * (1.0 + CUBE * square))
        slope = 0.5 * (1.0 + turn) + (0.5 * ROOT) * pre * (1.0 - turn * turn) * (1.0 + 3.0 * CUBE * square)
        pre_grad = (act_grad * slope).astype(BF)
        pre_grad_ref[rows, :] = pre_grad
        up_bias = up_bias + jnp.sum(pre_grad.astype(F32), axis=0, keepdims=True)
        norm_grad = dot(pre_grad, up_ref[...], 1, 1)
        for at in range(2):
            blocks[first // size + at][...] = norm_grad[at * size : at * size + plan.own_rows].astype(BF)
    up_bias_ref[...] = up_bias


def send_kernel(plan, level, starts, width, me_ref, weight_ref, *refs):
    outs, (stack_ref,) = refs[: plan.chips], refs[plan.chips :]
    for to, begins in enumerate(starts):
        for at, begin in enumerate(begins):
            stack_ref[to, : plan.cols, at * width : (at + 1) * width] = weight_ref[
                level, :, begin : begin + width
            ]
        if plan.cols < plan.part:
            stack_ref[to, plan.cols :, :] = jnp.zeros(
                (plan.part - plan.cols, stack_ref.shape[2]), BF
            )
    for at, ref in enumerate(outs):
        ref[...] = stack_ref[me_ref[1] ^ at]


def weight_grad_kernel(plan, me_ref, left_ref, right_ref, weight_ref, sums_ref, vector_ref, *refs):
    passengers, (mine_ref, other_ref, whole_ref) = refs[:-3], refs[-3:]
    width = right_ref.shape[1]
    step = 2 * plan.part
    for first in range(0, plan.features, step):
        rows = slice(first, first + step)
        product = dot(left_ref[:, rows], right_ref[...], 0, 0)
        weight = weight_ref[rows, :].astype(F32)
        shift_grad = jnp.sum(weight * sums_ref[...], axis=1, keepdims=True)
        both = jnp.sum(weight * product, axis=1, keepdims=True)
        turned = vector_ref[:, rows].T
        gain_grad = (both - turned[:, 0:1] * shift_grad) / turned[:, 1:2]
        whole_ref[rows, :width] = product
        whole_ref[rows, width : width + 2] = jnp.concatenate([shift_grad, gain_grad], 1)
    for at in range(plan.chips):
        owner = me_ref[0] ^ (2 * at)
        mine_ref[at, :, : width + 2] = whole_ref[aligned(owner, plan.part), :].astype(BF)
        other_ref[at, :, : width + 2] = whole_ref[aligned(owner ^ 1, plan.part), :].astype(BF)
        for ref, rider in zip((mine_ref, other_ref), passengers):
            rows = rider.shape[0]
            lanes = slice(at * plan.chip_cols, (at + 1) * plan.chip_cols)
            filler = jnp.zeros((plan.part - rows, plan.chip_cols), F32)
            ref[at, :, width + 2 :] = jnp.concatenate([rider[:, lanes], filler], 0).astype(BF)


def join_kernel(plan, blocks, width, me_ref, *refs):
    parts, (out_ref, vector_ref) = refs[:LAYERS], refs[LAYERS:]
    each = width // blocks
    for level, ref in enumerate(parts):
        vectors = 0.0
        for source in range(plan.chips):
            value = ref[me_ref[1] ^ source].astype(F32)
            for block in range(blocks):
                begin = (block * plan.chips + source) * each
                out_ref[:, level, begin : begin + each] = value[
                    : plan.cols, block * each : (block + 1) * each
                ]
            vectors = vectors + value[:, width : width + 2]
        padded = jnp.concatenate([vectors, jnp.zeros((plan.part, LANES - 2), F32)], 1)
        vector_ref[level] = padded.T[:8]


def body(
    genes,
    prefix,
    cot_genes,
    cot_prefix,
    w_qkv,
    w_out,
    w_up,
    w_down,
    norm1_gain,
    norm1_bias,
    norm2_gain,
    norm2_bias,
    bias_q,
    bias_v,
    bias_out,
    bias_up,
    bias_down,
):
    groups = lax.axis_size("gene")
    cells = lax.axis_size("cell")
    me = lax.axis_index("gene")
    cell = lax.axis_index("cell")
    chip, core = me // 2, me % 2
    plan = Plan(groups, genes.shape[1])
    chips, cols, chip_cols, wide = plan.chips, plan.cols, plan.chip_cols, plan.wide
    hidden, chip_hidden = plan.hidden, plan.chip_hidden
    first_head = jnp.asarray(plan.first_heads, jnp.int32)[chip]
    offset = chip * chip_cols - first_head * HEAD_DIM
    turn = chip if plan.by_links else jnp.zeros_like(chip)
    where = jnp.stack([2 * turn + core, turn, core]).astype(jnp.int32)
    same_core = [[2 * at + one for at in range(chips)] for one in range(2)]
    here = functools.partial

    def after(value, *others):
        return lax.optimization_barrier((value,) + others)[0]

    def after_all(values, *others):
        return list(lax.optimization_barrier((tuple(values), others))[0])

    def together(*lists):
        return [list(got) for got in lax.optimization_barrier(tuple(tuple(x) for x in lists))]

    def swap(value, bits):
        return lax.ppermute(value, "gene", [(at, at ^ bits) for at in range(groups)])

    def to_chips(parts):
        if not plan.by_links:
            got = lax.all_to_all(jnp.stack(parts), "gene", 0, 0, axis_index_groups=same_core)
            return [got[at] for at in range(chips)]
        return [parts[0]] + [swap(parts[at], 2 * at) for at in range(1, chips)]

    def gather(piece):
        if not plan.by_links:
            got = lax.all_gather(piece, "gene", axis=0, axis_index_groups=same_core)
            return [got[at] for at in range(chips)]
        return to_chips([piece] * chips)

    def scatter(blocks):
        if not plan.by_links:
            return [
                lax.psum_scatter(
                    jnp.stack(blocks), "gene", scatter_dimension=0, axis_index_groups=same_core
                )
            ]
        return to_chips(blocks)

    def across(near):
        far = [swap(value, 1) for value in near]
        return [value for pair in zip(near, far) for value in pair]

    class CellSum:
        def __init__(self, mine, other, *steps):
            self.value = (mine.astype(F32) + other.astype(F32)).astype(BF)
            self.steps = list(steps) if cells == 4 else [steps[-1]]
            waiting.append(self)

        def move(self):
            if cells != 4:
                return lax.psum(self.value, "cell")
            inwards, between, outwards = [(0, 1), (3, 2)], [(1, 2), (2, 1)], [(1, 0), (2, 3)]
            pairs = {3: inwards, 2: between, 1: outwards}[len(self.steps)]
            return lax.ppermute(self.value, "cell", pairs)

        def land(self, got):
            if cells != 4:
                self.value = got
            elif len(self.steps) > 1:
                self.value = (self.value.astype(F32) + got.astype(F32)).astype(BF)
            else:
                self.value = jnp.where((cell == 1) | (cell == 2), self.value, got)
            self.steps.pop(0)

    waiting = []

    def beside(step, *lists):
        moving = [item for item in waiting if item.steps and item.steps[0] == step]
        *lists, landed = together(*lists, [item.move() for item in moving])
        for item, got in zip(moving, landed):
            item.land(got)
        return lists

    def send(weight, level, starts, width, *others):
        total = len(starts[0]) * width
        return call(
            here(send_kernel, plan, level, starts, width),
            "send",
            [after(where, *others), weight],
            [shape_of(plan.part, total)] * chips,
            [pltpu.VMEM((chips, plan.part, total), BF)],
            True,
        )

    qkv_starts = [
        [block * D + head * HEAD_DIM for block in range(3)] for head in plan.first_heads
    ]
    up_starts = [[to * chip_hidden] for to in range(chips)]

    def chooser(wanted, there):
        return (wanted[:, None] == there[None, :]).astype(BF)

    def own_of(block, column, real):
        ok = real & (column >= offset) & (column < offset + chip_cols)
        return jnp.where(ok, block * chip_cols + column - offset, -1)

    window_at = jnp.arange(3 * wide)
    block, column = window_at // wide, window_at % wide
    lane = (column // HEAD_DIM) * LANES + column % HEAD_DIM
    lane = lane + jnp.where(block == 0, 0, plan.lanes + HALF * (block - 1))
    widen = chooser(lane, jnp.arange(2 * plan.lanes))
    own_columns = jnp.arange(3 * chip_cols)
    cut = chooser(own_of(block, column, True), own_columns)
    lanes = jnp.arange(2 * plan.lanes)
    inner = lanes % LANES
    is_pair = lanes >= plan.lanes
    block = jnp.where(is_pair, 1 + inner // HALF, 0)
    inner = jnp.where(is_pair, inner % HALF, inner)
    column = (lanes % plan.lanes) // LANES * HEAD_DIM + inner
    select = chooser(own_of(block, column, inner < HEAD_DIM), own_columns)
    at_out = jnp.arange(plan.lanes)
    inner = at_out % LANES - HALF
    out_col = (at_out // LANES) * HEAD_DIM + inner
    out_ok = (inner >= 0) & (inner < HEAD_DIM)
    out_select = chooser(own_of(0, out_col, out_ok), jnp.arange(chip_cols))

    def by_core(mine, other):
        first, second = jnp.where(core == 0, mine, other), jnp.where(core == 0, other, mine)
        return jnp.concatenate([first, second], 1)

    def out_windows(chip_out):
        if plan.by_links:
            rows, owner = chip_out, chip * chip_cols + jnp.arange(chip_cols)
        else:
            rows = lax.all_gather(w_out, "gene", axis=1, tiled=True)
            owner = jnp.arange(D)
        pick = chooser(jnp.where(out_ok, first_head * HEAD_DIM + out_col, -1), owner)
        return [dot(pick, rows[level]).astype(BF) for level in range(LAYERS)]

    def window_of(vec):
        return lax.dynamic_slice_in_dim(vec, first_head * HEAD_DIM, wide, 1)

    def norm_vectors(token):
        every = jnp.stack([norm1_bias, norm1_gain, norm2_bias, norm2_gain])
        every = after(every, token).reshape(2, 2, LAYERS, groups, cols)
        every = jnp.pad(every, ((0, 0),) * 4 + ((0, plan.part - cols),), constant_values=1.0)
        every = every.transpose(0, 2, 1, 3, 4).reshape(2 * LAYERS, 2, plan.features)
        every = jnp.pad(every, ((0, 0), (0, 6), (0, 0)))
        return [every[at] for at in range(2 * LAYERS)]

    def up_biases_of(token):
        return lax.dynamic_slice_in_dim(after(bias_up, token), chip * chip_hidden, chip_hidden, 1)

    rows_f32 = shape_of(plan.own_rows, D, dtype=F32)
    normed_like = shape_of(plan.own_rows, plan.features)
    grad_like = shape_of(plan.own_rows, D)
    row_blocks = [grad_like] * chips
    feature_blocks = [normed_like] * chips
    vector = shape_of(1, D, dtype=F32)
    ends_like = [
        shape_of(D, plan.gene_rows, dtype=F32),
        shape_of(plan.pre_block, D, dtype=F32),
    ]

    own_prefix = lax.dynamic_slice_in_dim(prefix[0], me * plan.pre_rows, plan.pre_rows, 0)
    filler = ((0, plan.pre_block - plan.pre_rows), (0, 0))
    rows, piece = call(
        here(begin_kernel, plan),
        "begin",
        [genes[0].T, jnp.pad(own_prefix, filler), norm1_gain, norm1_bias],
        [rows_f32, normed_like],
    )
    qkv_parts, up_parts = [None] * LAYERS, [None] * LAYERS
    qkv_sent = send(w_qkv, 0, qkv_starts, wide, piece)
    pieces, near = gather(piece), to_chips(qkv_sent)
    token = qkv_sent[-1]
    up_sent = send(w_up, 0, up_starts, chip_hidden, token)
    qkv_biases = jnp.concatenate(
        [window_of(bias_q), jnp.zeros((LAYERS, wide), F32), window_of(bias_v)], 1
    )
    held_out = after(w_out, token)
    chip_out = by_core(held_out, swap(held_out, 1))
    out_weights = [chip_out[level] for level in range(LAYERS)]
    pieces, near, up_sent, _ = together(
        pieces, near, up_sent, [widen, out_select, qkv_biases] + out_weights
    )
    (qkv_parts[0],) = together(across(near))

    saved = []
    for level in range(LAYERS):
        last = level + 1 == LAYERS
        if level:
            (pieces, far) = together(gather(piece), across(near[chips // 2 :]))
            qkv_parts[level] = qkv_far + far
        up_near = to_chips(after_all(up_sent, *pieces, *qkv_parts[level]))
        low_one, query, pair, qkv_weight = call(
            here(project_kernel, plan),
            "project",
            [where] + pieces + qkv_parts[level] + [qkv_biases[level : level + 1], widen],
            [
                shape_of(plan.rows, plan.features),
                shape_of(plan.rows, plan.lanes),
                shape_of(plan.rows, plan.lanes),
                shape_of(plan.features, 3 * wide),
            ],
            [pltpu.VMEM((plan.prefix, plan.features), F32)],
            True,
        )
        outs = call(
            here(attend_kernel, plan),
            "attend",
            [where, query, pair, swap(pair, 1), out_select, out_weights[level]],
            [
                shape_of(2 * plan.rows, plan.lanes),
                shape_of(plan.rows, chip_cols),
                shape_of(plan.window, 1, plan.rows, dtype=F32),
            ]
            + row_blocks,
            [
                pltpu.VMEM((2 * plan.prefix, plan.lanes), F32),
                pltpu.VMEM((plan.prefix, D), F32),
                pltpu.VMEM((LANES, 2 * plan.rows), BF),
                pltpu.VMEM((2 * plan.rows, plan.gene_rows), F32),
                pltpu.VMEM((plan.rows, plan.lanes), BF),
            ],
            True,
        )
        outs, up_near = together(outs, up_near)
        keys, mixed, lse = outs[:3]
        spare = []
        if level == 0:
            spare = [swap(after(w_down, mixed), 1), up_biases_of(mixed)]
        if not last:
            spare = spare + send(w_qkv, level + 1, qkv_starts, wide, mixed)
        parts, up_far, spare = together(scatter(outs[3:]), across(up_near[: chips // 2]), spare)
        if level == 0:
            other_down, up_biases = spare[:2]
        qkv_sent = spare[-chips:]
        middle, piece = call(
            here(middle_kernel, plan, len(parts), level, level),
            "middle",
            parts + [rows, bias_out, norm2_gain, norm2_bias],
            [rows_f32, normed_like],
        )
        if last:
            cot_grad, cot_piece = call(
                here(cot_kernel, plan),
                "cotangent",
                [after(cot_genes[0].T, piece), jnp.pad(cot_prefix[0], filler)],
                [rows_f32, grad_like],
            )
            spare = [cot_grad, cot_piece]
        else:
            spare = send(w_up, level + 1, up_starts, chip_hidden, piece)
        pieces, far, spare = together(gather(piece), across(up_near[chips // 2 :]), spare)
        up_parts[level] = up_far + far
        if last:
            cot_grad, cot_piece = spare
            near = gather(after(cot_piece, *pieces))
        else:
            up_sent = spare
            near = to_chips(after_all(qkv_sent, *pieces))
        outs = call(
            here(lift_kernel, plan, level),
            "lift",
            [where]
            + pieces
            + up_parts[level]
            + [up_biases[level : level + 1], w_down, other_down],
            [
                shape_of(plan.all_rows, plan.features),
                shape_of(plan.all_rows, chip_hidden, dtype=F32),
                shape_of(plan.all_rows, chip_hidden),
                shape_of(plan.features, chip_hidden),
            ]
            + row_blocks,
            [pltpu.VMEM((chip_hidden, D), BF)],
            True,
        )
        outs, near = together(outs, near)
        low_two, pre_act, active, up_weight = outs[:4]
        saved.append(
            (rows, low_one, query, keys, mixed, lse, qkv_weight, middle, low_two, pre_act, active, up_weight)
        )
        if last:
            cot_pieces = near
            last_blocks, last_middle = outs[4:], middle
        else:
            spare = []
            if level == 0:
                spare = out_windows(after(chip_out, low_two)) + [select] + norm_vectors(low_two)
            parts, qkv_far, spare = together(scatter(outs[4:]), across(near[: chips // 2]), spare)
            if level == 0:
                windows, select, vectors = spare[:LAYERS], spare[LAYERS], spare[LAYERS + 1 :]
            rows, piece = call(
                here(middle_kernel, plan, len(parts), level, level + 1),
                "next_rows",
                parts + [middle, bias_down, norm1_gain, norm1_bias],
                [rows_f32, normed_like],
            )

    def of_cores(value, size, dim):
        return [
            lax.dynamic_slice_in_dim(value, at * size, size, dim) for at in (core, 1 - core)
        ]

    grad, pieces = cot_grad, cot_pieces
    down_sums, up_sums, qkv_sums = ([None] * LAYERS for _ in range(3))
    long_rows, short_rows, up_rows = [None] * (2 * LAYERS), [None] * (2 * LAYERS), [None] * LAYERS
    for level in reversed(range(LAYERS)):
        rows, low_one, query, keys, mixed, lse, qkv_weight, middle, low_two, pre_act, active, up_weight = saved[level]
        if level + 1 < LAYERS:
            (pieces,) = beside(f"rows {level}", gather(piece))
        outs = call(
            here(lift_back_kernel, plan, level),
            "lift_back",
            [where] + pieces + [up_weight, pre_act, w_down, other_down],
            [
                shape_of(plan.all_rows, D),
                shape_of(plan.all_rows, chip_hidden),
                vector,
                shape_of(1, chip_hidden, dtype=F32),
            ]
            + feature_blocks,
            [pltpu.VMEM((chip_hidden, D), BF)],
            True,
        )
        (outs,) = beside(f"lifted {level}", outs)
        low_grad, pre_grad, long_rows[level], up_rows[level] = outs[:4]
        up_mine, up_other = call(
            here(weight_grad_kernel, plan),
            "up_grad",
            [where, low_two, pre_grad, up_weight, up_rows[level], vectors[LAYERS + level]],
            [shape_of(chips, plan.part, chip_hidden + 2)] * 2,
            [pltpu.VMEM((plan.features, chip_hidden + 2), F32)],
            True,
        )
        down_mine, down_other = of_cores(dot(active, low_grad, 0, 0).astype(BF), hidden, 0)
        parts, (up_mine, up_other, down_mine, down_other) = beside(
            f"lift {level}", scatter(outs[4:]), [up_mine, up_other, down_mine, down_other]
        )
        middle_grad, piece = call(
            here(back_kernel, plan, len(parts), level),
            "middle_back",
            parts + [middle, norm2_gain, grad],
            [rows_f32, grad_like],
        )
        (middle_grad, piece, up_got, down_got), = beside(
            f"turn {level}", [middle_grad, piece, swap(up_other, 1), swap(down_other, 1)]
        )
        if level:
            down_sums[level] = CellSum(down_mine, down_got, "attend 1", "project 1", "lifted 0")
            up_sums[level] = CellSum(up_mine, up_got, "project 1", "lifted 0", "turn 0")
        else:
            down_sums[level] = CellSum(down_mine, down_got, "attend 0", "qkv 0", "end 1")
            up_sums[level] = CellSum(up_mine, up_got, "qkv 0", "end 1", "end 2")
        (pieces,) = beside(f"middle {level}", gather(piece))
        outs = call(
            here(attend_back_kernel, plan),
            "attend_back",
            [where] + pieces + [windows[level], query, keys, lse],
            [
                shape_of(plan.rows, D),
                shape_of(plan.rows, plan.lanes),
                shape_of(plan.rows, plan.lanes, dtype=F32),
                shape_of(plan.rows, plan.lanes),
                vector,
            ],
            [
                pltpu.VMEM((plan.prefix, D), F32),
                pltpu.VMEM((plan.rows, plan.lanes), BF),
                pltpu.VMEM((LANES, 2 * plan.rows), BF),
                pltpu.VMEM((2 * plan.rows, plan.gene_rows), F32),
                pltpu.VMEM((2 * plan.rows, plan.gene_rows), F32),
                pltpu.VMEM((2 * plan.rows, LANES), F32),
            ],
            True,
        )
        (outs,) = beside(f"attend {level}", outs)
        low_grad, query_grad, pair_mine, pair_other, long_rows[LAYERS + level] = outs
        own_weight = qkv_weight
        if wide != chip_cols:
            own_weight = dot(qkv_weight, cut).astype(BF)
        outs = call(
            here(project_back_kernel, plan),
            "project_back",
            [where, query_grad, pair_mine, swap(pair_other, 1), select, own_weight],
            [shape_of(plan.rows, 3 * chip_cols), shape_of(1, 3 * chip_cols, dtype=F32)]
            + feature_blocks,
            [pltpu.VMEM((plan.prefix, plan.features), F32)],
            True,
        )
        qkv_grad, qkv_bias = outs[:2]
        short_rows[level] = qkv_bias[:, :chip_cols]
        short_rows[LAYERS + level] = qkv_bias[:, 2 * chip_cols :]
        riders = of_cores(dot(mixed, low_grad, 0, 0), cols, 0)
        if not level:
            long_own = lax.dynamic_slice_in_dim(
                jnp.concatenate(long_rows, 0), chip * chip_cols, chip_cols, 1
            )
            small = [
                jnp.concatenate([vec.reshape(-1) for vec in vecs])
                for vecs in zip(
                    of_cores(long_own, cols, 1),
                    of_cores(jnp.concatenate(short_rows, 0), cols, 1),
                    of_cores(jnp.concatenate(up_rows, 0), hidden, 1),
                )
            ]
            extra = -(-small[0].size // D)
            small = [jnp.pad(vec, (0, extra * D - vec.size)).reshape(extra, D) for vec in small]
            riders = [jnp.concatenate(pair, 0) for pair in zip(riders, small)]
        width = 3 * chip_cols + 2 + chip_cols
        qkv_mine, qkv_other = call(
            here(weight_grad_kernel, plan),
            "qkv_grad",
            [where, low_one, qkv_grad, own_weight, qkv_bias, vectors[level]] + riders,
            [shape_of(chips, plan.part, width)] * 2,
            [pltpu.VMEM((plan.features, 3 * chip_cols + 2), F32)],
            True,
        )
        parts = scatter(outs[2:])
        if level:
            parts, (qkv_mine, qkv_other) = beside(
                "project 1", parts, [qkv_mine, qkv_other]
            )
            grad, piece = call(
                here(back_kernel, plan, len(parts), level),
                "rows_back",
                parts + [rows, norm1_gain, middle_grad],
                [rows_f32, grad_like],
            )
            grad, piece, qkv_got = together([grad, piece, swap(qkv_other, 1)])[0]
            qkv_sums[level] = [CellSum(qkv_mine, qkv_got, "turn 0", "attend 0", "qkv 0")]

    def messages_of(item, width):
        return [item.value[at, :, :width] for at in range(chips)]

    ((qkv_mine, qkv_other),) = beside("qkv 0", [qkv_mine, qkv_other])
    (qkv_got,) = together([swap(qkv_other, 1)])[0]
    qkv_sums[0] = [CellSum(qkv_mine, qkv_got, "end 1", "end 2", "end 3")]
    (parts,) = beside("end 1", parts)
    ends = call(
        here(back_end_kernel, plan, len(parts), 0),
        "rows_back_end",
        parts + [rows, norm1_gain, middle_grad],
        ends_like,
    )
    up_width, qkv_width = chip_hidden + 2, 3 * chip_cols + 2
    parts, ends = beside(
        "end 2",
        scatter(after_all(last_blocks, parts[0])),
        ends,
    )
    result = call(
        here(finish_kernel, plan, len(parts), LAYERS - 1),
        "finish",
        parts + [last_middle, bias_down],
        ends_like,
    )
    near, far, result = beside(
        "end 3",
        to_chips(after_all(messages_of(up_sums[1], up_width), result[0])),
        to_chips(after_all(messages_of(qkv_sums[1][0], qkv_width), result[0])),
        result,
    )
    last_near = to_chips(messages_of(qkv_sums[0][0], qkv_width))
    last_up = to_chips(messages_of(up_sums[0], up_width))
    up_parts = [jnp.stack(last_up), jnp.stack(near)]
    qkv_parts = [jnp.stack(last_near), jnp.stack(far)]
    out_sums = []
    for items in qkv_sums:
        riders = [items[0].value[at, :, qkv_width:] for at in range(chips)]
        out_sums.append(jnp.concatenate(riders, 1))
    small = out_sums[0][cols : cols + extra].reshape(-1).astype(F32)
    out_sums = [value[:cols] for value in out_sums]
    down_sums = [item.value for item in down_sums]
    size = LAYERS * cols
    b_down, b_out, b_q, b_v = (small[at * size : (at + 1) * size].reshape(LAYERS, cols) for at in range(4))
    b_up = small[4 * size : 4 * size + LAYERS * hidden].reshape(LAYERS, hidden)

    def join(parts, blocks, width):
        whole, vectors = call(
            here(join_kernel, plan, blocks, width),
            "join",
            [where] + parts,
            [
                shape_of(cols, LAYERS, blocks * D if blocks > 1 else FF, dtype=F32),
                shape_of(LAYERS, 8, plan.part, dtype=F32),
            ],
            scalar=True,
        )
        return whole.transpose(1, 0, 2), vectors[:, 0, :cols], vectors[:, 1, :cols]

    g_up, shift_two, gain_two = join(up_parts, 1, chip_hidden)
    g_qkv, shift_one, gain_one = join(qkv_parts, 3, 3 * chip_cols)
    return (
        result[0].T[None],
        result[1][: plan.pre_rows][None],
        ends[0].T[None],
        ends[1][: plan.pre_rows][None],
        g_qkv,
        jnp.stack(out_sums).astype(F32),
        g_up,
        jnp.stack(down_sums).astype(F32),
        gain_one,
        shift_one,
        gain_two,
        shift_two,
        b_q,
        b_v,
        b_out,
        b_up,
        b_down,
    )


def solution(mesh):
    rows = P("cell", "gene", None)
    weight = P(None, "gene", None)
    vector = P(None, "gene")
    return jax.shard_map(
        body,
        mesh=mesh,
        in_specs=(rows, P("cell", None, None), rows, rows) + (weight,) * 4 + (P(),) * 9,
        out_specs=(rows,) * 4 + (weight,) * 4 + (vector,) * 9,
        check_vma=False,
    )
```

```python
import functools
import math

import jax
import jax.numpy as jnp
from jax import lax
from jax.experimental import pallas as pl
from jax.experimental.pallas import tpu as pltpu
from jax.sharding import PartitionSpec as P

D = 1120
HEADS = 20
HEAD_DIM = 56
FF = 4480
PREFIX = 64
LAYERS = 2
LANES = 128
HALF = 64
SCALE = HEAD_DIM ** (-0.5)
SCALE2 = SCALE * math.log2(math.e)
BF = jnp.bfloat16
F32 = jnp.float32
COST = 1000


def dot(left, right, left_dim=1, right_dim=0):
    return lax.dot_general(
        left, right, (((left_dim,), (right_dim,)), ((), ())), preferred_element_type=F32
    )


class Plan:
    def __init__(self, groups, gene_rows):
        self.groups = groups
        self.chips = groups // 2
        self.gene_rows = gene_rows
        self.pre_rows = PREFIX // groups
        self.pre_block = -(-self.pre_rows // 8) * 8
        self.own_rows = gene_rows + self.pre_block
        self.step_rows = -(-self.own_rows // 16) * 16
        self.genes = self.chips * gene_rows
        self.prefix = self.chips * self.pre_block
        self.rows = self.genes + self.prefix
        self.all_rows = self.chips * self.step_rows
        self.cols = D // groups
        self.chip_cols = D // self.chips
        self.hidden = FF // groups
        self.chip_hidden = FF // self.chips
        self.part = -(-self.cols // 16) * 16
        self.features = groups * self.part
        spans = [
            (self.chip_cols * at // HEAD_DIM, -(-self.chip_cols * (at + 1) // HEAD_DIM))
            for at in range(self.chips)
        ]
        self.window = max(last - first for first, last in spans)
        self.first_heads = [min(first, HEADS - self.window) for first, _ in spans]
        self.wide = self.window * HEAD_DIM
        self.lanes = self.window * LANES
        self.whole = self.wide == self.chip_cols
        self.by_links = groups == 8

    def halves(self, total):
        step = -(-total // 32) * 16
        return [slice(first, min(first + step, total)) for first in range(0, total, step)]


SCALAR = pl.BlockSpec(memory_space=pltpu.SMEM)
WHOLE = pl.BlockSpec(memory_space=pltpu.VMEM)


def call(kernel, name, args, outs, scratch=(), scalar=False):
    got = pl.pallas_call(
        kernel,
        in_specs=[SCALAR if scalar and at == 0 else WHOLE for at in range(len(args))],
        out_specs=[WHOLE] * len(outs),
        out_shape=outs,
        scratch_shapes=list(scratch),
        compiler_params=pltpu.CompilerParams(vmem_limit_bytes=58 << 20),
        cost_estimate=pl.CostEstimate(flops=COST, bytes_accessed=COST, transcendentals=0),
        name=name,
    )(*args)
    return list(got)


def shape_of(*dims, dtype=BF):
    return jax.ShapeDtypeStruct(dims, dtype)


def aligned(at, size):
    return pl.ds(pl.multiple_of(at * size, size), size)


def normed_of(values):
    centred = values - jnp.mean(values, axis=-1, keepdims=True)
    variance = jnp.mean(centred * centred, axis=-1, keepdims=True)
    inverse = lax.rsqrt(variance + 1e-05)
    return centred * inverse, inverse


def spread(plan, rows):
    filler = jnp.zeros((rows.shape[0], plan.part - plan.cols), rows.dtype)
    parts = []
    for at in range(plan.groups):
        parts += [rows[:, at * plan.cols : (at + 1) * plan.cols], filler]
    return jnp.concatenate(parts, 1)


def unspread(plan, rows):
    return jnp.concatenate(
        [rows[:, at * plan.part : at * plan.part + plan.cols] for at in range(plan.groups)], 1
    )


def real_rows(plan, rows):
    if plan.pre_rows == plan.pre_block:
        return rows
    at = lax.broadcasted_iota(jnp.int32, rows.shape, 0)
    return jnp.where(at < plan.gene_rows + plan.pre_rows, rows, 0.0)


def normed_piece(plan, rows, gain_ref, shift_ref, level):
    unit, _ = normed_of(rows)
    normed = unit * gain_ref[level : level + 1, :] + shift_ref[level : level + 1, :]
    return spread(plan, real_rows(plan, normed)).astype(BF)


def begin_kernel(plan, gene_ref, pre_ref, gain_ref, shift_ref, rows_ref, piece_ref):
    rows = jnp.concatenate([gene_ref[...].astype(F32).T, pre_ref[...].astype(F32)], 0)
    rows_ref[...] = rows
    piece_ref[...] = normed_piece(plan, rows, gain_ref, shift_ref, 0)


def add_parts(refs):
    total = refs[0][...].astype(F32)
    for ref in refs[1:]:
        total = total + ref[...].astype(F32)
    return total


def middle_kernel(plan, parts, level, gain_level, *refs):
    part_refs, (base_ref, bias_ref, gain_ref, shift_ref, rows_ref, piece_ref) = (
        refs[:parts],
        refs[parts:],
    )
    rows = base_ref[...] + add_parts(part_refs) + bias_ref[level : level + 1, :]
    rows_ref[...] = rows
    piece_ref[...] = normed_piece(plan, rows, gain_ref, shift_ref, gain_level)


def finish_kernel(plan, parts, level, *refs):
    part_refs, (base_ref, bias_ref, gene_ref, pre_ref) = refs[:parts], refs[parts:]
    rows = base_ref[...] + add_parts(part_refs) + bias_ref[level : level + 1, :]
    gene_ref[...] = rows[: plan.gene_rows].T
    pre_ref[...] = rows[plan.gene_rows :]


def norm_back(plan, parts, level, refs):
    part_refs, (x_ref, gain_ref, base_ref) = refs[:parts], refs[parts : parts + 3]
    grad_norm = unspread(plan, add_parts(part_refs))
    unit, inverse = normed_of(x_ref[...])
    scaled = grad_norm * gain_ref[level : level + 1, :]
    return base_ref[...] + inverse * (
        scaled
        - jnp.mean(scaled, axis=-1, keepdims=True)
        - unit * jnp.mean(scaled * unit, axis=-1, keepdims=True)
    )


def back_kernel(plan, parts, level, *refs):
    grad = norm_back(plan, parts, level, refs)
    grad_ref, piece_ref = refs[parts + 3 :]
    grad_ref[...] = grad
    piece_ref[...] = real_rows(plan, grad).astype(BF)


def back_end_kernel(plan, parts, level, *refs):
    grad = norm_back(plan, parts, level, refs)
    gene_ref, pre_ref = refs[parts + 3 :]
    gene_ref[...] = grad[: plan.gene_rows].T
    pre_ref[...] = grad[plan.gene_rows :]


def cot_kernel(plan, gene_ref, pre_ref, rows_ref, piece_ref):
    rows = jnp.concatenate([gene_ref[...].T, pre_ref[...]], 0)
    rows_ref[...] = rows
    piece_ref[...] = real_rows(plan, rows).astype(BF)


def query_chunks(plan):
    both, genes = 2 * plan.gene_rows, 2 * plan.genes
    chunks = []
    for chip in range(0, plan.chips, 2):
        blocks = [(genes, 2 * plan.prefix, False)]
        blocks += [
            (start, both, start >= chip * both) for start in range(0, (chip + 2) * both, both)
        ]
        chunks.append((chip * plan.gene_rows, both, blocks))
    chunks.append((plan.genes, plan.prefix, [(genes, 2 * plan.prefix, True)]))
    return chunks


def masked(plan, scores, start, diagonal, core):
    in_prefix = start == 2 * plan.genes
    holes = in_prefix and plan.pre_rows < plan.pre_block
    if not (diagonal or holes):
        return scores
    key_at = lax.broadcasted_iota(jnp.int32, scores.shape, 0)
    query_at = lax.broadcasted_iota(jnp.int32, scores.shape, 1)
    keep = None
    if diagonal:
        block = plan.pre_block if in_prefix else plan.gene_rows
        inner = lax.rem(query_at, block)
        before = 0 if in_prefix else start % (4 * block)
        keep = key_at <= 2 * query_at - inner + core * block - before
    if holes:
        real = lax.rem(key_at, plan.pre_block) < plan.pre_rows
        keep = real if keep is None else keep & real
    return jnp.where(keep, scores, -jnp.inf)


def collect(plan, chip, piece_refs, whole_ref, pre_ref):
    for at, ref in enumerate(piece_refs):
        owner = chip ^ at
        whole_ref[aligned(owner, plan.gene_rows), :] = ref[: plan.gene_rows, :]
        pre_ref[aligned(owner, plan.pre_block), :] = ref[plan.gene_rows :, :].astype(F32)
    whole_ref[plan.genes :, :] = pre_ref[...].astype(BF)


def collect_weight(plan, me, part_refs, weight_ref):
    for at, ref in enumerate(part_refs):
        weight_ref[aligned(me ^ at, plan.part), :] = ref[...]


def collect_own(plan, me, part_refs, cut_refs, own_ref, weight_ref):
    collect_weight(plan, me, part_refs, own_ref if plan.whole else weight_ref)
    if not plan.whole:
        own_ref[...] = dot(weight_ref[...], cut_refs[0][...]).astype(BF)


def give_blocks(plan, chip, block_refs, rows_ref, weight, weight_dim, pre_ref):
    pre_ref[...] = dot(rows_ref[plan.genes :, :], weight, 1, weight_dim)
    for at, ref in enumerate(block_refs):
        owner = chip ^ at
        ref[: plan.gene_rows, :] = dot(
            rows_ref[aligned(owner, plan.gene_rows), :], weight, 1, weight_dim
        ).astype(BF)
        ref[plan.gene_rows :, :] = pre_ref[aligned(owner, plan.pre_block), :].astype(BF)


def project_kernel(plan, me_ref, *refs):
    chips, groups = plan.chips, plan.groups
    pieces, parts, refs = refs[:chips], refs[chips : chips + groups], refs[chips + groups :]
    bias_ref, query_ref, pair_ref, pre_ref, low_ref, weight_ref = refs
    collect(plan, me_ref[1], pieces, low_ref, pre_ref)
    collect_weight(plan, me_ref[0], parts, weight_ref)
    query_ref[...] = jnp.zeros_like(query_ref)
    pair_ref[...] = jnp.zeros_like(pair_ref)
    for rows in plan.halves(plan.rows):
        narrow = (dot(low_ref[rows, :], weight_ref[...]) + bias_ref[...]).astype(BF)
        for head in range(plan.window):
            for block, (ref, to) in enumerate(((query_ref, 0), (pair_ref, 0), (pair_ref, HALF))):
                to += head * LANES
                begin = block * plan.wide + head * HEAD_DIM
                ref[rows, to : to + HEAD_DIM] = narrow[:, begin : begin + HEAD_DIM]


def order_pairs(plan, core, mine_ref, other_ref, keys_ref, pre_ref):
    for chip in range(plan.chips):
        for ref, place in ((mine_ref, 2 * chip + core), (other_ref, 2 * chip + 1 - core)):
            genes = slice(chip * plan.gene_rows, (chip + 1) * plan.gene_rows)
            keys_ref[aligned(place, plan.gene_rows), :] = ref[genes, :]
            prefix = slice(
                plan.genes + chip * plan.pre_block, plan.genes + (chip + 1) * plan.pre_block
            )
            pre_ref[aligned(place, plan.pre_block), :] = ref[prefix, :].astype(F32)
    keys_ref[2 * plan.genes :, :] = pre_ref[...].astype(BF)


def attend_kernel(plan, me_ref, *refs):
    query_ref, mine_ref, other_ref, out_weight_ref, padded_ref, lse_ref = refs[:6]
    blocks = refs[6 : 6 + plan.chips]
    key_pre_ref, out_pre_ref, keys_ref, turned_ref, score_ref = refs[6 + plan.chips :]
    core = me_ref[2]
    order_pairs(plan, core, mine_ref, other_ref, keys_ref, key_pre_ref)
    for head in range(plan.window):
        at = slice(LANES * head, LANES * (head + 1))
        turned_ref[...] = keys_ref[:, at].astype(F32).T.astype(BF)
        for first, count, key_parts in query_chunks(plan):
            query = query_ref[first : first + count, at]
            top = None
            for start, size, diagonal in key_parts:
                scores = dot(keys_ref[start : start + size, at], query, 1, 1)
                scores = masked(plan, scores, start, diagonal, core)
                score_ref[start : start + size, :count] = scores
                high = jnp.max(scores, axis=0, keepdims=True)
                top = high if top is None else jnp.maximum(top, high)
            top = top * SCALE2
            total, mixed = 0.0, 0.0
            for start, size, _ in key_parts:
                weights = jnp.exp2(score_ref[start : start + size, :count] * SCALE2 - top)
                total = total + jnp.sum(weights, axis=0, keepdims=True)
                mixed = mixed + dot(turned_ref[:, start : start + size], weights.astype(BF))
            padded_ref[first : first + count, at] = (mixed * (1.0 / total)).T.astype(BF)
            lse_ref[head, :, first : first + count] = top + jnp.log2(total)
    give_blocks(plan, me_ref[1], blocks, padded_ref, out_weight_ref[...], 0, out_pre_ref)


def attend_back_kernel(plan, me_ref, *refs):
    pieces, refs = refs[: plan.chips], refs[plan.chips :]
    out_weight_ref, query_ref, own_pair_ref, other_pair_ref, lse_ref = refs[:5]
    query_grad_ref, mine_ref, other_ref, out_bias_ref = refs[5:9]
    pre_ref, key_pre_ref, low_ref, keys_ref, grad_ref, turned_ref, prob_ref, pgrad_ref, pair_ref = refs[9:]
    core = me_ref[2]
    collect(plan, me_ref[1], pieces, low_ref, pre_ref)
    order_pairs(plan, core, own_pair_ref, other_pair_ref, keys_ref, key_pre_ref)
    out_bias_ref[...] = jnp.sum(low_ref[...].astype(F32), axis=0, keepdims=True)
    for rows in plan.halves(plan.rows):
        grad_ref[rows, :] = dot(low_ref[rows, :], out_weight_ref[...], 1, 1).astype(BF)
    lane = lax.broadcasted_iota(jnp.int32, (1, LANES), 1)
    pair_scale = jnp.where(lane < HALF, SCALE, 1.0)
    for head in range(plan.window):
        at = slice(LANES * head, LANES * (head + 1))
        turned_ref[...] = keys_ref[:, at].astype(F32).T.astype(BF)
        pair_ref[...] = jnp.zeros_like(pair_ref)
        for first, count, key_parts in query_chunks(plan):
            query = query_ref[first : first + count, at]
            grad = grad_ref[first : first + count, at]
            both = jnp.concatenate([grad, query], 0)
            lse = lse_ref[head, :, first : first + count]
            delta = 0.0
            for start, size, diagonal in key_parts:
                pair = keys_ref[start : start + size, at]
                scores = masked(plan, dot(pair, query, 1, 1), start, diagonal, core)
                probs = jnp.exp2(scores * SCALE2 - lse)
                prob_grad = dot(pair, grad, 1, 1)
                delta = delta + jnp.sum(probs * prob_grad, axis=0, keepdims=True)
                prob_ref[start : start + size, :count] = probs
                pgrad_ref[start : start + size, :count] = prob_grad
            query_grad = 0.0
            for start, size, _ in key_parts:
                probs = prob_ref[start : start + size, :count]
                score_grad = (probs * (pgrad_ref[start : start + size, :count] - delta)).astype(BF)
                pair_ref[start : start + size, :] += dot(
                    jnp.concatenate([probs.astype(BF), score_grad], 1), both
                )
                query_grad = query_grad + dot(turned_ref[:, start : start + size], score_grad)
            query_grad_ref[first : first + count, at] = (query_grad.T * SCALE).astype(BF)
        for chip in range(plan.chips):
            for ref, place in ((mine_ref, 2 * chip + core), (other_ref, 2 * chip + 1 - core)):
                genes = slice(chip * plan.gene_rows, (chip + 1) * plan.gene_rows)
                ref[genes, at] = (pair_ref[aligned(place, plan.gene_rows), :] * pair_scale).astype(ref.dtype)
                prefix = slice(
                    plan.genes + chip * plan.pre_block, plan.genes + (chip + 1) * plan.pre_block
                )
                place = pl.ds(
                    pl.multiple_of(2 * plan.genes + place * plan.pre_block, plan.pre_block), plan.pre_block
                )
                ref[prefix, at] = (pair_ref[place, :] * pair_scale).astype(ref.dtype)


def project_back_kernel(plan, me_ref, *refs):
    groups = plan.groups
    query_grad_ref, mine_ref, other_ref = refs[:3]
    parts, refs = refs[3 : 3 + groups], refs[3 + groups :]
    choices, refs = ([], refs) if plan.whole else (refs[:2], refs[2:])
    qkv_grad_ref, bias_ref = refs[:2]
    blocks, (pre_ref, own_ref, weight_ref) = refs[2 : 2 + plan.chips], refs[2 + plan.chips :]
    collect_own(plan, me_ref[0], parts, choices[1:], own_ref, weight_ref)
    for rows in plan.halves(plan.rows):
        pairs = (mine_ref[rows, :] + other_ref[rows, :].astype(F32)).astype(BF)
        if not plan.whole:
            select_ref = choices[0]
            qkv_grad_ref[rows, :] = (
                dot(query_grad_ref[rows, :], select_ref[: plan.lanes, :])
                + dot(pairs, select_ref[plan.lanes :, :])
            ).astype(BF)
            continue
        queries = query_grad_ref[rows, :]
        for head in range(plan.window):
            for block, (value, at) in enumerate(((queries, 0), (pairs, 0), (pairs, HALF))):
                at += head * LANES
                to = block * plan.wide + head * HEAD_DIM
                qkv_grad_ref[rows, to : to + HEAD_DIM] = value[:, at : at + HEAD_DIM]
    bias_ref[...] = jnp.sum(qkv_grad_ref[...].astype(F32), axis=0, keepdims=True)
    give_blocks(plan, me_ref[1], blocks, qkv_grad_ref, own_ref[...], 1, pre_ref)


ROOT = math.sqrt(2.0 / math.pi)
CUBE = 0.044715


def stack_pieces(plan, pieces, low_ref):
    size = plan.step_rows
    for at, ref in enumerate(pieces):
        low_ref[at * size : at * size + plan.own_rows, :] = ref[...]
        if plan.own_rows < size:
            low_ref[at * size + plan.own_rows : (at + 1) * size, :] = jnp.zeros(
                (size - plan.own_rows, low_ref.shape[1]), BF
            )


def collect_down(plan, core, mine_ref, other_ref, down_ref):
    if plan.hidden % 16 == 0:
        down_ref[aligned(core, plan.hidden), :] = mine_ref[...]
        down_ref[aligned(1 - core, plan.hidden), :] = other_ref[...]
        return
    mine, other = mine_ref[...].astype(F32), other_ref[...].astype(F32)
    halves = [jnp.where(core == 0, mine, other), jnp.where(core == 0, other, mine)]
    down_ref[...] = jnp.concatenate(halves, 0).astype(BF)


def lift_kernel(plan, me_ref, *refs):
    chips, groups = plan.chips, plan.groups
    pieces, parts, refs = refs[:chips], refs[chips : chips + groups], refs[chips + groups :]
    bias_ref, mine_ref, other_ref = refs[:3]
    blocks, (low_ref, up_ref, down_ref) = refs[3 : 3 + chips], refs[3 + chips :]
    collect_weight(plan, me_ref[0], parts, up_ref)
    stack_pieces(plan, pieces, low_ref)
    collect_down(plan, me_ref[2], mine_ref, other_ref, down_ref)
    size = plan.step_rows
    for first in range(0, plan.all_rows, 2 * size):
        rows = slice(first, first + 2 * size)
        pre = dot(low_ref[rows, :], up_ref[...]) + bias_ref[...]
        active = (0.5 * pre * (1.0 + jnp.tanh(ROOT * (pre + CUBE * pre * pre * pre)))).astype(BF)
        lifted = dot(active, down_ref[...])
        for at in range(2):
            blocks[first // size + at][...] = lifted[at * size : at * size + plan.own_rows].astype(BF)


def lift_back_kernel(plan, me_ref, *refs):
    chips, groups = plan.chips, plan.groups
    pieces, grads, refs = refs[:chips], refs[chips : 2 * chips], refs[2 * chips :]
    parts, refs = refs[:groups], refs[groups:]
    bias_ref, mine_ref, other_ref, active_ref, pre_grad_ref, down_bias_ref, up_bias_ref = refs[:7]
    blocks, (low_ref, grad_ref, up_ref, down_ref) = refs[7 : 7 + chips], refs[7 + chips :]
    collect_weight(plan, me_ref[0], parts, up_ref)
    stack_pieces(plan, pieces, low_ref)
    stack_pieces(plan, grads, grad_ref)
    collect_down(plan, me_ref[2], mine_ref, other_ref, down_ref)
    size = plan.step_rows
    down_bias_ref[...] = jnp.sum(grad_ref[...].astype(F32), axis=0, keepdims=True)
    up_bias = 0.0
    for first in range(0, plan.all_rows, 2 * size):
        rows = slice(first, first + 2 * size)
        pre = dot(low_ref[rows, :], up_ref[...]) + bias_ref[...]
        act_grad = dot(grad_ref[rows, :], down_ref[...], 1, 1)
        square = pre * pre
        turn = jnp.tanh(ROOT * pre * (1.0 + CUBE * square))
        active_ref[rows, :] = (0.5 * pre * (1.0 + turn)).astype(BF)
        slope = 0.5 * (1.0 + turn) + (0.5 * ROOT) * pre * (1.0 - turn * turn) * (1.0 + 3.0 * CUBE * square)
        pre_grad = (act_grad * slope).astype(BF)
        pre_grad_ref[rows, :] = pre_grad
        up_bias = up_bias + jnp.sum(pre_grad.astype(F32), axis=0, keepdims=True)
        norm_grad = dot(pre_grad, up_ref[...], 1, 1)
        for at in range(2):
            blocks[first // size + at][...] = norm_grad[at * size : at * size + plan.own_rows].astype(BF)
    up_bias_ref[...] = up_bias


def send_kernel(plan, level, starts, width, me_ref, weight_ref, *refs):
    outs, (stack_ref,) = refs[: plan.chips], refs[plan.chips :]
    for to, begins in enumerate(starts):
        for at, begin in enumerate(begins):
            stack_ref[to, : plan.cols, at * width : (at + 1) * width] = weight_ref[
                level, :, begin : begin + width
            ]
        if plan.cols < plan.part:
            stack_ref[to, plan.cols :, :] = jnp.zeros(
                (plan.part - plan.cols, stack_ref.shape[2]), BF
            )
    for at, ref in enumerate(outs):
        ref[...] = stack_ref[me_ref[1] ^ at]


def norm_weight_grad(plan, left_ref, right_ref, weight_ref, sums_ref, vector_ref, whole_ref):
    width = right_ref.shape[1]
    step = 2 * plan.part
    for first in range(0, plan.features, step):
        rows = slice(first, first + step)
        product = dot(left_ref[:, rows], right_ref[...], 0, 0)
        weight = weight_ref[rows, :].astype(F32)
        shift_grad = jnp.sum(weight * sums_ref[...], axis=1, keepdims=True)
        both = jnp.sum(weight * product, axis=1, keepdims=True)
        turned = vector_ref[:, rows].T
        gain_grad = (both - turned[:, 0:1] * shift_grad) / turned[:, 1:2]
        whole_ref[rows, :width] = product
        whole_ref[rows, width : width + 2] = jnp.concatenate([shift_grad, gain_grad], 1)


def give_parts(plan, me, whole_ref, mine_ref, other_ref):
    width = whole_ref.shape[1]
    for at in range(plan.chips):
        owner = me ^ (2 * at)
        mine_ref[at, :, :width] = whole_ref[aligned(owner, plan.part), :].astype(BF)
        other_ref[at, :, :width] = whole_ref[aligned(owner ^ 1, plan.part), :].astype(BF)


def lift_grad_kernel(plan, me_ref, *refs):
    chips, groups = plan.chips, plan.groups
    pieces, grads, refs = refs[:chips], refs[chips : 2 * chips], refs[2 * chips :]
    parts, refs = refs[:groups], refs[groups:]
    active_ref, pre_grad_ref, sums_ref, vector_ref, up_mine, up_other, down_mine, down_other = refs[:8]
    low_ref, grad_ref, up_ref, whole_ref, down_ref = refs[8:]
    core = me_ref[2]
    stack_pieces(plan, pieces, low_ref)
    collect_weight(plan, me_ref[0], parts, up_ref)
    norm_weight_grad(plan, low_ref, pre_grad_ref, up_ref, sums_ref, vector_ref, whole_ref)
    give_parts(plan, me_ref[0], whole_ref, up_mine, up_other)
    stack_pieces(plan, grads, grad_ref)
    for rows in plan.halves(plan.chip_hidden):
        down_ref[rows, :] = dot(active_ref[:, rows], grad_ref[...], 0, 0)
    size = plan.hidden // 4
    filler = jnp.zeros((down_mine.shape[1] - size, D), F32)
    for at in range(4):
        first = down_ref[at * size : (at + 1) * size, :]
        second = down_ref[plan.hidden + at * size : plan.hidden + (at + 1) * size, :]
        for ref, rows in (
            (down_mine, jnp.where(core == 0, first, second)),
            (down_other, jnp.where(core == 0, second, first)),
        ):
            ref[at] = jnp.concatenate([rows, filler], 0).astype(BF)


def attend_grad_kernel(plan, riding, me_ref, *refs):
    chips, groups = plan.chips, plan.groups
    pieces, grads, refs = refs[:chips], refs[chips : 2 * chips], refs[2 * chips :]
    parts, refs = refs[:groups], refs[groups:]
    choices, refs = ([], refs) if plan.whole else (refs[:2], refs[2:])
    mixed_ref, qkv_grad_ref, sums_ref, vector_ref, small_ref, mine_ref, other_ref = refs[:7]
    low_ref, grad_ref, pre_ref, grad_pre_ref, own_ref, weight_ref, whole_ref, out_ref = refs[-8:]
    core = me_ref[2]
    collect(plan, me_ref[1], pieces, low_ref, pre_ref)
    collect_own(plan, me_ref[0], parts, choices[1:], own_ref, weight_ref)
    norm_weight_grad(plan, low_ref, qkv_grad_ref, own_ref, sums_ref, vector_ref, whole_ref)
    give_parts(plan, me_ref[0], whole_ref, mine_ref, other_ref)
    collect(plan, me_ref[1], grads, grad_ref, grad_pre_ref)
    if plan.whole:
        for head in range(plan.window):
            product = dot(mixed_ref[:, head * LANES : (head + 1) * LANES], grad_ref[...], 0, 0)
            out_ref[head * HEAD_DIM : (head + 1) * HEAD_DIM, :] = product[HALF : HALF + HEAD_DIM]
    else:
        own = dot(mixed_ref[...], choices[0][...]).astype(BF)
        out_ref[...] = dot(own, grad_ref[...], 0, 0)
    halves = out_ref[: plan.cols, :], out_ref[plan.cols :, :]
    extra = small_ref.shape[1]
    filler = jnp.zeros((plan.part - plan.cols - extra, D), F32)
    first = whole_ref.shape[1]
    for at, (ref, one, two) in enumerate(((mine_ref, 0, 1), (other_ref, 1, 0))):
        rows = jnp.where(core == 0, halves[one], halves[two])
        rows = jnp.concatenate([rows, small_ref[at], filler], 0).astype(BF)
        if not riding:
            refs[7 + at][...] = rows
            continue
        for chip in range(chips):
            ref[chip, :, first:] = rows[:, chip * plan.chip_cols : (chip + 1) * plan.chip_cols]


def join_down_kernel(plan, *refs):
    parts, out_ref = refs[:LAYERS], refs[LAYERS]
    size = plan.hidden // 4
    for level, ref in enumerate(parts):
        for at in range(4):
            out_ref[level, at * size : (at + 1) * size, :] = ref[at, :size, :].astype(F32)


def join_kernel(plan, blocks, width, me_ref, *refs):
    count = LAYERS * plan.chips
    parts, (out_ref, vector_ref, stack_ref) = refs[:count], refs[count:]
    each = width // blocks
    for level in range(LAYERS):
        for at in range(plan.chips):
            stack_ref[at] = parts[level * plan.chips + at][...]
        vectors = 0.0
        for source in range(plan.chips):
            value = stack_ref[me_ref[1] ^ source].astype(F32)
            for block in range(blocks):
                begin = (block * plan.chips + source) * each
                out_ref[:, level, begin : begin + each] = value[
                    : plan.cols, block * each : (block + 1) * each
                ]
            vectors = vectors + value[:, width : width + 2]
        padded = jnp.concatenate([vectors, jnp.zeros((plan.part, LANES - 2), F32)], 1)
        vector_ref[level] = padded.T[:8]


def body(
    genes,
    prefix,
    cot_genes,
    cot_prefix,
    w_qkv,
    w_out,
    w_up,
    w_down,
    norm1_gain,
    norm1_bias,
    norm2_gain,
    norm2_bias,
    bias_q,
    bias_v,
    bias_out,
    bias_up,
    bias_down,
):
    groups = lax.axis_size("gene")
    cells = lax.axis_size("cell")
    me = lax.axis_index("gene")
    cell = lax.axis_index("cell")
    chip, core = me // 2, me % 2
    plan = Plan(groups, genes.shape[1])
    chips, cols, chip_cols, wide = plan.chips, plan.cols, plan.chip_cols, plan.wide
    hidden, chip_hidden = plan.hidden, plan.chip_hidden
    first_head = jnp.asarray(plan.first_heads, jnp.int32)[chip]
    offset = chip * chip_cols - first_head * HEAD_DIM
    turn = chip if plan.by_links else jnp.zeros_like(chip)
    where = jnp.stack([2 * turn + core, turn, core]).astype(jnp.int32)
    same_core = [[2 * at + one for at in range(chips)] for one in range(2)]
    here = functools.partial

    def after(value, *others):
        return lax.optimization_barrier((value,) + others)[0]

    def after_all(values, *others):
        return list(lax.optimization_barrier((tuple(values), others))[0])

    def together(*lists):
        return [list(got) for got in lax.optimization_barrier(tuple(tuple(x) for x in lists))]

    def swap(value, bits):
        return lax.ppermute(value, "gene", [(at, at ^ bits) for at in range(groups)])

    def to_chips(parts):
        if not plan.by_links:
            got = lax.all_to_all(jnp.stack(parts), "gene", 0, 0, axis_index_groups=same_core)
            return [got[at] for at in range(chips)]
        return [parts[0]] + [swap(parts[at], 2 * at) for at in range(1, chips)]

    def gather(piece):
        if not plan.by_links:
            got = lax.all_gather(piece, "gene", axis=0, axis_index_groups=same_core)
            return [got[at] for at in range(chips)]
        return to_chips([piece] * chips)

    def scatter(blocks):
        if not plan.by_links:
            return [
                lax.psum_scatter(
                    jnp.stack(blocks), "gene", scatter_dimension=0, axis_index_groups=same_core
                )
            ]
        return to_chips(blocks)

    def across(near):
        far = [swap(value, 1) for value in near]
        return [value for pair in zip(near, far) for value in pair]

    class CellSum:
        def __init__(self, mine, other, *steps):
            self.value = (mine.astype(F32) + other.astype(F32)).astype(BF)
            self.steps = list(steps) if cells == 4 else [steps[-1]]
            self.moves = len(steps)
            waiting.append(self)

        def half(self, bit):
            halves = self.value.reshape((2, self.value.shape[0] // 2) + self.value.shape[1:])
            return lax.dynamic_index_in_dim(halves, bit, 0, keepdims=False)

        def move(self):
            if cells != 4:
                return lax.psum(self.value, "cell")
            left = len(self.steps)
            if self.moves == 3:
                inwards, between, outwards = [(0, 1), (3, 2)], [(1, 2), (2, 1)], [(1, 0), (2, 3)]
                return lax.ppermute(self.value, "cell", {3: inwards, 2: between, 1: outwards}[left])
            self.away = 1 if left in (1, 4) else 2
            self.bit = cell // self.away % 2
            value = self.half(1 - self.bit) if left > 2 else self.value
            return lax.ppermute(value, "cell", [(at, at ^ self.away) for at in range(4)])

        def land(self, got):
            left = len(self.steps)
            if cells != 4:
                self.value = got
            elif self.moves == 3 and left == 1:
                self.value = jnp.where((cell == 1) | (cell == 2), self.value, got)
            elif left > 2 or self.moves == 3:
                value = self.value if self.moves == 3 else self.half(self.bit)
                self.value = (value.astype(F32) + got.astype(F32)).astype(BF)
            else:
                first, second = (
                    jnp.where(self.bit == at, self.value, got) for at in range(2)
                )
                self.value = jnp.concatenate([first, second], 0)
            self.steps.pop(0)

    waiting = []

    def beside(step, *lists):
        moving = [item for item in waiting if item.steps and item.steps[0] == step]
        *lists, landed = together(*lists, [item.move() for item in moving])
        for item, got in zip(moving, landed):
            item.land(got)
        return lists

    def send(weight, level, starts, width, *others):
        total = len(starts[0]) * width
        return call(
            here(send_kernel, plan, level, starts, width),
            "send",
            [after(where, *others), weight],
            [shape_of(plan.part, total)] * chips,
            [pltpu.VMEM((chips, plan.part, total), BF)],
            True,
        )

    qkv_starts = [
        [block * D + head * HEAD_DIM for block in range(3)] for head in plan.first_heads
    ]
    up_starts = [[to * chip_hidden] for to in range(chips)]

    def chooser(wanted, there):
        return (wanted[:, None] == there[None, :]).astype(BF)

    def own_of(block, column, real):
        ok = real & (column >= offset) & (column < offset + chip_cols)
        return jnp.where(ok, block * chip_cols + column - offset, -1)

    window_at = jnp.arange(3 * wide)
    own_columns = jnp.arange(3 * chip_cols)
    cut = chooser(own_of(window_at // wide, window_at % wide, True), own_columns)
    lanes = jnp.arange(2 * plan.lanes)
    inner = lanes % LANES
    is_pair = lanes >= plan.lanes
    block = jnp.where(is_pair, 1 + inner // HALF, 0)
    inner = jnp.where(is_pair, inner % HALF, inner)
    column = (lanes % plan.lanes) // LANES * HEAD_DIM + inner
    select = chooser(own_of(block, column, inner < HEAD_DIM), own_columns)
    at_out = jnp.arange(plan.lanes)
    inner = at_out % LANES - HALF
    out_col = (at_out // LANES) * HEAD_DIM + inner
    out_ok = (inner >= 0) & (inner < HEAD_DIM)
    out_select = chooser(own_of(0, out_col, out_ok), jnp.arange(chip_cols))

    def out_windows():
        if plan.by_links:
            rows = jnp.concatenate([w_out, swap(w_out, 1)], 1)
            own = jnp.arange(cols)
            owner = jnp.concatenate([me * cols + own, (me ^ 1) * cols + own])
        else:
            rows = lax.all_gather(w_out, "gene", axis=1, tiled=True)
            owner = jnp.arange(D)
        wanted = jnp.where(out_ok, first_head * HEAD_DIM + out_col, -1)
        is_own = (out_col >= offset) & (out_col < offset + chip_cols)
        picks = [chooser(wanted, owner)]
        if not plan.whole:
            picks.append(chooser(jnp.where(is_own, wanted, -1), owner))
        got = [[dot(pick, rows[level]).astype(BF) for level in range(LAYERS)] for pick in picks]
        return got[0], got[-1]

    def window_of(vec):
        return lax.dynamic_slice_in_dim(vec, first_head * HEAD_DIM, wide, 1)

    def norm_vectors(token):
        every = jnp.stack([norm1_bias, norm1_gain, norm2_bias, norm2_gain])
        every = after(every, token).reshape(2, 2, LAYERS, groups, cols)
        every = jnp.pad(every, ((0, 0),) * 4 + ((0, plan.part - cols),), constant_values=1.0)
        every = every.transpose(0, 2, 1, 3, 4).reshape(2 * LAYERS, 2, plan.features)
        every = jnp.pad(every, ((0, 0), (0, 6), (0, 0)))
        return [every[at] for at in range(2 * LAYERS)]

    rows_f32 = shape_of(plan.own_rows, D, dtype=F32)
    normed_like = shape_of(plan.own_rows, plan.features)
    grad_like = shape_of(plan.own_rows, D)
    row_blocks = [grad_like] * chips
    feature_blocks = [normed_like] * chips
    vector = shape_of(1, D, dtype=F32)
    ends_like = [
        shape_of(D, plan.gene_rows, dtype=F32),
        shape_of(plan.pre_block, D, dtype=F32),
    ]

    own_prefix = lax.dynamic_slice_in_dim(prefix[0], me * plan.pre_rows, plan.pre_rows, 0)
    filler = ((0, plan.pre_block - plan.pre_rows), (0, 0))
    rows, piece = call(
        here(begin_kernel, plan),
        "begin",
        [genes[0].T, jnp.pad(own_prefix, filler), norm1_gain, norm1_bias],
        [rows_f32, normed_like],
    )
    qkv_parts, up_parts = [None] * LAYERS, [None] * LAYERS
    qkv_sent = send(w_qkv, 0, qkv_starts, wide, piece)
    pieces, near = gather(piece), to_chips(qkv_sent)
    token = qkv_sent[-1]
    up_sent = send(w_up, 0, up_starts, chip_hidden, token)
    qkv_biases = jnp.concatenate(
        [window_of(bias_q), jnp.zeros((LAYERS, wide), F32), window_of(bias_v)], 1
    )
    windows, out_weights = out_windows()
    pieces, near, up_sent, _ = together(
        pieces, near, up_sent, [qkv_biases] + windows + out_weights
    )
    up_biases = lax.dynamic_slice_in_dim(bias_up, chip * chip_hidden, chip_hidden, 1)
    (qkv_parts[0],) = together(across(near))

    saved, downs = [], []
    for level in range(LAYERS):
        last = level + 1 == LAYERS
        if level:
            (pieces, far) = together(gather(piece), across(near[chips // 2 :]))
            qkv_parts[level] = qkv_far + far
        up_near = to_chips(after_all(up_sent, *pieces, *qkv_parts[level]))
        low_one = pieces
        query, pair = call(
            here(project_kernel, plan),
            "project",
            [where] + pieces + qkv_parts[level] + [qkv_biases[level : level + 1]],
            [shape_of(plan.rows, plan.lanes), shape_of(plan.rows, plan.lanes)],
            [
                pltpu.VMEM((plan.prefix, plan.features), F32),
                pltpu.VMEM((plan.rows, plan.features), BF),
                pltpu.VMEM((plan.features, 3 * wide), BF),
            ],
            True,
        )
        other_pair = swap(pair, 1)
        own_down = after(w_down, pair)[level]
        other_down = swap(own_down, 1)
        if not last:
            qkv_sent = send(w_qkv, level + 1, qkv_starts, wide, pair)
            up_sent = send(w_up, level + 1, up_starts, chip_hidden, pair)
            other_pair = after(other_pair, qkv_sent[-1], up_sent[-1])
        outs = call(
            here(attend_kernel, plan),
            "attend",
            [where, query, pair, other_pair, out_weights[level]],
            [
                shape_of(plan.rows, plan.lanes),
                shape_of(plan.window, 1, plan.rows, dtype=F32),
            ]
            + row_blocks,
            [
                pltpu.VMEM((2 * plan.prefix, plan.lanes), F32),
                pltpu.VMEM((plan.prefix, D), F32),
                pltpu.VMEM((2 * plan.rows, plan.lanes), BF),
                pltpu.VMEM((LANES, 2 * plan.rows), BF),
                pltpu.VMEM((2 * plan.rows, 2 * plan.gene_rows), F32),
            ],
            True,
        )
        outs, up_near, (own_down, other_down) = together(outs, up_near, [own_down, other_down])
        downs.append([own_down, other_down])
        mixed, lse = outs[:2]
        parts, up_far = together(scatter(outs[2:]), across(up_near[: chips // 2]))
        middle, piece = call(
            here(middle_kernel, plan, len(parts), level, level),
            "middle",
            parts + [rows, bias_out, norm2_gain, norm2_bias],
            [rows_f32, normed_like],
        )
        if last:
            cot_grad, cot_piece = call(
                here(cot_kernel, plan),
                "cotangent",
                [after(cot_genes[0].T, piece), jnp.pad(cot_prefix[0], filler)],
                [rows_f32, grad_like],
            )
            spare = [cot_grad, cot_piece]
        else:
            spare = []
        pieces, far, spare = together(gather(piece), across(up_near[chips // 2 :]), spare)
        up_parts[level] = up_far + far
        if last:
            cot_grad, cot_piece = spare
            near = gather(after(cot_piece, *pieces))
        else:
            near = to_chips(after_all(qkv_sent, *pieces))
        low_two = pieces
        blocks = call(
            here(lift_kernel, plan),
            "lift",
            [where]
            + pieces
            + up_parts[level]
            + [up_biases[level : level + 1]] + downs[level],
            row_blocks,
            [
                pltpu.VMEM((plan.all_rows, plan.features), BF),
                pltpu.VMEM((plan.features, chip_hidden), BF),
                pltpu.VMEM((chip_hidden, D), BF),
            ],
            True,
        )
        blocks, near = together(blocks, near)
        saved.append((rows, low_one, query, pair, other_pair, mixed, lse, middle, low_two))
        if last:
            cot_pieces = near
            last_blocks, last_middle = blocks, middle
        else:
            spare = []
            if level == 0:
                spare = norm_vectors(low_two[0])
            parts, qkv_far, spare = together(scatter(blocks), across(near[: chips // 2]), spare)
            if level == 0:
                vectors = spare
            rows, piece = call(
                here(middle_kernel, plan, len(parts), level, level + 1),
                "next_rows",
                parts + [middle, bias_down, norm1_gain, norm1_bias],
                [rows_f32, normed_like],
            )

    def of_cores(value, size, dim):
        return [
            lax.dynamic_slice_in_dim(value, at * size, size, dim) for at in (core, 1 - core)
        ]

    def messages_of(item, width):
        return [item.value[at, :, :width] for at in range(chips)]

    grad, pieces = cot_grad, cot_pieces
    down_sums, up_sums, qkv_sums = ([None] * LAYERS for _ in range(3))
    long_rows, short_rows, up_rows = [None] * (2 * LAYERS), [None] * (2 * LAYERS), [None] * LAYERS
    extra = -(-LAYERS * (4 * cols + hidden) // D)
    choices = [] if plan.whole else [select, cut]
    out_choices = [] if plan.whole else [out_select, cut]
    stacked = pltpu.VMEM((plan.all_rows, plan.features), BF)
    stacked_grad = pltpu.VMEM((plan.all_rows, D), BF)
    up_room = pltpu.VMEM((plan.features, chip_hidden), BF)
    own_room = pltpu.VMEM((plan.features, 3 * chip_cols), BF)
    window_room = pltpu.VMEM((8, LANES) if plan.whole else (plan.features, 3 * wide), BF)
    for level in reversed(range(LAYERS)):
        rows, low_one, query, pair, other_pair, mixed, lse, middle, low_two = saved[level]
        if level + 1 < LAYERS:
            (pieces,) = beside(f"rows {level}", gather(piece))
        down_grad = pieces
        outs = call(
            here(lift_back_kernel, plan),
            "lift_back",
            [where]
            + low_two
            + pieces
            + up_parts[level]
            + [up_biases[level : level + 1]] + downs[level],
            [
                shape_of(plan.all_rows, chip_hidden),
                shape_of(plan.all_rows, chip_hidden),
                vector,
                shape_of(1, chip_hidden, dtype=F32),
            ]
            + feature_blocks,
            [stacked, stacked_grad, up_room, pltpu.VMEM((chip_hidden, D), BF)],
            True,
        )
        (outs,) = beside(f"lifted {level}", outs)
        if not level:
            outs = after_all(outs, up_sums[1].value)
        active, pre_grad, long_rows[level], up_rows[level] = outs[:4]
        up_mine, up_other, down_mine, down_other = call(
            here(lift_grad_kernel, plan),
            "lift_grad",
            [where]
            + low_two
            + down_grad
            + up_parts[level]
            + [active, pre_grad, up_rows[level], vectors[LAYERS + level]],
            [shape_of(chips, plan.part, chip_hidden + 2)] * 2
            + [shape_of(4, -(-hidden // 64) * 16, D)] * 2,
            [
                stacked,
                stacked_grad,
                up_room,
                pltpu.VMEM((plan.features, chip_hidden + 2), F32),
                pltpu.VMEM((chip_hidden, D), F32),
            ],
            True,
        )
        parts, (up_mine, up_other, down_mine, down_other) = beside(
            f"lift {level}", scatter(outs[4:]), [up_mine, up_other, down_mine, down_other]
        )
        middle_grad, piece = call(
            here(back_kernel, plan, len(parts), level),
            "middle_back",
            parts + [middle, norm2_gain, grad],
            [rows_f32, grad_like],
        )
        (middle_grad, piece, up_got, down_got), = beside(
            f"turn {level}", [middle_grad, piece, swap(up_other, 1), swap(down_other, 1)]
        )
        if level:
            down_sums[level] = CellSum(down_mine, down_got, "attend 1", "project 1", "lifted 0")
            up_sums[level] = CellSum(up_mine, up_got, "project 1", "lifted 0", "turn 0")
        else:
            down_sums[level] = CellSum(down_mine, down_got, "attend 0", "end 1", "end 2")
            up_sums[level] = CellSum(up_mine, up_got, "end 1", "end 2", "end 3")
        (pieces,) = beside(f"middle {level}", gather(piece))
        branch_grad = pieces
        outs = call(
            here(attend_back_kernel, plan),
            "attend_back",
            [where] + pieces + [windows[level], query, pair, other_pair, lse],
            [
                shape_of(plan.rows, plan.lanes),
                shape_of(plan.rows, plan.lanes, dtype=F32),
                shape_of(plan.rows, plan.lanes),
                vector,
            ],
            [
                pltpu.VMEM((plan.prefix, D), F32),
                pltpu.VMEM((2 * plan.prefix, plan.lanes), F32),
                pltpu.VMEM((plan.rows, D), BF),
                pltpu.VMEM((2 * plan.rows, plan.lanes), BF),
                pltpu.VMEM((plan.rows, plan.lanes), BF),
                pltpu.VMEM((LANES, 2 * plan.rows), BF),
                pltpu.VMEM((2 * plan.rows, 2 * plan.gene_rows), F32),
                pltpu.VMEM((2 * plan.rows, 2 * plan.gene_rows), F32),
                pltpu.VMEM((2 * plan.rows, LANES), F32),
            ],
            True,
        )
        if level:
            (outs,) = beside("attend 1", outs)
        else:
            up_width, qkv_width = chip_hidden + 2, 3 * chip_cols + 2
            up_near = to_chips(after_all(messages_of(up_sums[1], up_width), *pieces))
            outs, up_near = beside("attend 0", outs, up_near)
        query_grad, pair_mine, pair_other, long_rows[LAYERS + level] = outs
        outs = call(
            here(project_back_kernel, plan),
            "project_back",
            [where, query_grad, pair_mine, swap(pair_other, 1)] + qkv_parts[level] + choices,
            [shape_of(plan.rows, 3 * chip_cols), shape_of(1, 3 * chip_cols, dtype=F32)]
            + feature_blocks,
            [pltpu.VMEM((plan.prefix, plan.features), F32), own_room, window_room],
            True,
        )
        qkv_grad, qkv_bias = outs[:2]
        short_rows[level] = qkv_bias[:, :chip_cols]
        short_rows[LAYERS + level] = qkv_bias[:, 2 * chip_cols :]
        small = jnp.zeros((2, extra, D), F32)
        if not level:
            long_own = lax.dynamic_slice_in_dim(
                jnp.concatenate(long_rows, 0), chip * chip_cols, chip_cols, 1
            )
            small = [
                jnp.concatenate([vec.reshape(-1) for vec in vecs])
                for vecs in zip(
                    of_cores(long_own, cols, 1),
                    of_cores(jnp.concatenate(short_rows, 0), cols, 1),
                    of_cores(jnp.concatenate(up_rows, 0), hidden, 1),
                )
            ]
            small = jnp.stack(
                [jnp.pad(vec, (0, extra * D - vec.size)).reshape(extra, D) for vec in small]
            )
        width = 3 * chip_cols + 2
        made = call(
            here(attend_grad_kernel, plan, bool(level)),
            "attend_grad",
            [where]
            + low_one
            + branch_grad
            + qkv_parts[level]
            + out_choices
            + [mixed, qkv_grad, qkv_bias, vectors[level], small],
            [shape_of(chips, plan.part, width + (chip_cols if level else 0))] * 2
            + [shape_of(plan.part, D)] * (0 if level else 2),
            [
                pltpu.VMEM((plan.rows, plan.features), BF),
                pltpu.VMEM((plan.rows, D), BF),
                pltpu.VMEM((plan.prefix, plan.features), F32),
                pltpu.VMEM((plan.prefix, D), F32),
                own_room,
                window_room,
                pltpu.VMEM((plan.features, 3 * chip_cols + 2), F32),
                pltpu.VMEM((chip_cols, D), F32),
            ],
            True,
        )
        blocks = outs[2:]
        if level:
            parts = scatter(blocks)
            parts, (qkv_mine, qkv_other) = beside("project 1", parts, made)
            grad, piece = call(
                here(back_kernel, plan, len(parts), level),
                "rows_back",
                parts + [rows, norm1_gain, middle_grad],
                [rows_f32, grad_like],
            )
            grad, piece, qkv_got = together([grad, piece, swap(qkv_other, 1)])[0]
            qkv_sums[level] = CellSum(qkv_mine, qkv_got, "lift 0", "attend 0", "end 1")

    (made,) = together(made)
    qkv_mine, qkv_other, out_mine, out_other = made
    qkv_got, out_got = together([swap(qkv_other, 1), swap(out_other, 1)])[0]
    qkv_sums[0] = CellSum(qkv_mine, qkv_got, "end 2", "end 3", "end 4")
    beside("end 1", [qkv_sums[0].value])
    parts, _ = beside("end 2", scatter(after_all(blocks, qkv_sums[0].value)), [up_sums[0].value])
    ends = call(
        here(back_end_kernel, plan, len(parts), 0),
        "rows_back_end",
        parts + [rows, norm1_gain, middle_grad],
        ends_like,
    )
    out_sum = (after(out_mine, parts[0]).astype(F32) + out_got.astype(F32)).astype(BF)
    parts, ends = beside("end 3", scatter(after_all(last_blocks, *parts)), ends)
    result = call(
        here(finish_kernel, plan, len(parts), LAYERS - 1),
        "finish",
        parts + [last_middle, bias_down],
        ends_like,
    )
    def sum_near(value, away):
        if cells != 4:
            return lax.psum(value, "cell") if away == 1 else value
        got = lax.ppermute(value, "cell", [(at, at ^ away) for at in range(cells)])
        return (value.astype(F32) + got.astype(F32)).astype(BF)

    near = to_chips(after_all(messages_of(qkv_sums[1], qkv_width), *parts))
    last_up = to_chips(after_all(messages_of(up_sums[0], up_width), *parts))
    (out_sum,) = after_all([out_sum], *parts)
    (g_down,) = call(
        here(join_down_kernel, plan),
        "join_down",
        after_all([item.value for item in down_sums], parts[0]),
        [shape_of(LAYERS, hidden, D, dtype=F32)],
    )
    near, last_up, result, (out_sum, g_down) = beside(
        "end 4", near, last_up, result, [sum_near(out_sum, 1), g_down]
    )
    last_near = to_chips(messages_of(qkv_sums[0], qkv_width))
    out_sum = sum_near(out_sum, 2)
    up_parts = [last_up, up_near]
    riders = [qkv_sums[1].value[at, : plan.cols, qkv_width:] for at in range(chips)]
    out_sums = [out_sum[:cols], after(jnp.concatenate(riders, 1), last_up[0])]
    small = out_sum[cols : cols + extra].reshape(-1).astype(F32)
    size = LAYERS * cols
    b_down, b_out, b_q, b_v = (small[at * size : (at + 1) * size].reshape(LAYERS, cols) for at in range(4))
    b_up = small[4 * size : 4 * size + LAYERS * hidden].reshape(LAYERS, hidden)

    def join(parts, blocks, width):
        whole, vectors = call(
            here(join_kernel, plan, blocks, width),
            "join",
            [where] + parts[0] + parts[1],
            [
                shape_of(cols, LAYERS, blocks * D if blocks > 1 else FF, dtype=F32),
                shape_of(LAYERS, 8, plan.part, dtype=F32),
            ],
            [pltpu.VMEM((chips, plan.part, width + 2), BF)],
            scalar=True,
        )
        return whole.transpose(1, 0, 2), vectors[:, 0, :cols], vectors[:, 1, :cols]

    ups = join(up_parts, 1, chip_hidden)
    last_near, (g_up, shift_two, gain_two) = together(last_near, ups)
    qkv_parts = [last_near, near]
    g_qkv, shift_one, gain_one = join(qkv_parts, 3, 3 * chip_cols)
    return (
        result[0].T[None],
        result[1][: plan.pre_rows][None],
        ends[0].T[None],
        ends[1][: plan.pre_rows][None],
        g_qkv,
        jnp.stack(out_sums).astype(F32),
        g_up,
        g_down,
        gain_one,
        shift_one,
        gain_two,
        shift_two,
        b_q,
        b_v,
        b_out,
        b_up,
        b_down,
    )


def solution(mesh):
    rows = P("cell", "gene", None)
    weight = P(None, "gene", None)
    vector = P(None, "gene")
    return jax.shard_map(
        body,
        mesh=mesh,
        in_specs=(rows, P("cell", None, None), rows, rows) + (weight,) * 4 + (P(),) * 9,
        out_specs=(rows,) * 4 + (weight,) * 4 + (vector,) * 9,
        check_vma=False,
    )
```

```python
import functools
import math

import jax
import jax.numpy as jnp
from jax import lax
from jax.experimental import pallas as pl
from jax.experimental.pallas import tpu as pltpu
from jax.sharding import PartitionSpec as P

D = 1120
HEADS = 20
HEAD_DIM = 56
FF = 4480
PREFIX = 64
LAYERS = 2
LANES = 128
HALF = 64
SCALE = HEAD_DIM ** (-0.5)
SCALE2 = SCALE * math.log2(math.e)
BF = jnp.bfloat16
F32 = jnp.float32
COST = 1000


def dot(left, right, left_dim=1, right_dim=0):
    return lax.dot_general(
        left, right, (((left_dim,), (right_dim,)), ((), ())), preferred_element_type=F32
    )


class Plan:
    def __init__(self, groups, gene_rows):
        self.groups = groups
        self.chips = groups // 2
        self.gene_rows = gene_rows
        self.pre_rows = PREFIX // groups
        self.pre_block = -(-self.pre_rows // 8) * 8
        self.own_rows = gene_rows + self.pre_block
        self.step_rows = -(-self.own_rows // 16) * 16
        self.genes = self.chips * gene_rows
        self.prefix = self.chips * self.pre_block
        self.rows = self.genes + self.prefix
        self.all_rows = self.chips * self.step_rows
        self.cols = D // groups
        self.chip_cols = D // self.chips
        self.hidden = FF // groups
        self.chip_hidden = FF // self.chips
        self.part = -(-self.cols // 16) * 16
        self.features = groups * self.part
        spans = [
            (self.chip_cols * at // HEAD_DIM, -(-self.chip_cols * (at + 1) // HEAD_DIM))
            for at in range(self.chips)
        ]
        self.window = max(last - first for first, last in spans)
        self.first_heads = [min(first, HEADS - self.window) for first, _ in spans]
        self.wide = self.window * HEAD_DIM
        self.lanes = self.window * LANES
        self.whole = self.wide == self.chip_cols
        self.by_links = groups == 8

    def halves(self, total):
        step = -(-total // 32) * 16
        return [slice(first, min(first + step, total)) for first in range(0, total, step)]


SCALAR = pl.BlockSpec(memory_space=pltpu.SMEM)
WHOLE = pl.BlockSpec(memory_space=pltpu.VMEM)


def call(kernel, name, args, outs, scratch=(), scalar=False):
    got = pl.pallas_call(
        kernel,
        in_specs=[SCALAR if scalar and at == 0 else WHOLE for at in range(len(args))],
        out_specs=[WHOLE] * len(outs),
        out_shape=outs,
        scratch_shapes=list(scratch),
        compiler_params=pltpu.CompilerParams(vmem_limit_bytes=58 << 20),
        cost_estimate=pl.CostEstimate(flops=COST, bytes_accessed=COST, transcendentals=0),
        name=name,
    )(*args)
    return list(got)


def shape_of(*dims, dtype=BF):
    return jax.ShapeDtypeStruct(dims, dtype)


def aligned(at, size):
    return pl.ds(pl.multiple_of(at * size, size), size)


def normed_of(values):
    centred = values - jnp.mean(values, axis=-1, keepdims=True)
    variance = jnp.mean(centred * centred, axis=-1, keepdims=True)
    inverse = lax.rsqrt(variance + 1e-05)
    return centred * inverse, inverse


def spread(plan, rows):
    filler = jnp.zeros((rows.shape[0], plan.part - plan.cols), rows.dtype)
    parts = []
    for at in range(plan.groups):
        parts += [rows[:, at * plan.cols : (at + 1) * plan.cols], filler]
    return jnp.concatenate(parts, 1)


def unspread(plan, rows):
    return jnp.concatenate(
        [rows[:, at * plan.part : at * plan.part + plan.cols] for at in range(plan.groups)], 1
    )


def real_rows(plan, rows):
    if plan.pre_rows == plan.pre_block:
        return rows
    at = lax.broadcasted_iota(jnp.int32, rows.shape, 0)
    return jnp.where(at < plan.gene_rows + plan.pre_rows, rows, 0.0)


def normed_piece(plan, rows, gain_ref, shift_ref, level):
    unit, _ = normed_of(rows)
    normed = unit * gain_ref[level : level + 1, :] + shift_ref[level : level + 1, :]
    return spread(plan, real_rows(plan, normed)).astype(BF)


def begin_kernel(plan, gene_ref, pre_ref, gain_ref, shift_ref, rows_ref, piece_ref):
    rows = jnp.concatenate([gene_ref[...].astype(F32).T, pre_ref[...].astype(F32)], 0)
    rows_ref[...] = rows
    piece_ref[...] = normed_piece(plan, rows, gain_ref, shift_ref, 0)


def add_parts(refs):
    total = refs[0][...].astype(F32)
    for ref in refs[1:]:
        total = total + ref[...].astype(F32)
    return total


def middle_kernel(plan, parts, level, gain_level, *refs):
    part_refs, (base_ref, bias_ref, gain_ref, shift_ref, rows_ref, piece_ref) = (
        refs[:parts],
        refs[parts:],
    )
    rows = base_ref[...] + add_parts(part_refs) + bias_ref[level : level + 1, :]
    rows_ref[...] = rows
    piece_ref[...] = normed_piece(plan, rows, gain_ref, shift_ref, gain_level)


def finish_kernel(plan, parts, level, *refs):
    part_refs, (base_ref, bias_ref, gene_ref, pre_ref) = refs[:parts], refs[parts:]
    rows = base_ref[...] + add_parts(part_refs) + bias_ref[level : level + 1, :]
    gene_ref[...] = rows[: plan.gene_rows].T
    pre_ref[...] = rows[plan.gene_rows :]


def norm_back(plan, parts, level, refs):
    part_refs, (x_ref, gain_ref, base_ref) = refs[:parts], refs[parts : parts + 3]
    grad_norm = unspread(plan, add_parts(part_refs))
    unit, inverse = normed_of(x_ref[...])
    scaled = grad_norm * gain_ref[level : level + 1, :]
    return base_ref[...] + inverse * (
        scaled
        - jnp.mean(scaled, axis=-1, keepdims=True)
        - unit * jnp.mean(scaled * unit, axis=-1, keepdims=True)
    )


def back_kernel(plan, parts, level, *refs):
    grad = norm_back(plan, parts, level, refs)
    grad_ref, piece_ref = refs[parts + 3 :]
    grad_ref[...] = grad
    piece_ref[...] = real_rows(plan, grad).astype(BF)


def back_end_kernel(plan, parts, level, *refs):
    grad = norm_back(plan, parts, level, refs)
    gene_ref, pre_ref = refs[parts + 3 :]
    gene_ref[...] = grad[: plan.gene_rows].T
    pre_ref[...] = grad[plan.gene_rows :]


def cot_kernel(plan, gene_ref, pre_ref, rows_ref, piece_ref):
    rows = jnp.concatenate([gene_ref[...].T, pre_ref[...]], 0)
    rows_ref[...] = rows
    piece_ref[...] = real_rows(plan, rows).astype(BF)


def query_chunks(plan):
    both, genes = 2 * plan.gene_rows, 2 * plan.genes
    chunks = []
    for chip in range(0, plan.chips, 2):
        blocks = [(genes, 2 * plan.prefix, False)]
        blocks += [
            (start, both, start >= chip * both) for start in range(0, (chip + 2) * both, both)
        ]
        chunks.append((chip * plan.gene_rows, both, blocks))
    chunks.append((plan.genes, plan.prefix, [(genes, 2 * plan.prefix, True)]))
    return chunks


def masked(plan, scores, start, diagonal, core):
    in_prefix = start == 2 * plan.genes
    holes = in_prefix and plan.pre_rows < plan.pre_block
    if not (diagonal or holes):
        return scores
    key_at = lax.broadcasted_iota(jnp.int32, scores.shape, 0)
    query_at = lax.broadcasted_iota(jnp.int32, scores.shape, 1)
    keep = None
    if diagonal:
        block = plan.pre_block if in_prefix else plan.gene_rows
        inner = lax.rem(query_at, block)
        before = 0 if in_prefix else start % (4 * block)
        keep = key_at <= 2 * query_at - inner + core * block - before
    if holes:
        real = lax.rem(key_at, plan.pre_block) < plan.pre_rows
        keep = real if keep is None else keep & real
    return jnp.where(keep, scores, -jnp.inf)


def collect(plan, chip, piece_refs, whole_ref, pre_ref):
    for at, ref in enumerate(piece_refs):
        owner = chip ^ at
        whole_ref[aligned(owner, plan.gene_rows), :] = ref[: plan.gene_rows, :]
        pre_ref[aligned(owner, plan.pre_block), :] = ref[plan.gene_rows :, :].astype(F32)
    whole_ref[plan.genes :, :] = pre_ref[...].astype(BF)


def collect_weight(plan, me, part_refs, weight_ref):
    for at, ref in enumerate(part_refs):
        weight_ref[aligned(me ^ at, plan.part), :] = ref[...]


def collect_own(plan, me, part_refs, cut_refs, own_ref, weight_ref):
    collect_weight(plan, me, part_refs, own_ref if plan.whole else weight_ref)
    if not plan.whole:
        own_ref[...] = dot(weight_ref[...], cut_refs[0][...]).astype(BF)


def give_blocks(plan, chip, block_refs, rows_ref, weight, weight_dim, pre_ref):
    pre_ref[...] = dot(rows_ref[plan.genes :, :], weight, 1, weight_dim)
    for at, ref in enumerate(block_refs):
        owner = chip ^ at
        ref[: plan.gene_rows, :] = dot(
            rows_ref[aligned(owner, plan.gene_rows), :], weight, 1, weight_dim
        ).astype(BF)
        ref[plan.gene_rows :, :] = pre_ref[aligned(owner, plan.pre_block), :].astype(BF)


def project_kernel(plan, me_ref, *refs):
    chips, groups = plan.chips, plan.groups
    pieces, parts, refs = refs[:chips], refs[chips : chips + groups], refs[chips + groups :]
    bias_ref, query_ref, pair_ref, pre_ref, low_ref, weight_ref = refs
    collect(plan, me_ref[1], pieces, low_ref, pre_ref)
    collect_weight(plan, me_ref[0], parts, weight_ref)
    query_ref[...] = jnp.zeros_like(query_ref)
    pair_ref[...] = jnp.zeros_like(pair_ref)
    for rows in plan.halves(plan.rows):
        narrow = (dot(low_ref[rows, :], weight_ref[...]) + bias_ref[...]).astype(BF)
        for head in range(plan.window):
            for block, (ref, to) in enumerate(((query_ref, 0), (pair_ref, 0), (pair_ref, HALF))):
                to += head * LANES
                begin = block * plan.wide + head * HEAD_DIM
                ref[rows, to : to + HEAD_DIM] = narrow[:, begin : begin + HEAD_DIM]


def order_pairs(plan, core, mine_ref, other_ref, keys_ref, pre_ref):
    for chip in range(plan.chips):
        for ref, place in ((mine_ref, 2 * chip + core), (other_ref, 2 * chip + 1 - core)):
            genes = slice(chip * plan.gene_rows, (chip + 1) * plan.gene_rows)
            keys_ref[aligned(place, plan.gene_rows), :] = ref[genes, :]
            prefix = slice(
                plan.genes + chip * plan.pre_block, plan.genes + (chip + 1) * plan.pre_block
            )
            pre_ref[aligned(place, plan.pre_block), :] = ref[prefix, :].astype(F32)
    keys_ref[2 * plan.genes :, :] = pre_ref[...].astype(BF)


def attend_kernel(plan, me_ref, *refs):
    query_ref, mine_ref, other_ref, out_weight_ref, padded_ref, lse_ref = refs[:6]
    blocks = refs[6 : 6 + plan.chips]
    key_pre_ref, out_pre_ref, keys_ref, turned_ref, score_ref = refs[6 + plan.chips :]
    core = me_ref[2]
    order_pairs(plan, core, mine_ref, other_ref, keys_ref, key_pre_ref)
    for head in range(plan.window):
        at = slice(LANES * head, LANES * (head + 1))
        turned_ref[...] = keys_ref[:, at].astype(F32).T.astype(BF)
        for first, count, key_parts in query_chunks(plan):
            query = query_ref[first : first + count, at]
            top = None
            for start, size, diagonal in key_parts:
                scores = dot(keys_ref[start : start + size, at], query, 1, 1)
                scores = masked(plan, scores, start, diagonal, core)
                score_ref[start : start + size, :count] = scores
                high = jnp.max(scores, axis=0, keepdims=True)
                top = high if top is None else jnp.maximum(top, high)
            top = top * SCALE2
            total, mixed = 0.0, 0.0
            for start, size, _ in key_parts:
                weights = jnp.exp2(score_ref[start : start + size, :count] * SCALE2 - top)
                total = total + jnp.sum(weights, axis=0, keepdims=True)
                mixed = mixed + dot(turned_ref[:, start : start + size], weights.astype(BF))
            padded_ref[first : first + count, at] = (mixed * (1.0 / total)).T.astype(BF)
            lse_ref[head, :, first : first + count] = top + jnp.log2(total)
    give_blocks(plan, me_ref[1], blocks, padded_ref, out_weight_ref[...], 0, out_pre_ref)


def attend_back_kernel(plan, me_ref, *refs):
    pieces, refs = refs[: plan.chips], refs[plan.chips :]
    out_weight_ref, query_ref, own_pair_ref, other_pair_ref, lse_ref = refs[:5]
    query_grad_ref, mine_ref, other_ref, out_bias_ref = refs[5:9]
    pre_ref, key_pre_ref, low_ref, keys_ref, grad_ref, turned_ref, prob_ref, pgrad_ref, pair_ref = refs[9:]
    core = me_ref[2]
    collect(plan, me_ref[1], pieces, low_ref, pre_ref)
    order_pairs(plan, core, own_pair_ref, other_pair_ref, keys_ref, key_pre_ref)
    out_bias_ref[...] = jnp.sum(low_ref[...].astype(F32), axis=0, keepdims=True)
    for rows in plan.halves(plan.rows):
        grad_ref[rows, :] = dot(low_ref[rows, :], out_weight_ref[...], 1, 1).astype(BF)
    lane = lax.broadcasted_iota(jnp.int32, (1, LANES), 1)
    pair_scale = jnp.where(lane < HALF, SCALE, 1.0)
    for head in range(plan.window):
        at = slice(LANES * head, LANES * (head + 1))
        turned_ref[...] = keys_ref[:, at].astype(F32).T.astype(BF)
        pair_ref[...] = jnp.zeros_like(pair_ref)
        for first, count, key_parts in query_chunks(plan):
            query = query_ref[first : first + count, at]
            grad = grad_ref[first : first + count, at]
            both = jnp.concatenate([grad, query], 0)
            lse = lse_ref[head, :, first : first + count]
            delta = 0.0
            for start, size, diagonal in key_parts:
                pair = keys_ref[start : start + size, at]
                scores = masked(plan, dot(pair, query, 1, 1), start, diagonal, core)
                probs = jnp.exp2(scores * SCALE2 - lse)
                prob_grad = dot(pair, grad, 1, 1)
                delta = delta + jnp.sum(probs * prob_grad, axis=0, keepdims=True)
                prob_ref[start : start + size, :count] = probs
                pgrad_ref[start : start + size, :count] = prob_grad
            query_grad = 0.0
            for start, size, _ in key_parts:
                probs = prob_ref[start : start + size, :count]
                score_grad = (probs * (pgrad_ref[start : start + size, :count] - delta)).astype(BF)
                pair_ref[start : start + size, :] += dot(
                    jnp.concatenate([probs.astype(BF), score_grad], 1), both
                )
                query_grad = query_grad + dot(turned_ref[:, start : start + size], score_grad)
            query_grad_ref[first : first + count, at] = (query_grad.T * SCALE).astype(BF)
        for chip in range(plan.chips):
            for ref, place in ((mine_ref, 2 * chip + core), (other_ref, 2 * chip + 1 - core)):
                genes = slice(chip * plan.gene_rows, (chip + 1) * plan.gene_rows)
                ref[genes, at] = (pair_ref[aligned(place, plan.gene_rows), :] * pair_scale).astype(ref.dtype)
                prefix = slice(
                    plan.genes + chip * plan.pre_block, plan.genes + (chip + 1) * plan.pre_block
                )
                place = pl.ds(
                    pl.multiple_of(2 * plan.genes + place * plan.pre_block, plan.pre_block), plan.pre_block
                )
                ref[prefix, at] = (pair_ref[place, :] * pair_scale).astype(ref.dtype)


def project_back_kernel(plan, me_ref, *refs):
    groups = plan.groups
    query_grad_ref, mine_ref, other_ref = refs[:3]
    parts, refs = refs[3 : 3 + groups], refs[3 + groups :]
    choices, refs = ([], refs) if plan.whole else (refs[:2], refs[2:])
    qkv_grad_ref, bias_ref = refs[:2]
    blocks, (pre_ref, own_ref, weight_ref) = refs[2 : 2 + plan.chips], refs[2 + plan.chips :]
    collect_own(plan, me_ref[0], parts, choices[1:], own_ref, weight_ref)
    for rows in plan.halves(plan.rows):
        pairs = (mine_ref[rows, :] + other_ref[rows, :].astype(F32)).astype(BF)
        if not plan.whole:
            select_ref = choices[0]
            qkv_grad_ref[rows, :] = (
                dot(query_grad_ref[rows, :], select_ref[: plan.lanes, :])
                + dot(pairs, select_ref[plan.lanes :, :])
            ).astype(BF)
            continue
        queries = query_grad_ref[rows, :]
        for head in range(plan.window):
            for block, (value, at) in enumerate(((queries, 0), (pairs, 0), (pairs, HALF))):
                at += head * LANES
                to = block * plan.wide + head * HEAD_DIM
                qkv_grad_ref[rows, to : to + HEAD_DIM] = value[:, at : at + HEAD_DIM]
    bias_ref[...] = jnp.sum(qkv_grad_ref[...].astype(F32), axis=0, keepdims=True)
    give_blocks(plan, me_ref[1], blocks, qkv_grad_ref, own_ref[...], 1, pre_ref)


ROOT = math.sqrt(2.0 / math.pi)
CUBE = 0.044715


def stack_pieces(plan, pieces, low_ref):
    size = plan.step_rows
    for at, ref in enumerate(pieces):
        low_ref[at * size : at * size + plan.own_rows, :] = ref[...]
        if plan.own_rows < size:
            low_ref[at * size + plan.own_rows : (at + 1) * size, :] = jnp.zeros(
                (size - plan.own_rows, low_ref.shape[1]), BF
            )


def collect_down(plan, core, mine_ref, other_ref, down_ref):
    if plan.hidden % 16 == 0:
        down_ref[aligned(core, plan.hidden), :] = mine_ref[...]
        down_ref[aligned(1 - core, plan.hidden), :] = other_ref[...]
        return
    mine, other = mine_ref[...].astype(F32), other_ref[...].astype(F32)
    halves = [jnp.where(core == 0, mine, other), jnp.where(core == 0, other, mine)]
    down_ref[...] = jnp.concatenate(halves, 0).astype(BF)


def lift_kernel(plan, me_ref, *refs):
    chips, groups = plan.chips, plan.groups
    pieces, parts, refs = refs[:chips], refs[chips : chips + groups], refs[chips + groups :]
    bias_ref, mine_ref, other_ref = refs[:3]
    blocks, (low_ref, up_ref, down_ref) = refs[3 : 3 + chips], refs[3 + chips :]
    collect_weight(plan, me_ref[0], parts, up_ref)
    stack_pieces(plan, pieces, low_ref)
    collect_down(plan, me_ref[2], mine_ref, other_ref, down_ref)
    size = plan.step_rows
    for first in range(0, plan.all_rows, 2 * size):
        rows = slice(first, first + 2 * size)
        pre = dot(low_ref[rows, :], up_ref[...]) + bias_ref[...]
        active = (0.5 * pre * (1.0 + jnp.tanh(ROOT * (pre + CUBE * pre * pre * pre)))).astype(BF)
        lifted = dot(active, down_ref[...])
        for at in range(2):
            blocks[first // size + at][...] = lifted[at * size : at * size + plan.own_rows].astype(BF)


def lift_back_kernel(plan, me_ref, *refs):
    chips, groups = plan.chips, plan.groups
    pieces, grads, refs = refs[:chips], refs[chips : 2 * chips], refs[2 * chips :]
    parts, refs = refs[:groups], refs[groups:]
    bias_ref, mine_ref, other_ref, active_ref, pre_grad_ref, down_bias_ref, up_bias_ref = refs[:7]
    blocks, (low_ref, grad_ref, up_ref, down_ref) = refs[7 : 7 + chips], refs[7 + chips :]
    collect_weight(plan, me_ref[0], parts, up_ref)
    stack_pieces(plan, pieces, low_ref)
    stack_pieces(plan, grads, grad_ref)
    collect_down(plan, me_ref[2], mine_ref, other_ref, down_ref)
    size = plan.step_rows
    down_bias_ref[...] = jnp.sum(grad_ref[...].astype(F32), axis=0, keepdims=True)
    up_bias = 0.0
    for first in range(0, plan.all_rows, 2 * size):
        rows = slice(first, first + 2 * size)
        pre = dot(low_ref[rows, :], up_ref[...]) + bias_ref[...]
        act_grad = dot(grad_ref[rows, :], down_ref[...], 1, 1)
        square = pre * pre
        turn = jnp.tanh(ROOT * pre * (1.0 + CUBE * square))
        active_ref[rows, :] = (0.5 * pre * (1.0 + turn)).astype(BF)
        slope = 0.5 * (1.0 + turn) + (0.5 * ROOT) * pre * (1.0 - turn * turn) * (1.0 + 3.0 * CUBE * square)
        pre_grad = (act_grad * slope).astype(BF)
        pre_grad_ref[rows, :] = pre_grad
        up_bias = up_bias + jnp.sum(pre_grad.astype(F32), axis=0, keepdims=True)
        norm_grad = dot(pre_grad, up_ref[...], 1, 1)
        for at in range(2):
            blocks[first // size + at][...] = norm_grad[at * size : at * size + plan.own_rows].astype(BF)
    up_bias_ref[...] = up_bias


def send_kernel(plan, level, starts, width, me_ref, weight_ref, *refs):
    outs, (stack_ref,) = refs[: plan.chips], refs[plan.chips :]
    for to, begins in enumerate(starts):
        for at, begin in enumerate(begins):
            stack_ref[to, : plan.cols, at * width : (at + 1) * width] = weight_ref[
                level, :, begin : begin + width
            ]
        if plan.cols < plan.part:
            stack_ref[to, plan.cols :, :] = jnp.zeros(
                (plan.part - plan.cols, stack_ref.shape[2]), BF
            )
    for at, ref in enumerate(outs):
        ref[...] = stack_ref[me_ref[1] ^ at]


def norm_weight_grad(plan, left_ref, right_ref, weight_ref, sums_ref, vector_ref, whole_ref):
    width = right_ref.shape[1]
    step = 2 * plan.part
    for first in range(0, plan.features, step):
        rows = slice(first, first + step)
        product = dot(left_ref[:, rows], right_ref[...], 0, 0)
        weight = weight_ref[rows, :].astype(F32)
        shift_grad = jnp.sum(weight * sums_ref[...], axis=1, keepdims=True)
        both = jnp.sum(weight * product, axis=1, keepdims=True)
        turned = vector_ref[:, rows].T
        gain_grad = (both - turned[:, 0:1] * shift_grad) / turned[:, 1:2]
        whole_ref[rows, :width] = product
        whole_ref[rows, width : width + 2] = jnp.concatenate([shift_grad, gain_grad], 1)


def give_parts(plan, me, whole_ref, mine_ref, other_ref):
    width = whole_ref.shape[1]
    for at in range(plan.chips):
        owner = me ^ (2 * at)
        mine_ref[at, :, :width] = whole_ref[aligned(owner, plan.part), :].astype(BF)
        other_ref[at, :, :width] = whole_ref[aligned(owner ^ 1, plan.part), :].astype(BF)


def lift_grad_kernel(plan, me_ref, *refs):
    chips, groups = plan.chips, plan.groups
    pieces, grads, refs = refs[:chips], refs[chips : 2 * chips], refs[2 * chips :]
    parts, refs = refs[:groups], refs[groups:]
    active_ref, pre_grad_ref, sums_ref, vector_ref, up_mine, up_other, down_mine, down_other = refs[:8]
    low_ref, grad_ref, up_ref, whole_ref, down_ref = refs[8:]
    core = me_ref[2]
    stack_pieces(plan, pieces, low_ref)
    collect_weight(plan, me_ref[0], parts, up_ref)
    norm_weight_grad(plan, low_ref, pre_grad_ref, up_ref, sums_ref, vector_ref, whole_ref)
    give_parts(plan, me_ref[0], whole_ref, up_mine, up_other)
    stack_pieces(plan, grads, grad_ref)
    for rows in plan.halves(plan.chip_hidden):
        down_ref[rows, :] = dot(active_ref[:, rows], grad_ref[...], 0, 0)
    size = plan.hidden // 4
    filler = jnp.zeros((down_mine.shape[1] - size, D), F32)
    for at in range(4):
        first = down_ref[at * size : (at + 1) * size, :]
        second = down_ref[plan.hidden + at * size : plan.hidden + (at + 1) * size, :]
        for ref, rows in (
            (down_mine, jnp.where(core == 0, first, second)),
            (down_other, jnp.where(core == 0, second, first)),
        ):
            ref[at] = jnp.concatenate([rows, filler], 0).astype(BF)


def attend_grad_kernel(plan, riding, me_ref, *refs):
    chips, groups = plan.chips, plan.groups
    pieces, grads, refs = refs[:chips], refs[chips : 2 * chips], refs[2 * chips :]
    parts, refs = refs[:groups], refs[groups:]
    choices, refs = ([], refs) if plan.whole else (refs[:2], refs[2:])
    mixed_ref, qkv_grad_ref, sums_ref, vector_ref, small_ref, mine_ref, other_ref = refs[:7]
    low_ref, grad_ref, pre_ref, grad_pre_ref, own_ref, weight_ref, whole_ref, out_ref = refs[-8:]
    core = me_ref[2]
    collect(plan, me_ref[1], pieces, low_ref, pre_ref)
    collect_own(plan, me_ref[0], parts, choices[1:], own_ref, weight_ref)
    norm_weight_grad(plan, low_ref, qkv_grad_ref, own_ref, sums_ref, vector_ref, whole_ref)
    give_parts(plan, me_ref[0], whole_ref, mine_ref, other_ref)
    collect(plan, me_ref[1], grads, grad_ref, grad_pre_ref)
    if plan.whole:
        for head in range(plan.window):
            product = dot(mixed_ref[:, head * LANES : (head + 1) * LANES], grad_ref[...], 0, 0)
            out_ref[head * HEAD_DIM : (head + 1) * HEAD_DIM, :] = product[HALF : HALF + HEAD_DIM]
    else:
        own = dot(mixed_ref[...], choices[0][...]).astype(BF)
        out_ref[...] = dot(own, grad_ref[...], 0, 0)
    halves = out_ref[: plan.cols, :], out_ref[plan.cols :, :]
    extra = small_ref.shape[1]
    filler = jnp.zeros((plan.part - plan.cols - extra, D), F32)
    first = whole_ref.shape[1]
    for at, (ref, one, two) in enumerate(((mine_ref, 0, 1), (other_ref, 1, 0))):
        rows = jnp.where(core == 0, halves[one], halves[two])
        rows = jnp.concatenate([rows, small_ref[at], filler], 0).astype(BF)
        if not riding:
            refs[7 + at][...] = rows
            continue
        for chip in range(chips):
            ref[chip, :, first:] = rows[:, chip * plan.chip_cols : (chip + 1) * plan.chip_cols]


def join_down_kernel(plan, *refs):
    parts, out_ref = refs[:LAYERS], refs[LAYERS]
    size = plan.hidden // 4
    for level, ref in enumerate(parts):
        for at in range(4):
            out_ref[level, at * size : (at + 1) * size, :] = ref[at, :size, :].astype(F32)


def join_kernel(plan, blocks, width, me_ref, *refs):
    count = LAYERS * plan.chips
    parts, (out_ref, vector_ref, stack_ref) = refs[:count], refs[count:]
    each = width // blocks
    for level in range(LAYERS):
        for at in range(plan.chips):
            stack_ref[at] = parts[level * plan.chips + at][...]
        vectors = 0.0
        for source in range(plan.chips):
            value = stack_ref[me_ref[1] ^ source].astype(F32)
            for block in range(blocks):
                begin = (block * plan.chips + source) * each
                out_ref[:, level, begin : begin + each] = value[
                    : plan.cols, block * each : (block + 1) * each
                ]
            vectors = vectors + value[:, width : width + 2]
        padded = jnp.concatenate([vectors, jnp.zeros((plan.part, LANES - 2), F32)], 1)
        vector_ref[level] = padded.T[:8]


def body(
    genes,
    prefix,
    cot_genes,
    cot_prefix,
    w_qkv,
    w_out,
    w_up,
    w_down,
    norm1_gain,
    norm1_bias,
    norm2_gain,
    norm2_bias,
    bias_q,
    bias_v,
    bias_out,
    bias_up,
    bias_down,
):
    groups = lax.axis_size("gene")
    cells = lax.axis_size("cell")
    me = lax.axis_index("gene")
    cell = lax.axis_index("cell")
    chip, core = me // 2, me % 2
    plan = Plan(groups, genes.shape[1])
    chips, cols, chip_cols, wide = plan.chips, plan.cols, plan.chip_cols, plan.wide
    hidden, chip_hidden = plan.hidden, plan.chip_hidden
    first_head = jnp.asarray(plan.first_heads, jnp.int32)[chip]
    offset = chip * chip_cols - first_head * HEAD_DIM
    turn = chip if plan.by_links else jnp.zeros_like(chip)
    where = jnp.stack([2 * turn + core, turn, core]).astype(jnp.int32)
    same_core = [[2 * at + one for at in range(chips)] for one in range(2)]
    here = functools.partial

    def after(value, *others):
        return lax.optimization_barrier((value,) + others)[0]

    def after_all(values, *others):
        return list(lax.optimization_barrier((tuple(values), others))[0])

    def together(*lists):
        return [list(got) for got in lax.optimization_barrier(tuple(tuple(x) for x in lists))]

    def swap(value, bits):
        return lax.ppermute(value, "gene", [(at, at ^ bits) for at in range(groups)])

    def to_chips(parts):
        if not plan.by_links:
            got = lax.all_to_all(jnp.stack(parts), "gene", 0, 0, axis_index_groups=same_core)
            return [got[at] for at in range(chips)]
        return [parts[0]] + [swap(parts[at], 2 * at) for at in range(1, chips)]

    def gather(piece):
        if not plan.by_links:
            got = lax.all_gather(piece, "gene", axis=0, axis_index_groups=same_core)
            return [got[at] for at in range(chips)]
        return to_chips([piece] * chips)

    def scatter(blocks):
        if not plan.by_links:
            return [
                lax.psum_scatter(
                    jnp.stack(blocks), "gene", scatter_dimension=0, axis_index_groups=same_core
                )
            ]
        return to_chips(blocks)

    def across(near):
        far = [swap(value, 1) for value in near]
        return [value for pair in zip(near, far) for value in pair]

    class CellSum:
        def __init__(self, mine, other, *steps):
            self.value = (mine.astype(F32) + other.astype(F32)).astype(BF)
            self.steps = list(steps) if cells == 4 else [steps[-1]]
            self.moves = len(steps)
            waiting.append(self)

        def half(self, bit):
            halves = self.value.reshape((2, self.value.shape[0] // 2) + self.value.shape[1:])
            return lax.dynamic_index_in_dim(halves, bit, 0, keepdims=False)

        def move(self):
            if cells != 4:
                return lax.psum(self.value, "cell")
            left = len(self.steps)
            if self.moves == 3:
                inwards, between, outwards = [(0, 1), (3, 2)], [(1, 2), (2, 1)], [(1, 0), (2, 3)]
                return lax.ppermute(self.value, "cell", {3: inwards, 2: between, 1: outwards}[left])
            self.away = 1 if left in (1, 4) else 2
            self.bit = cell // self.away % 2
            value = self.half(1 - self.bit) if left > 2 else self.value
            return lax.ppermute(value, "cell", [(at, at ^ self.away) for at in range(4)])

        def land(self, got):
            left = len(self.steps)
            if cells != 4:
                self.value = got
            elif self.moves == 3 and left == 1:
                self.value = jnp.where((cell == 1) | (cell == 2), self.value, got)
            elif left > 2 or self.moves == 3:
                value = self.value if self.moves == 3 else self.half(self.bit)
                self.value = (value.astype(F32) + got.astype(F32)).astype(BF)
            else:
                first, second = (
                    jnp.where(self.bit == at, self.value, got) for at in range(2)
                )
                self.value = jnp.concatenate([first, second], 0)
            self.steps.pop(0)

    waiting = []

    def beside(step, *lists):
        moving = [item for item in waiting if item.steps and item.steps[0] == step]
        *lists, landed = together(*lists, [item.move() for item in moving])
        for item, got in zip(moving, landed):
            item.land(got)
        return lists

    def send(weight, level, starts, width, *others):
        total = len(starts[0]) * width
        return call(
            here(send_kernel, plan, level, starts, width),
            "send",
            [after(where, *others), weight],
            [shape_of(plan.part, total)] * chips,
            [pltpu.VMEM((chips, plan.part, total), BF)],
            True,
        )

    qkv_starts = [
        [block * D + head * HEAD_DIM for block in range(3)] for head in plan.first_heads
    ]
    up_starts = [[to * chip_hidden] for to in range(chips)]

    def chooser(wanted, there):
        return (wanted[:, None] == there[None, :]).astype(BF)

    def own_of(block, column, real):
        ok = real & (column >= offset) & (column < offset + chip_cols)
        return jnp.where(ok, block * chip_cols + column - offset, -1)

    window_at = jnp.arange(3 * wide)
    own_columns = jnp.arange(3 * chip_cols)
    cut = chooser(own_of(window_at // wide, window_at % wide, True), own_columns)
    lanes = jnp.arange(2 * plan.lanes)
    inner = lanes % LANES
    is_pair = lanes >= plan.lanes
    block = jnp.where(is_pair, 1 + inner // HALF, 0)
    inner = jnp.where(is_pair, inner % HALF, inner)
    column = (lanes % plan.lanes) // LANES * HEAD_DIM + inner
    select = chooser(own_of(block, column, inner < HEAD_DIM), own_columns)
    at_out = jnp.arange(plan.lanes)
    inner = at_out % LANES - HALF
    out_col = (at_out // LANES) * HEAD_DIM + inner
    out_ok = (inner >= 0) & (inner < HEAD_DIM)
    out_select = chooser(own_of(0, out_col, out_ok), jnp.arange(chip_cols))

    def out_windows():
        if plan.by_links:
            rows = jnp.concatenate([w_out, swap(w_out, 1)], 1)
            own = jnp.arange(cols)
            owner = jnp.concatenate([me * cols + own, (me ^ 1) * cols + own])
        else:
            rows = lax.all_gather(w_out, "gene", axis=1, tiled=True)
            owner = jnp.arange(D)
        wanted = jnp.where(out_ok, first_head * HEAD_DIM + out_col, -1)
        is_own = (out_col >= offset) & (out_col < offset + chip_cols)
        picks = [chooser(wanted, owner)]
        if not plan.whole:
            picks.append(chooser(jnp.where(is_own, wanted, -1), owner))
        got = [[dot(pick, rows[level]).astype(BF) for level in range(LAYERS)] for pick in picks]
        return got[0], got[-1]

    def window_of(vec):
        return lax.dynamic_slice_in_dim(vec, first_head * HEAD_DIM, wide, 1)

    def norm_vectors(token):
        every = jnp.stack([norm1_bias, norm1_gain, norm2_bias, norm2_gain])
        every = after(every, token).reshape(2, 2, LAYERS, groups, cols)
        every = jnp.pad(every, ((0, 0),) * 4 + ((0, plan.part - cols),), constant_values=1.0)
        every = every.transpose(0, 2, 1, 3, 4).reshape(2 * LAYERS, 2, plan.features)
        every = jnp.pad(every, ((0, 0), (0, 6), (0, 0)))
        return [every[at] for at in range(2 * LAYERS)]

    rows_f32 = shape_of(plan.own_rows, D, dtype=F32)
    normed_like = shape_of(plan.own_rows, plan.features)
    grad_like = shape_of(plan.own_rows, D)
    row_blocks = [grad_like] * chips
    feature_blocks = [normed_like] * chips
    vector = shape_of(1, D, dtype=F32)
    ends_like = [
        shape_of(D, plan.gene_rows, dtype=F32),
        shape_of(plan.pre_block, D, dtype=F32),
    ]

    own_prefix = lax.dynamic_slice_in_dim(prefix[0], me * plan.pre_rows, plan.pre_rows, 0)
    filler = ((0, plan.pre_block - plan.pre_rows), (0, 0))
    rows, piece = call(
        here(begin_kernel, plan),
        "begin",
        [genes[0].T, jnp.pad(own_prefix, filler), norm1_gain, norm1_bias],
        [rows_f32, normed_like],
    )
    qkv_parts, up_parts = [None] * LAYERS, [None] * LAYERS
    qkv_sent = send(w_qkv, 0, qkv_starts, wide, piece)
    pieces, near = gather(piece), to_chips(qkv_sent)
    token = qkv_sent[-1]
    up_sent = send(w_up, 0, up_starts, chip_hidden, token)
    qkv_biases = jnp.concatenate(
        [window_of(bias_q), jnp.zeros((LAYERS, wide), F32), window_of(bias_v)], 1
    )
    windows, out_weights = out_windows()
    pieces, near, up_sent, _ = together(
        pieces, near, up_sent, [qkv_biases] + windows + out_weights
    )
    up_biases = lax.dynamic_slice_in_dim(bias_up, chip * chip_hidden, chip_hidden, 1)
    (qkv_parts[0],) = together(across(near))

    saved, downs = [], []
    for level in range(LAYERS):
        last = level + 1 == LAYERS
        if level:
            (pieces, far) = together(gather(piece), across(near[chips // 2 :]))
            qkv_parts[level] = qkv_far + far
        up_near = to_chips(after_all(up_sent, *pieces, *qkv_parts[level]))
        low_one = pieces
        query, pair = call(
            here(project_kernel, plan),
            "project",
            [where] + pieces + qkv_parts[level] + [qkv_biases[level : level + 1]],
            [shape_of(plan.rows, plan.lanes), shape_of(plan.rows, plan.lanes)],
            [
                pltpu.VMEM((plan.prefix, plan.features), F32),
                pltpu.VMEM((plan.rows, plan.features), BF),
                pltpu.VMEM((plan.features, 3 * wide), BF),
            ],
            True,
        )
        other_pair = swap(pair, 1)
        own_down = after(w_down, pair)[level]
        other_down = swap(own_down, 1)
        if not last:
            qkv_sent = send(w_qkv, level + 1, qkv_starts, wide, pair)
            up_sent = send(w_up, level + 1, up_starts, chip_hidden, pair)
            other_pair = after(other_pair, qkv_sent[-1], up_sent[-1])
        outs = call(
            here(attend_kernel, plan),
            "attend",
            [where, query, pair, other_pair, out_weights[level]],
            [
                shape_of(plan.rows, plan.lanes),
                shape_of(plan.window, 1, plan.rows, dtype=F32),
            ]
            + row_blocks,
            [
                pltpu.VMEM((2 * plan.prefix, plan.lanes), F32),
                pltpu.VMEM((plan.prefix, D), F32),
                pltpu.VMEM((2 * plan.rows, plan.lanes), BF),
                pltpu.VMEM((LANES, 2 * plan.rows), BF),
                pltpu.VMEM((2 * plan.rows, 2 * plan.gene_rows), F32),
            ],
            True,
        )
        outs, up_near, (own_down, other_down) = together(outs, up_near, [own_down, other_down])
        downs.append([own_down, other_down])
        mixed, lse = outs[:2]
        parts, up_far = together(scatter(outs[2:]), across(up_near[: chips // 2]))
        middle, piece = call(
            here(middle_kernel, plan, len(parts), level, level),
            "middle",
            parts + [rows, bias_out, norm2_gain, norm2_bias],
            [rows_f32, normed_like],
        )
        if last:
            cot_grad, cot_piece = call(
                here(cot_kernel, plan),
                "cotangent",
                [after(cot_genes[0].T, piece), jnp.pad(cot_prefix[0], filler)],
                [rows_f32, grad_like],
            )
            spare = [cot_grad, cot_piece]
        else:
            spare = []
        pieces, far, spare = together(gather(piece), across(up_near[chips // 2 :]), spare)
        up_parts[level] = up_far + far
        if last:
            cot_grad, cot_piece = spare
            near = gather(after(cot_piece, *pieces))
        else:
            near = to_chips(after_all(qkv_sent, *pieces))
        low_two = pieces
        blocks = call(
            here(lift_kernel, plan),
            "lift",
            [where]
            + pieces
            + up_parts[level]
            + [up_biases[level : level + 1]] + downs[level],
            row_blocks,
            [
                pltpu.VMEM((plan.all_rows, plan.features), BF),
                pltpu.VMEM((plan.features, chip_hidden), BF),
                pltpu.VMEM((chip_hidden, D), BF),
            ],
            True,
        )
        blocks, near = together(blocks, near)
        saved.append((rows, low_one, query, pair, other_pair, mixed, lse, middle, low_two))
        if last:
            cot_pieces = near
            last_blocks, last_middle = blocks, middle
        else:
            spare = []
            if level == 0:
                spare = norm_vectors(low_two[0])
            parts, qkv_far, spare = together(scatter(blocks), across(near[: chips // 2]), spare)
            if level == 0:
                vectors = spare
            rows, piece = call(
                here(middle_kernel, plan, len(parts), level, level + 1),
                "next_rows",
                parts + [middle, bias_down, norm1_gain, norm1_bias],
                [rows_f32, normed_like],
            )

    def of_cores(value, size, dim):
        return [
            lax.dynamic_slice_in_dim(value, at * size, size, dim) for at in (core, 1 - core)
        ]

    def messages_of(item, width):
        return [item.value[at, :, :width] for at in range(chips)]

    grad, pieces = cot_grad, cot_pieces
    down_sums, up_sums, qkv_sums = ([None] * LAYERS for _ in range(3))
    long_rows, short_rows, up_rows = [None] * (2 * LAYERS), [None] * (2 * LAYERS), [None] * LAYERS
    extra = -(-LAYERS * (4 * cols + hidden) // D)
    choices = [] if plan.whole else [select, cut]
    out_choices = [] if plan.whole else [out_select, cut]
    stacked = pltpu.VMEM((plan.all_rows, plan.features), BF)
    stacked_grad = pltpu.VMEM((plan.all_rows, D), BF)
    up_room = pltpu.VMEM((plan.features, chip_hidden), BF)
    own_room = pltpu.VMEM((plan.features, 3 * chip_cols), BF)
    window_room = pltpu.VMEM((8, LANES) if plan.whole else (plan.features, 3 * wide), BF)
    for level in reversed(range(LAYERS)):
        rows, low_one, query, pair, other_pair, mixed, lse, middle, low_two = saved[level]
        if level + 1 < LAYERS:
            (pieces,) = beside(f"rows {level}", gather(piece))
        down_grad = pieces
        outs = call(
            here(lift_back_kernel, plan),
            "lift_back",
            [where]
            + low_two
            + pieces
            + up_parts[level]
            + [up_biases[level : level + 1]] + downs[level],
            [
                shape_of(plan.all_rows, chip_hidden),
                shape_of(plan.all_rows, chip_hidden),
                vector,
                shape_of(1, chip_hidden, dtype=F32),
            ]
            + feature_blocks,
            [stacked, stacked_grad, up_room, pltpu.VMEM((chip_hidden, D), BF)],
            True,
        )
        (outs,) = beside(f"lifted {level}", outs)
        if not level:
            outs = after_all(outs, up_sums[1].value)
        active, pre_grad, long_rows[level], up_rows[level] = outs[:4]
        up_mine, up_other, down_mine, down_other = call(
            here(lift_grad_kernel, plan),
            "lift_grad",
            [where]
            + low_two
            + down_grad
            + up_parts[level]
            + [active, pre_grad, up_rows[level], vectors[LAYERS + level]],
            [shape_of(chips, plan.part, chip_hidden + 2)] * 2
            + [shape_of(4, -(-hidden // 64) * 16, D)] * 2,
            [
                stacked,
                stacked_grad,
                up_room,
                pltpu.VMEM((plan.features, chip_hidden + 2), F32),
                pltpu.VMEM((chip_hidden, D), F32),
            ],
            True,
        )
        parts, (up_mine, up_other, down_mine, down_other) = beside(
            f"lift {level}", scatter(outs[4:]), [up_mine, up_other, down_mine, down_other]
        )
        middle_grad, piece = call(
            here(back_kernel, plan, len(parts), level),
            "middle_back",
            parts + [middle, norm2_gain, grad],
            [rows_f32, grad_like],
        )
        (middle_grad, piece, up_got, down_got), = beside(
            f"turn {level}", [middle_grad, piece, swap(up_other, 1), swap(down_other, 1)]
        )
        if level:
            down_sums[level] = CellSum(down_mine, down_got, "attend 1", "project 1", "lifted 0")
            up_sums[level] = CellSum(up_mine, up_got, "project 1", "lifted 0", "turn 0")
        else:
            down_sums[level] = CellSum(down_mine, down_got, "attend 0", "end 1", "end 2")
            up_sums[level] = CellSum(up_mine, up_got, "end 1", "end 2", "end 3")
        (pieces,) = beside(f"middle {level}", gather(piece))
        branch_grad = pieces
        outs = call(
            here(attend_back_kernel, plan),
            "attend_back",
            [where] + pieces + [windows[level], query, pair, other_pair, lse],
            [
                shape_of(plan.rows, plan.lanes),
                shape_of(plan.rows, plan.lanes, dtype=F32),
                shape_of(plan.rows, plan.lanes),
                vector,
            ],
            [
                pltpu.VMEM((plan.prefix, D), F32),
                pltpu.VMEM((2 * plan.prefix, plan.lanes), F32),
                pltpu.VMEM((plan.rows, D), BF),
                pltpu.VMEM((2 * plan.rows, plan.lanes), BF),
                pltpu.VMEM((plan.rows, plan.lanes), BF),
                pltpu.VMEM((LANES, 2 * plan.rows), BF),
                pltpu.VMEM((2 * plan.rows, 2 * plan.gene_rows), F32),
                pltpu.VMEM((2 * plan.rows, 2 * plan.gene_rows), F32),
                pltpu.VMEM((2 * plan.rows, LANES), F32),
            ],
            True,
        )
        if level:
            (outs,) = beside("attend 1", outs)
        else:
            up_width, qkv_width = chip_hidden + 2, 3 * chip_cols + 2
            (outs,) = beside("attend 0", outs)
        query_grad, pair_mine, pair_other, long_rows[LAYERS + level] = outs
        outs = call(
            here(project_back_kernel, plan),
            "project_back",
            [where, query_grad, pair_mine, swap(pair_other, 1)] + qkv_parts[level] + choices,
            [shape_of(plan.rows, 3 * chip_cols), shape_of(1, 3 * chip_cols, dtype=F32)]
            + feature_blocks,
            [pltpu.VMEM((plan.prefix, plan.features), F32), own_room, window_room],
            True,
        )
        qkv_grad, qkv_bias = outs[:2]
        short_rows[level] = qkv_bias[:, :chip_cols]
        short_rows[LAYERS + level] = qkv_bias[:, 2 * chip_cols :]
        small = jnp.zeros((2, extra, D), F32)
        if not level:
            long_own = lax.dynamic_slice_in_dim(
                jnp.concatenate(long_rows, 0), chip * chip_cols, chip_cols, 1
            )
            small = [
                jnp.concatenate([vec.reshape(-1) for vec in vecs])
                for vecs in zip(
                    of_cores(long_own, cols, 1),
                    of_cores(jnp.concatenate(short_rows, 0), cols, 1),
                    of_cores(jnp.concatenate(up_rows, 0), hidden, 1),
                )
            ]
            small = jnp.stack(
                [jnp.pad(vec, (0, extra * D - vec.size)).reshape(extra, D) for vec in small]
            )
        width = 3 * chip_cols + 2
        made = call(
            here(attend_grad_kernel, plan, bool(level)),
            "attend_grad",
            [where]
            + low_one
            + branch_grad
            + qkv_parts[level]
            + out_choices
            + [mixed, qkv_grad, qkv_bias, vectors[level], small],
            [shape_of(chips, plan.part, width + (chip_cols if level else 0))] * 2
            + [shape_of(plan.part, D)] * (0 if level else 2),
            [
                pltpu.VMEM((plan.rows, plan.features), BF),
                pltpu.VMEM((plan.rows, D), BF),
                pltpu.VMEM((plan.prefix, plan.features), F32),
                pltpu.VMEM((plan.prefix, D), F32),
                own_room,
                window_room,
                pltpu.VMEM((plan.features, 3 * chip_cols + 2), F32),
                pltpu.VMEM((chip_cols, D), F32),
            ],
            True,
        )
        blocks = outs[2:]
        if level:
            parts = scatter(blocks)
            parts, (qkv_mine, qkv_other) = beside("project 1", parts, made)
            grad, piece = call(
                here(back_kernel, plan, len(parts), level),
                "rows_back",
                parts + [rows, norm1_gain, middle_grad],
                [rows_f32, grad_like],
            )
            grad, piece, qkv_got = together([grad, piece, swap(qkv_other, 1)])[0]
            qkv_sums[level] = CellSum(qkv_mine, qkv_got, "lift 0", "attend 0", "end 1")

    (made,) = together(made)
    qkv_mine, qkv_other, out_mine, out_other = made
    qkv_got, out_got = together([swap(qkv_other, 1), swap(out_other, 1)])[0]
    qkv_sums[0] = CellSum(qkv_mine, qkv_got, "end 2", "end 3", "end 4")
    beside("end 1", [qkv_sums[0].value])
    parts, _ = beside("end 2", scatter(after_all(blocks, qkv_sums[0].value)), [up_sums[0].value])
    ends = call(
        here(back_end_kernel, plan, len(parts), 0),
        "rows_back_end",
        parts + [rows, norm1_gain, middle_grad],
        ends_like,
    )
    out_sum = (after(out_mine, parts[0]).astype(F32) + out_got.astype(F32)).astype(BF)
    up_near = to_chips(after_all(messages_of(up_sums[1], up_width), *parts))
    parts, ends, up_near = beside(
        "end 3", scatter(after_all(last_blocks, *parts)), ends, up_near
    )
    result = call(
        here(finish_kernel, plan, len(parts), LAYERS - 1),
        "finish",
        parts + [last_middle, bias_down],
        ends_like,
    )
    near = to_chips(after_all(messages_of(qkv_sums[1], qkv_width), *parts))
    last_up = to_chips(after_all(messages_of(up_sums[0], up_width), *parts))
    def sum_near(value, away):
        if cells != 4:
            return lax.psum(value, "cell") if away == 1 else value
        got = lax.ppermute(value, "cell", [(at, at ^ away) for at in range(cells)])
        return (value.astype(F32) + got.astype(F32)).astype(BF)

    (g_down,) = call(
        here(join_down_kernel, plan),
        "join_down",
        after_all([item.value for item in down_sums], parts[0]),
        [shape_of(LAYERS, hidden, D, dtype=F32)],
    )
    near, last_up, result, (g_down,) = beside("end 4", near, last_up, result, [g_down])
    messages = after_all(messages_of(qkv_sums[0], qkv_width))
    last_near = to_chips(messages)
    (out_sum,) = after_all([out_sum], *messages)
    last_up, up_near = (after_all(values, *messages) for values in (last_up, up_near))
    up_parts = [last_up, up_near]
    def join(parts, blocks, width):
        whole, vectors = call(
            here(join_kernel, plan, blocks, width),
            "join",
            [where] + parts[0] + parts[1],
            [
                shape_of(cols, LAYERS, blocks * D if blocks > 1 else FF, dtype=F32),
                shape_of(LAYERS, 8, plan.part, dtype=F32),
            ],
            [pltpu.VMEM((chips, plan.part, width + 2), BF)],
            scalar=True,
        )
        return whole.transpose(1, 0, 2), vectors[:, 0, :cols], vectors[:, 1, :cols]

    ups = join(up_parts, 1, chip_hidden)
    last_near, (g_up, shift_two, gain_two), (out_sum,) = together(
        last_near, ups, [sum_near(out_sum, 1)]
    )
    out_sum = sum_near(out_sum, 2)
    qkv_parts = [last_near, near]
    g_qkv, shift_one, gain_one = join(qkv_parts, 3, 3 * chip_cols)
    riders = [qkv_sums[1].value[at, : plan.cols, qkv_width:] for at in range(chips)]
    out_sums = [out_sum[:cols], after(jnp.concatenate(riders, 1), last_up[0])]
    small = out_sum[cols : cols + extra].reshape(-1).astype(F32)
    size = LAYERS * cols
    b_down, b_out, b_q, b_v = (small[at * size : (at + 1) * size].reshape(LAYERS, cols) for at in range(4))
    b_up = small[4 * size : 4 * size + LAYERS * hidden].reshape(LAYERS, hidden)

    return (
        result[0].T[None],
        result[1][: plan.pre_rows][None],
        ends[0].T[None],
        ends[1][: plan.pre_rows][None],
        g_qkv,
        jnp.stack(out_sums).astype(F32),
        g_up,
        g_down,
        gain_one,
        shift_one,
        gain_two,
        shift_two,
        b_q,
        b_v,
        b_out,
        b_up,
        b_down,
    )


def solution(mesh):
    rows = P("cell", "gene", None)
    weight = P(None, "gene", None)
    vector = P(None, "gene")
    return jax.shard_map(
        body,
        mesh=mesh,
        in_specs=(rows, P("cell", None, None), rows, rows) + (weight,) * 4 + (P(),) * 9,
        out_specs=(rows,) * 4 + (weight,) * 4 + (vector,) * 9,
        check_vma=False,
    )
```

```python
import functools
import math

import jax
import jax.numpy as jnp
from jax import lax
from jax.experimental import pallas as pl
from jax.experimental.pallas import tpu as pltpu
from jax.sharding import PartitionSpec as P

D = 1120
HEADS = 20
HEAD_DIM = 56
FF = 4480
PREFIX = 64
LAYERS = 2
LANES = 128
HALF = 64
SCALE = HEAD_DIM ** (-0.5)
SCALE2 = SCALE * math.log2(math.e)
BF = jnp.bfloat16
F32 = jnp.float32
COST = 1000


def dot(left, right, left_dim=1, right_dim=0):
    return lax.dot_general(
        left, right, (((left_dim,), (right_dim,)), ((), ())), preferred_element_type=F32
    )


class Plan:
    def __init__(self, groups, gene_rows):
        self.groups = groups
        self.chips = groups // 2
        self.gene_rows = gene_rows
        self.pre_rows = PREFIX // groups
        self.pre_block = -(-self.pre_rows // 8) * 8
        self.own_rows = gene_rows + self.pre_block
        self.step_rows = -(-self.own_rows // 16) * 16
        self.genes = self.chips * gene_rows
        self.prefix = self.chips * self.pre_block
        self.rows = self.genes + self.prefix
        self.all_rows = self.chips * self.step_rows
        self.cols = D // groups
        self.chip_cols = D // self.chips
        self.hidden = FF // groups
        self.chip_hidden = FF // self.chips
        self.part = -(-self.cols // 16) * 16
        self.features = groups * self.part
        spans = [
            (self.chip_cols * at // HEAD_DIM, -(-self.chip_cols * (at + 1) // HEAD_DIM))
            for at in range(self.chips)
        ]
        self.window = max(last - first for first, last in spans)
        self.first_heads = [min(first, HEADS - self.window) for first, _ in spans]
        self.wide = self.window * HEAD_DIM
        self.lanes = self.window * LANES
        self.whole = self.wide == self.chip_cols
        self.by_links = groups == 8

    def halves(self, total):
        step = -(-total // 32) * 16
        return [slice(first, min(first + step, total)) for first in range(0, total, step)]


SCALAR = pl.BlockSpec(memory_space=pltpu.SMEM)
WHOLE = pl.BlockSpec(memory_space=pltpu.VMEM)


def call(kernel, name, args, outs, scratch=(), scalar=False):
    got = pl.pallas_call(
        kernel,
        in_specs=[SCALAR if scalar and at == 0 else WHOLE for at in range(len(args))],
        out_specs=[WHOLE] * len(outs),
        out_shape=outs,
        scratch_shapes=list(scratch),
        compiler_params=pltpu.CompilerParams(vmem_limit_bytes=58 << 20),
        cost_estimate=pl.CostEstimate(flops=COST, bytes_accessed=COST, transcendentals=0),
        name=name,
    )(*args)
    return list(got)


def shape_of(*dims, dtype=BF):
    return jax.ShapeDtypeStruct(dims, dtype)


def aligned(at, size):
    return pl.ds(pl.multiple_of(at * size, size), size)


def normed_of(values):
    centred = values - jnp.mean(values, axis=-1, keepdims=True)
    variance = jnp.mean(centred * centred, axis=-1, keepdims=True)
    inverse = lax.rsqrt(variance + 1e-05)
    return centred * inverse, inverse


def spread(plan, rows):
    filler = jnp.zeros((rows.shape[0], plan.part - plan.cols), rows.dtype)
    parts = []
    for at in range(plan.groups):
        parts += [rows[:, at * plan.cols : (at + 1) * plan.cols], filler]
    return jnp.concatenate(parts, 1)


def unspread(plan, rows):
    return jnp.concatenate(
        [rows[:, at * plan.part : at * plan.part + plan.cols] for at in range(plan.groups)], 1
    )


def real_rows(plan, rows):
    if plan.pre_rows == plan.pre_block:
        return rows
    at = lax.broadcasted_iota(jnp.int32, rows.shape, 0)
    return jnp.where(at < plan.gene_rows + plan.pre_rows, rows, 0.0)


def normed_piece(plan, rows, gain_ref, shift_ref, level):
    unit, _ = normed_of(rows)
    normed = unit * gain_ref[level : level + 1, :] + shift_ref[level : level + 1, :]
    return spread(plan, real_rows(plan, normed).astype(BF))


def begin_kernel(plan, gene_ref, pre_ref, gain_ref, shift_ref, rows_ref, piece_ref):
    rows = jnp.concatenate([gene_ref[...].astype(F32).T, pre_ref[...].astype(F32)], 0)
    rows_ref[...] = rows
    piece_ref[...] = normed_piece(plan, rows, gain_ref, shift_ref, 0)


def add_parts(refs):
    total = refs[0][...].astype(F32)
    for ref in refs[1:]:
        total = total + ref[...].astype(F32)
    return total


def middle_kernel(plan, parts, level, gain_level, *refs):
    part_refs, (base_ref, bias_ref, gain_ref, shift_ref, rows_ref, piece_ref) = (
        refs[:parts],
        refs[parts:],
    )
    rows = base_ref[...] + add_parts(part_refs) + bias_ref[level : level + 1, :]
    rows_ref[...] = rows
    piece_ref[...] = normed_piece(plan, rows, gain_ref, shift_ref, gain_level)


def finish_kernel(plan, parts, level, *refs):
    part_refs, (base_ref, bias_ref, gene_ref, pre_ref) = refs[:parts], refs[parts:]
    rows = base_ref[...] + add_parts(part_refs) + bias_ref[level : level + 1, :]
    gene_ref[...] = rows[: plan.gene_rows].T
    pre_ref[...] = rows[plan.gene_rows :]


def norm_back(plan, parts, level, refs):
    part_refs, (x_ref, gain_ref, base_ref) = refs[:parts], refs[parts : parts + 3]
    grad_norm = unspread(plan, add_parts(part_refs))
    unit, inverse = normed_of(x_ref[...])
    scaled = grad_norm * gain_ref[level : level + 1, :]
    return base_ref[...] + inverse * (
        scaled
        - jnp.mean(scaled, axis=-1, keepdims=True)
        - unit * jnp.mean(scaled * unit, axis=-1, keepdims=True)
    )


def back_kernel(plan, parts, level, *refs):
    grad = norm_back(plan, parts, level, refs)
    grad_ref, piece_ref = refs[parts + 3 :]
    grad_ref[...] = grad
    piece_ref[...] = real_rows(plan, grad).astype(BF)


def back_end_kernel(plan, parts, level, *refs):
    grad = norm_back(plan, parts, level, refs)
    gene_ref, pre_ref = refs[parts + 3 :]
    gene_ref[...] = grad[: plan.gene_rows].T
    pre_ref[...] = grad[plan.gene_rows :]


def cot_kernel(plan, gene_ref, pre_ref, rows_ref, piece_ref):
    rows = jnp.concatenate([gene_ref[...].T, pre_ref[...]], 0)
    rows_ref[...] = rows
    piece_ref[...] = real_rows(plan, rows).astype(BF)


def query_chunks(plan):
    both, genes = 2 * plan.gene_rows, 2 * plan.genes
    chunks = []
    for chip in range(0, plan.chips, 2):
        blocks = [(genes, 2 * plan.prefix, False)]
        blocks += [
            (start, both, start >= chip * both) for start in range(0, (chip + 2) * both, both)
        ]
        chunks.append((chip * plan.gene_rows, both, blocks))
    chunks.append((plan.genes, plan.prefix, [(genes, 2 * plan.prefix, True)]))
    return chunks


def masked(plan, scores, start, diagonal, core):
    in_prefix = start == 2 * plan.genes
    holes = in_prefix and plan.pre_rows < plan.pre_block
    if not (diagonal or holes):
        return scores
    key_at = lax.broadcasted_iota(jnp.int32, scores.shape, 0)
    query_at = lax.broadcasted_iota(jnp.int32, scores.shape, 1)
    keep = None
    if diagonal:
        block = plan.pre_block if in_prefix else plan.gene_rows
        inner = lax.rem(query_at, block)
        before = 0 if in_prefix else start % (4 * block)
        keep = key_at <= 2 * query_at - inner + core * block - before
    if holes:
        real = lax.rem(key_at, plan.pre_block) < plan.pre_rows
        keep = real if keep is None else keep & real
    return jnp.where(keep, scores, -jnp.inf)


def collect(plan, chip, piece_refs, whole_ref, pre_ref):
    for at, ref in enumerate(piece_refs):
        owner = chip ^ at
        whole_ref[aligned(owner, plan.gene_rows), :] = ref[: plan.gene_rows, :]
        pre_ref[aligned(owner, plan.pre_block), :] = ref[plan.gene_rows :, :].astype(F32)
    whole_ref[plan.genes :, :] = pre_ref[...].astype(BF)


def collect_weight(plan, me, part_refs, weight_ref):
    for at, ref in enumerate(part_refs):
        weight_ref[aligned(me ^ at, plan.part), :] = ref[...]


def collect_own(plan, me, part_refs, cut_refs, own_ref, weight_ref):
    collect_weight(plan, me, part_refs, own_ref if plan.whole else weight_ref)
    if not plan.whole:
        own_ref[...] = dot(weight_ref[...], cut_refs[0][...]).astype(BF)


def give_blocks(plan, chip, block_refs, rows_ref, weight, weight_dim, pre_ref):
    pre_ref[...] = dot(rows_ref[plan.genes :, :], weight, 1, weight_dim)
    for at, ref in enumerate(block_refs):
        owner = chip ^ at
        ref[: plan.gene_rows, :] = dot(
            rows_ref[aligned(owner, plan.gene_rows), :], weight, 1, weight_dim
        ).astype(BF)
        ref[plan.gene_rows :, :] = pre_ref[aligned(owner, plan.pre_block), :].astype(BF)


def project_kernel(plan, me_ref, *refs):
    chips, groups = plan.chips, plan.groups
    pieces, parts, refs = refs[:chips], refs[chips : chips + groups], refs[chips + groups :]
    bias_ref, query_ref, pair_ref, pre_ref, low_ref, weight_ref = refs
    collect(plan, me_ref[1], pieces, low_ref, pre_ref)
    collect_weight(plan, me_ref[0], parts, weight_ref)
    query_ref[...] = jnp.zeros_like(query_ref)
    pair_ref[...] = jnp.zeros_like(pair_ref)
    for rows in plan.halves(plan.rows):
        narrow = (dot(low_ref[rows, :], weight_ref[...]) + bias_ref[...]).astype(BF)
        for head in range(plan.window):
            for block, (ref, to) in enumerate(((query_ref, 0), (pair_ref, 0), (pair_ref, HALF))):
                to += head * LANES
                begin = block * plan.wide + head * HEAD_DIM
                ref[rows, to : to + HEAD_DIM] = narrow[:, begin : begin + HEAD_DIM]


def order_pairs(plan, core, mine_ref, other_ref, keys_ref, pre_ref):
    for chip in range(plan.chips):
        for ref, place in ((mine_ref, 2 * chip + core), (other_ref, 2 * chip + 1 - core)):
            genes = slice(chip * plan.gene_rows, (chip + 1) * plan.gene_rows)
            keys_ref[aligned(place, plan.gene_rows), :] = ref[genes, :]
            prefix = slice(
                plan.genes + chip * plan.pre_block, plan.genes + (chip + 1) * plan.pre_block
            )
            pre_ref[aligned(place, plan.pre_block), :] = ref[prefix, :].astype(F32)
    keys_ref[2 * plan.genes :, :] = pre_ref[...].astype(BF)


def attend_kernel(plan, me_ref, *refs):
    query_ref, mine_ref, other_ref, out_weight_ref, padded_ref, lse_ref = refs[:6]
    blocks = refs[6 : 6 + plan.chips]
    key_pre_ref, out_pre_ref, keys_ref, turned_ref, score_ref = refs[6 + plan.chips :]
    core = me_ref[2]
    order_pairs(plan, core, mine_ref, other_ref, keys_ref, key_pre_ref)
    for head in range(plan.window):
        at = slice(LANES * head, LANES * (head + 1))
        turned_ref[...] = keys_ref[:, at].astype(F32).T.astype(BF)
        for first, count, key_parts in query_chunks(plan):
            query = query_ref[first : first + count, at]
            top = None
            for start, size, diagonal in key_parts:
                scores = dot(keys_ref[start : start + size, at], query, 1, 1)
                scores = masked(plan, scores, start, diagonal, core)
                score_ref[start : start + size, :count] = scores
                high = jnp.max(scores, axis=0, keepdims=True)
                top = high if top is None else jnp.maximum(top, high)
            top = top * SCALE2
            total, mixed = 0.0, 0.0
            for start, size, _ in key_parts:
                weights = jnp.exp2(score_ref[start : start + size, :count] * SCALE2 - top)
                total = total + jnp.sum(weights, axis=0, keepdims=True)
                mixed = mixed + dot(turned_ref[:, start : start + size], weights.astype(BF))
            padded_ref[first : first + count, at] = (mixed * (1.0 / total)).T.astype(BF)
            lse_ref[head, :, first : first + count] = top + jnp.log2(total)
    give_blocks(plan, me_ref[1], blocks, padded_ref, out_weight_ref[...], 0, out_pre_ref)


def attend_back_kernel(plan, me_ref, *refs):
    pieces, refs = refs[: plan.chips], refs[plan.chips :]
    out_weight_ref, query_ref, own_pair_ref, other_pair_ref, lse_ref = refs[:5]
    query_grad_ref, mine_ref, other_ref, out_bias_ref = refs[5:9]
    pre_ref, key_pre_ref, low_ref, keys_ref, grad_ref, turned_ref, prob_ref, pgrad_ref, pair_ref = refs[9:]
    core = me_ref[2]
    collect(plan, me_ref[1], pieces, low_ref, pre_ref)
    order_pairs(plan, core, own_pair_ref, other_pair_ref, keys_ref, key_pre_ref)
    out_bias_ref[...] = jnp.sum(low_ref[...].astype(F32), axis=0, keepdims=True)
    for rows in plan.halves(plan.rows):
        grad_ref[rows, :] = dot(low_ref[rows, :], out_weight_ref[...], 1, 1).astype(BF)
    lane = lax.broadcasted_iota(jnp.int32, (1, LANES), 1)
    pair_scale = jnp.where(lane < HALF, SCALE, 1.0)
    for head in range(plan.window):
        at = slice(LANES * head, LANES * (head + 1))
        turned_ref[...] = keys_ref[:, at].astype(F32).T.astype(BF)
        pair_ref[...] = jnp.zeros_like(pair_ref)
        for first, count, key_parts in query_chunks(plan):
            query = query_ref[first : first + count, at]
            grad = grad_ref[first : first + count, at]
            both = jnp.concatenate([grad, query], 0)
            lse = lse_ref[head, :, first : first + count]
            delta = 0.0
            for start, size, diagonal in key_parts:
                pair = keys_ref[start : start + size, at]
                scores = masked(plan, dot(pair, query, 1, 1), start, diagonal, core)
                probs = jnp.exp2(scores * SCALE2 - lse)
                prob_grad = dot(pair, grad, 1, 1)
                delta = delta + jnp.sum(probs * prob_grad, axis=0, keepdims=True)
                prob_ref[start : start + size, :count] = probs
                pgrad_ref[start : start + size, :count] = prob_grad
            query_grad = 0.0
            for start, size, _ in key_parts:
                probs = prob_ref[start : start + size, :count]
                score_grad = (probs * (pgrad_ref[start : start + size, :count] - delta)).astype(BF)
                pair_ref[start : start + size, :] += dot(
                    jnp.concatenate([probs.astype(BF), score_grad], 1), both
                )
                query_grad = query_grad + dot(turned_ref[:, start : start + size], score_grad)
            query_grad_ref[first : first + count, at] = (query_grad.T * SCALE).astype(BF)
        for chip in range(plan.chips):
            for ref, place in ((mine_ref, 2 * chip + core), (other_ref, 2 * chip + 1 - core)):
                genes = slice(chip * plan.gene_rows, (chip + 1) * plan.gene_rows)
                ref[genes, at] = (pair_ref[aligned(place, plan.gene_rows), :] * pair_scale).astype(ref.dtype)
                prefix = slice(
                    plan.genes + chip * plan.pre_block, plan.genes + (chip + 1) * plan.pre_block
                )
                place = pl.ds(
                    pl.multiple_of(2 * plan.genes + place * plan.pre_block, plan.pre_block), plan.pre_block
                )
                ref[prefix, at] = (pair_ref[place, :] * pair_scale).astype(ref.dtype)


def project_back_kernel(plan, me_ref, *refs):
    groups = plan.groups
    query_grad_ref, mine_ref, other_ref = refs[:3]
    parts, refs = refs[3 : 3 + groups], refs[3 + groups :]
    choices, refs = ([], refs) if plan.whole else (refs[:2], refs[2:])
    qkv_grad_ref, bias_ref = refs[:2]
    blocks, (pre_ref, own_ref, weight_ref) = refs[2 : 2 + plan.chips], refs[2 + plan.chips :]
    collect_own(plan, me_ref[0], parts, choices[1:], own_ref, weight_ref)
    for rows in plan.halves(plan.rows):
        pairs = (mine_ref[rows, :].astype(F32) + other_ref[rows, :].astype(F32)).astype(BF)
        if not plan.whole:
            select_ref = choices[0]
            qkv_grad_ref[rows, :] = (
                dot(query_grad_ref[rows, :], select_ref[: plan.lanes, :])
                + dot(pairs, select_ref[plan.lanes :, :])
            ).astype(BF)
            continue
        queries = query_grad_ref[rows, :]
        for head in range(plan.window):
            for block, (value, at) in enumerate(((queries, 0), (pairs, 0), (pairs, HALF))):
                at += head * LANES
                to = block * plan.wide + head * HEAD_DIM
                qkv_grad_ref[rows, to : to + HEAD_DIM] = value[:, at : at + HEAD_DIM]
    bias_ref[...] = jnp.sum(qkv_grad_ref[...].astype(F32), axis=0, keepdims=True)
    give_blocks(plan, me_ref[1], blocks, qkv_grad_ref, own_ref[...], 1, pre_ref)


ROOT = math.sqrt(2.0 / math.pi)
CUBE = 0.044715


def stack_pieces(plan, pieces, low_ref):
    size = plan.step_rows
    for at, ref in enumerate(pieces):
        low_ref[at * size : at * size + plan.own_rows, :] = ref[...]
        if plan.own_rows < size:
            low_ref[at * size + plan.own_rows : (at + 1) * size, :] = jnp.zeros(
                (size - plan.own_rows, low_ref.shape[1]), BF
            )


def collect_down(plan, core, mine_ref, other_ref, down_ref):
    if plan.hidden % 16 == 0:
        down_ref[aligned(core, plan.hidden), :] = mine_ref[...]
        down_ref[aligned(1 - core, plan.hidden), :] = other_ref[...]
        return
    mine, other = mine_ref[...].astype(F32), other_ref[...].astype(F32)
    halves = [jnp.where(core == 0, mine, other), jnp.where(core == 0, other, mine)]
    down_ref[...] = jnp.concatenate(halves, 0).astype(BF)


def lift_kernel(plan, me_ref, *refs):
    chips, groups = plan.chips, plan.groups
    pieces, parts, refs = refs[:chips], refs[chips : chips + groups], refs[chips + groups :]
    bias_ref, mine_ref, other_ref = refs[:3]
    blocks, (low_ref, up_ref, down_ref) = refs[3 : 3 + chips], refs[3 + chips :]
    collect_weight(plan, me_ref[0], parts, up_ref)
    stack_pieces(plan, pieces, low_ref)
    collect_down(plan, me_ref[2], mine_ref, other_ref, down_ref)
    size = plan.step_rows
    for first in range(0, plan.all_rows, 2 * size):
        rows = slice(first, first + 2 * size)
        pre = dot(low_ref[rows, :], up_ref[...]) + bias_ref[...]
        active = (0.5 * pre * (1.0 + jnp.tanh(ROOT * (pre + CUBE * pre * pre * pre)))).astype(BF)
        lifted = dot(active, down_ref[...])
        for at in range(2):
            blocks[first // size + at][...] = lifted[at * size : at * size + plan.own_rows].astype(BF)


def lift_back_kernel(plan, me_ref, *refs):
    chips, groups = plan.chips, plan.groups
    pieces, grads, refs = refs[:chips], refs[chips : 2 * chips], refs[2 * chips :]
    parts, refs = refs[:groups], refs[groups:]
    bias_ref, mine_ref, other_ref, active_ref, pre_grad_ref, down_bias_ref, up_bias_ref = refs[:7]
    blocks, (low_ref, grad_ref, up_ref, down_ref) = refs[7 : 7 + chips], refs[7 + chips :]
    collect_weight(plan, me_ref[0], parts, up_ref)
    stack_pieces(plan, pieces, low_ref)
    stack_pieces(plan, grads, grad_ref)
    collect_down(plan, me_ref[2], mine_ref, other_ref, down_ref)
    size = plan.step_rows
    down_bias_ref[...] = jnp.sum(grad_ref[...].astype(F32), axis=0, keepdims=True)
    up_bias = 0.0
    for first in range(0, plan.all_rows, 2 * size):
        rows = slice(first, first + 2 * size)
        pre = dot(low_ref[rows, :], up_ref[...]) + bias_ref[...]
        act_grad = dot(grad_ref[rows, :], down_ref[...], 1, 1)
        square = pre * pre
        turn = jnp.tanh(ROOT * pre * (1.0 + CUBE * square))
        active_ref[rows, :] = (0.5 * pre * (1.0 + turn)).astype(BF)
        slope = 0.5 * (1.0 + turn) + (0.5 * ROOT) * pre * (1.0 - turn * turn) * (1.0 + 3.0 * CUBE * square)
        pre_grad = (act_grad * slope).astype(BF)
        pre_grad_ref[rows, :] = pre_grad
        up_bias = up_bias + jnp.sum(pre_grad.astype(F32), axis=0, keepdims=True)
        norm_grad = dot(pre_grad, up_ref[...], 1, 1)
        for at in range(2):
            blocks[first // size + at][...] = norm_grad[at * size : at * size + plan.own_rows].astype(BF)
    up_bias_ref[...] = up_bias


def send_kernel(plan, level, starts, width, me_ref, weight_ref, *refs):
    outs, (stack_ref,) = refs[: plan.chips], refs[plan.chips :]
    for to, begins in enumerate(starts):
        for at, begin in enumerate(begins):
            stack_ref[to, : plan.cols, at * width : (at + 1) * width] = weight_ref[
                level, :, begin : begin + width
            ]
        if plan.cols < plan.part:
            stack_ref[to, plan.cols :, :] = jnp.zeros(
                (plan.part - plan.cols, stack_ref.shape[2]), BF
            )
    for at, ref in enumerate(outs):
        ref[...] = stack_ref[me_ref[1] ^ at]


def norm_weight_grad(plan, left_ref, right_ref, weight_ref, sums_ref, vector_ref, whole_ref):
    width = right_ref.shape[1]
    step = 2 * plan.part
    for first in range(0, plan.features, step):
        rows = slice(first, first + step)
        product = dot(left_ref[:, rows], right_ref[...], 0, 0)
        weight = weight_ref[rows, :].astype(F32)
        shift_grad = jnp.sum(weight * sums_ref[...], axis=1, keepdims=True)
        both = jnp.sum(weight * product, axis=1, keepdims=True)
        turned = vector_ref[:, rows].T
        gain_grad = (both - turned[:, 0:1] * shift_grad) / turned[:, 1:2]
        whole_ref[rows, :width] = product
        whole_ref[rows, width : width + 2] = jnp.concatenate([shift_grad, gain_grad], 1)


def give_parts(plan, me, whole_ref, mine_ref, other_ref):
    width = whole_ref.shape[1]
    for at in range(plan.chips):
        owner = me ^ (2 * at)
        mine_ref[at, :, :width] = whole_ref[aligned(owner, plan.part), :].astype(BF)
        other_ref[at, :, :width] = whole_ref[aligned(owner ^ 1, plan.part), :].astype(BF)


def lift_grad_kernel(plan, me_ref, *refs):
    chips, groups = plan.chips, plan.groups
    pieces, grads, refs = refs[:chips], refs[chips : 2 * chips], refs[2 * chips :]
    parts, refs = refs[:groups], refs[groups:]
    active_ref, pre_grad_ref, sums_ref, vector_ref, up_mine, up_other, down_mine, down_other = refs[:8]
    low_ref, grad_ref, up_ref, whole_ref, down_ref = refs[8:]
    core = me_ref[2]
    stack_pieces(plan, pieces, low_ref)
    collect_weight(plan, me_ref[0], parts, up_ref)
    norm_weight_grad(plan, low_ref, pre_grad_ref, up_ref, sums_ref, vector_ref, whole_ref)
    give_parts(plan, me_ref[0], whole_ref, up_mine, up_other)
    stack_pieces(plan, grads, grad_ref)
    for rows in plan.halves(plan.chip_hidden):
        down_ref[rows, :] = dot(active_ref[:, rows], grad_ref[...], 0, 0)
    size = plan.hidden // 4
    filler = jnp.zeros((down_mine.shape[1] - size, D), F32)
    for at in range(4):
        first = down_ref[at * size : (at + 1) * size, :]
        second = down_ref[plan.hidden + at * size : plan.hidden + (at + 1) * size, :]
        for ref, rows in (
            (down_mine, jnp.where(core == 0, first, second)),
            (down_other, jnp.where(core == 0, second, first)),
        ):
            ref[at] = jnp.concatenate([rows, filler], 0).astype(BF)


def attend_grad_kernel(plan, riding, me_ref, *refs):
    chips, groups = plan.chips, plan.groups
    pieces, grads, refs = refs[:chips], refs[chips : 2 * chips], refs[2 * chips :]
    parts, refs = refs[:groups], refs[groups:]
    choices, refs = ([], refs) if plan.whole else (refs[:2], refs[2:])
    mixed_ref, qkv_grad_ref, sums_ref, vector_ref, small_ref, mine_ref, other_ref = refs[:7]
    low_ref, grad_ref, pre_ref, grad_pre_ref, own_ref, weight_ref, whole_ref, out_ref = refs[-8:]
    core = me_ref[2]
    collect(plan, me_ref[1], pieces, low_ref, pre_ref)
    collect_own(plan, me_ref[0], parts, choices[1:], own_ref, weight_ref)
    norm_weight_grad(plan, low_ref, qkv_grad_ref, own_ref, sums_ref, vector_ref, whole_ref)
    give_parts(plan, me_ref[0], whole_ref, mine_ref, other_ref)
    collect(plan, me_ref[1], grads, grad_ref, grad_pre_ref)
    if plan.whole:
        for head in range(plan.window):
            product = dot(mixed_ref[:, head * LANES : (head + 1) * LANES], grad_ref[...], 0, 0)
            out_ref[head * HEAD_DIM : (head + 1) * HEAD_DIM, :] = product[HALF : HALF + HEAD_DIM]
    else:
        own = dot(mixed_ref[...], choices[0][...]).astype(BF)
        out_ref[...] = dot(own, grad_ref[...], 0, 0)
    halves = out_ref[: plan.cols, :], out_ref[plan.cols :, :]
    extra = small_ref.shape[1]
    filler = jnp.zeros((plan.part - plan.cols - extra, D), F32)
    first = whole_ref.shape[1]
    for at, (ref, one, two) in enumerate(((mine_ref, 0, 1), (other_ref, 1, 0))):
        rows = jnp.where(core == 0, halves[one], halves[two])
        rows = jnp.concatenate([rows, small_ref[at], filler], 0).astype(BF)
        if not riding:
            refs[7 + at][...] = rows
            continue
        for chip in range(chips):
            ref[chip, :, first:] = rows[:, chip * plan.chip_cols : (chip + 1) * plan.chip_cols]


def join_down_kernel(plan, *refs):
    parts, out_ref = refs[:LAYERS], refs[LAYERS]
    size = plan.hidden // 4
    for level, ref in enumerate(parts):
        for at in range(4):
            out_ref[level, at * size : (at + 1) * size, :] = ref[at, :size, :].astype(F32)


def join_kernel(plan, blocks, width, me_ref, *refs):
    count = LAYERS * plan.chips
    parts, (out_ref, vector_ref, stack_ref) = refs[:count], refs[count:]
    each = width // blocks
    for level in range(LAYERS):
        for at in range(plan.chips):
            stack_ref[at] = parts[level * plan.chips + at][...]
        vectors = 0.0
        for source in range(plan.chips):
            value = stack_ref[me_ref[1] ^ source].astype(F32)
            for block in range(blocks):
                begin = (block * plan.chips + source) * each
                out_ref[:, level, begin : begin + each] = value[
                    : plan.cols, block * each : (block + 1) * each
                ]
            vectors = vectors + value[:, width : width + 2]
        padded = jnp.concatenate([vectors, jnp.zeros((plan.part, LANES - 2), F32)], 1)
        vector_ref[level] = padded.T[:8]


def body(
    genes,
    prefix,
    cot_genes,
    cot_prefix,
    w_qkv,
    w_out,
    w_up,
    w_down,
    norm1_gain,
    norm1_bias,
    norm2_gain,
    norm2_bias,
    bias_q,
    bias_v,
    bias_out,
    bias_up,
    bias_down,
):
    groups = lax.axis_size("gene")
    cells = lax.axis_size("cell")
    me = lax.axis_index("gene")
    cell = lax.axis_index("cell")
    chip, core = me // 2, me % 2
    plan = Plan(groups, genes.shape[1])
    chips, cols, chip_cols, wide = plan.chips, plan.cols, plan.chip_cols, plan.wide
    hidden, chip_hidden = plan.hidden, plan.chip_hidden
    first_head = jnp.asarray(plan.first_heads, jnp.int32)[chip]
    offset = chip * chip_cols - first_head * HEAD_DIM
    turn = chip if plan.by_links else jnp.zeros_like(chip)
    where = jnp.stack([2 * turn + core, turn, core]).astype(jnp.int32)
    same_core = [[2 * at + one for at in range(chips)] for one in range(2)]
    here = functools.partial

    def after(value, *others):
        return lax.optimization_barrier((value,) + others)[0]

    def after_all(values, *others):
        return list(lax.optimization_barrier((tuple(values), others))[0])

    def together(*lists):
        return [list(got) for got in lax.optimization_barrier(tuple(tuple(x) for x in lists))]

    def swap(value, bits):
        return lax.ppermute(value, "gene", [(at, at ^ bits) for at in range(groups)])

    def to_chips(parts):
        if not plan.by_links:
            got = lax.all_to_all(jnp.stack(parts), "gene", 0, 0, axis_index_groups=same_core)
            return [got[at] for at in range(chips)]
        return [parts[0]] + [swap(parts[at], 2 * at) for at in range(1, chips)]

    def gather(piece):
        if not plan.by_links:
            got = lax.all_gather(piece, "gene", axis=0, axis_index_groups=same_core)
            return [got[at] for at in range(chips)]
        return to_chips([piece] * chips)

    def scatter(blocks):
        if not plan.by_links:
            return [
                lax.psum_scatter(
                    jnp.stack(blocks), "gene", scatter_dimension=0, axis_index_groups=same_core
                )
            ]
        return to_chips(blocks)

    def across(near):
        far = [swap(value, 1) for value in near]
        return [value for pair in zip(near, far) for value in pair]

    class CellSum:
        def __init__(self, mine, other, *steps):
            self.value = (mine.astype(F32) + other.astype(F32)).astype(BF)
            self.steps = list(steps) if cells == 4 else [steps[-1]]
            self.moves = len(steps)
            waiting.append(self)

        def half(self, bit):
            halves = self.value.reshape((2, self.value.shape[0] // 2) + self.value.shape[1:])
            return lax.dynamic_index_in_dim(halves, bit, 0, keepdims=False)

        def move(self):
            if cells != 4:
                return lax.psum(self.value, "cell")
            left = len(self.steps)
            if self.moves == 3:
                inwards, between, outwards = [(0, 1), (3, 2)], [(1, 2), (2, 1)], [(1, 0), (2, 3)]
                return lax.ppermute(self.value, "cell", {3: inwards, 2: between, 1: outwards}[left])
            self.away = 1 if left in (1, 4) else 2
            self.bit = cell // self.away % 2
            value = self.half(1 - self.bit) if left > 2 else self.value
            return lax.ppermute(value, "cell", [(at, at ^ self.away) for at in range(4)])

        def land(self, got):
            left = len(self.steps)
            if cells != 4:
                self.value = got
            elif self.moves == 3 and left == 1:
                self.value = jnp.where((cell == 1) | (cell == 2), self.value, got)
            elif left > 2 or self.moves == 3:
                value = self.value if self.moves == 3 else self.half(self.bit)
                self.value = (value.astype(F32) + got.astype(F32)).astype(BF)
            else:
                first, second = (
                    jnp.where(self.bit == at, self.value, got) for at in range(2)
                )
                self.value = jnp.concatenate([first, second], 0)
            self.steps.pop(0)

    waiting = []

    def beside(step, *lists):
        moving = [item for item in waiting if item.steps and item.steps[0] == step]
        *lists, landed = together(*lists, [item.move() for item in moving])
        for item, got in zip(moving, landed):
            item.land(got)
        return lists

    def send(weight, level, starts, width, *others):
        total = len(starts[0]) * width
        return call(
            here(send_kernel, plan, level, starts, width),
            "send",
            [after(where, *others), weight],
            [shape_of(plan.part, total)] * chips,
            [pltpu.VMEM((chips, plan.part, total), BF)],
            True,
        )

    qkv_starts = [
        [block * D + head * HEAD_DIM for block in range(3)] for head in plan.first_heads
    ]
    up_starts = [[to * chip_hidden] for to in range(chips)]

    def chooser(wanted, there):
        return (wanted[:, None] == there[None, :]).astype(BF)

    def own_of(block, column, real):
        ok = real & (column >= offset) & (column < offset + chip_cols)
        return jnp.where(ok, block * chip_cols + column - offset, -1)

    window_at = jnp.arange(3 * wide)
    own_columns = jnp.arange(3 * chip_cols)
    cut = chooser(own_of(window_at // wide, window_at % wide, True), own_columns)
    lanes = jnp.arange(2 * plan.lanes)
    inner = lanes % LANES
    is_pair = lanes >= plan.lanes
    block = jnp.where(is_pair, 1 + inner // HALF, 0)
    inner = jnp.where(is_pair, inner % HALF, inner)
    column = (lanes % plan.lanes) // LANES * HEAD_DIM + inner
    select = chooser(own_of(block, column, inner < HEAD_DIM), own_columns)
    at_out = jnp.arange(plan.lanes)
    inner = at_out % LANES - HALF
    out_col = (at_out // LANES) * HEAD_DIM + inner
    out_ok = (inner >= 0) & (inner < HEAD_DIM)
    out_select = chooser(own_of(0, out_col, out_ok), jnp.arange(chip_cols))

    def out_windows():
        if plan.by_links:
            rows = jnp.concatenate([w_out, swap(w_out, 1)], 1)
            own = jnp.arange(cols)
            owner = jnp.concatenate([me * cols + own, (me ^ 1) * cols + own])
        else:
            rows = lax.all_gather(w_out, "gene", axis=1, tiled=True)
            owner = jnp.arange(D)
        wanted = jnp.where(out_ok, first_head * HEAD_DIM + out_col, -1)
        is_own = (out_col >= offset) & (out_col < offset + chip_cols)
        picks = [chooser(wanted, owner)]
        if not plan.whole:
            picks.append(chooser(jnp.where(is_own, wanted, -1), owner))
        got = [[dot(pick, rows[level]).astype(BF) for level in range(LAYERS)] for pick in picks]
        return got[0], got[-1]

    def window_of(vec):
        return lax.dynamic_slice_in_dim(vec, first_head * HEAD_DIM, wide, 1)

    def norm_vectors(token):
        every = jnp.stack([norm1_bias, norm1_gain, norm2_bias, norm2_gain])
        every = after(every, token).reshape(2, 2, LAYERS, groups, cols)
        every = jnp.pad(every, ((0, 0),) * 4 + ((0, plan.part - cols),), constant_values=1.0)
        every = every.transpose(0, 2, 1, 3, 4).reshape(2 * LAYERS, 2, plan.features)
        every = jnp.pad(every, ((0, 0), (0, 6), (0, 0)))
        return [every[at] for at in range(2 * LAYERS)]

    rows_f32 = shape_of(plan.own_rows, D, dtype=F32)
    normed_like = shape_of(plan.own_rows, plan.features)
    grad_like = shape_of(plan.own_rows, D)
    row_blocks = [grad_like] * chips
    feature_blocks = [normed_like] * chips
    vector = shape_of(1, D, dtype=F32)
    ends_like = [
        shape_of(D, plan.gene_rows, dtype=F32),
        shape_of(plan.pre_block, D, dtype=F32),
    ]

    own_prefix = lax.dynamic_slice_in_dim(prefix[0], me * plan.pre_rows, plan.pre_rows, 0)
    filler = ((0, plan.pre_block - plan.pre_rows), (0, 0))
    rows, piece = call(
        here(begin_kernel, plan),
        "begin",
        [genes[0].T, jnp.pad(own_prefix, filler), norm1_gain, norm1_bias],
        [rows_f32, normed_like],
    )
    qkv_parts, up_parts = [None] * LAYERS, [None] * LAYERS
    qkv_sent = send(w_qkv, 0, qkv_starts, wide, piece)
    pieces, near = gather(piece), to_chips(qkv_sent)
    token = qkv_sent[-1]
    up_sent = send(w_up, 0, up_starts, chip_hidden, token)
    qkv_biases = jnp.concatenate(
        [window_of(bias_q), jnp.zeros((LAYERS, wide), F32), window_of(bias_v)], 1
    )
    windows, out_weights = out_windows()
    pieces, near, up_sent, _ = together(
        pieces, near, up_sent, [qkv_biases] + windows + out_weights
    )
    up_biases = lax.dynamic_slice_in_dim(bias_up, chip * chip_hidden, chip_hidden, 1)
    (qkv_parts[0],) = together(across(near))

    saved, downs = [], []
    for level in range(LAYERS):
        last = level + 1 == LAYERS
        if level:
            (pieces, far) = together(gather(piece), across(near[chips // 2 :]))
            qkv_parts[level] = qkv_far + far
        up_near = to_chips(after_all(up_sent, *pieces, *qkv_parts[level]))
        low_one = pieces
        query, pair = call(
            here(project_kernel, plan),
            "project",
            [where] + pieces + qkv_parts[level] + [qkv_biases[level : level + 1]],
            [shape_of(plan.rows, plan.lanes), shape_of(plan.rows, plan.lanes)],
            [
                pltpu.VMEM((plan.prefix, plan.features), F32),
                pltpu.VMEM((plan.rows, plan.features), BF),
                pltpu.VMEM((plan.features, 3 * wide), BF),
            ],
            True,
        )
        other_pair = swap(pair, 1)
        own_down = after(w_down, pair)[level]
        other_down = swap(own_down, 1)
        if not last:
            qkv_sent = send(w_qkv, level + 1, qkv_starts, wide, pair)
            up_sent = send(w_up, level + 1, up_starts, chip_hidden, pair)
            other_pair = after(other_pair, qkv_sent[-1], up_sent[-1])
        outs = call(
            here(attend_kernel, plan),
            "attend",
            [where, query, pair, other_pair, out_weights[level]],
            [
                shape_of(plan.rows, plan.lanes),
                shape_of(plan.window, 1, plan.rows, dtype=F32),
            ]
            + row_blocks,
            [
                pltpu.VMEM((2 * plan.prefix, plan.lanes), F32),
                pltpu.VMEM((plan.prefix, D), F32),
                pltpu.VMEM((2 * plan.rows, plan.lanes), BF),
                pltpu.VMEM((LANES, 2 * plan.rows), BF),
                pltpu.VMEM((2 * plan.rows, 2 * plan.gene_rows), F32),
            ],
            True,
        )
        outs, up_near, (own_down, other_down) = together(outs, up_near, [own_down, other_down])
        downs.append([own_down, other_down])
        mixed, lse = outs[:2]
        parts, up_far = together(scatter(outs[2:]), across(up_near[: chips // 2]))
        middle, piece = call(
            here(middle_kernel, plan, len(parts), level, level),
            "middle",
            parts + [rows, bias_out, norm2_gain, norm2_bias],
            [rows_f32, normed_like],
        )
        if last:
            cot_grad, cot_piece = call(
                here(cot_kernel, plan),
                "cotangent",
                [after(cot_genes[0].T, piece), jnp.pad(cot_prefix[0], filler)],
                [rows_f32, grad_like],
            )
            spare = [cot_grad, cot_piece]
        else:
            spare = []
        pieces, far, spare = together(gather(piece), across(up_near[chips // 2 :]), spare)
        up_parts[level] = up_far + far
        if last:
            cot_grad, cot_piece = spare
            near = gather(after(cot_piece, *pieces))
        else:
            near = to_chips(after_all(qkv_sent, *pieces))
        low_two = pieces
        blocks = call(
            here(lift_kernel, plan),
            "lift",
            [where]
            + pieces
            + up_parts[level]
            + [up_biases[level : level + 1]] + downs[level],
            row_blocks,
            [
                pltpu.VMEM((plan.all_rows, plan.features), BF),
                pltpu.VMEM((plan.features, chip_hidden), BF),
                pltpu.VMEM((chip_hidden, D), BF),
            ],
            True,
        )
        blocks, near = together(blocks, near)
        saved.append((rows, low_one, query, pair, other_pair, mixed, lse, middle, low_two))
        if last:
            cot_pieces = near
            last_blocks, last_middle = blocks, middle
        else:
            spare = []
            if level == 0:
                spare = norm_vectors(low_two[0])
            parts, qkv_far, spare = together(scatter(blocks), across(near[: chips // 2]), spare)
            if level == 0:
                vectors = spare
            rows, piece = call(
                here(middle_kernel, plan, len(parts), level, level + 1),
                "next_rows",
                parts + [middle, bias_down, norm1_gain, norm1_bias],
                [rows_f32, normed_like],
            )

    def of_cores(value, size, dim):
        return [
            lax.dynamic_slice_in_dim(value, at * size, size, dim) for at in (core, 1 - core)
        ]

    def messages_of(item, width):
        return [item.value[at, :, :width] for at in range(chips)]

    grad, pieces = cot_grad, cot_pieces
    down_sums, up_sums, qkv_sums = ([None] * LAYERS for _ in range(3))
    long_rows, short_rows, up_rows = [None] * (2 * LAYERS), [None] * (2 * LAYERS), [None] * LAYERS
    extra = -(-LAYERS * (4 * cols + hidden) // D)
    choices = [] if plan.whole else [select, cut]
    out_choices = [] if plan.whole else [out_select, cut]
    stacked = pltpu.VMEM((plan.all_rows, plan.features), BF)
    stacked_grad = pltpu.VMEM((plan.all_rows, D), BF)
    up_room = pltpu.VMEM((plan.features, chip_hidden), BF)
    own_room = pltpu.VMEM((plan.features, 3 * chip_cols), BF)
    window_room = pltpu.VMEM((8, LANES) if plan.whole else (plan.features, 3 * wide), BF)
    for level in reversed(range(LAYERS)):
        rows, low_one, query, pair, other_pair, mixed, lse, middle, low_two = saved[level]
        if level + 1 < LAYERS:
            (pieces,) = beside(f"rows {level}", gather(piece))
        down_grad = pieces
        outs = call(
            here(lift_back_kernel, plan),
            "lift_back",
            [where]
            + low_two
            + pieces
            + up_parts[level]
            + [up_biases[level : level + 1]] + downs[level],
            [
                shape_of(plan.all_rows, chip_hidden),
                shape_of(plan.all_rows, chip_hidden),
                vector,
                shape_of(1, chip_hidden, dtype=F32),
            ]
            + feature_blocks,
            [stacked, stacked_grad, up_room, pltpu.VMEM((chip_hidden, D), BF)],
            True,
        )
        (outs,) = beside(f"lifted {level}", outs)
        if not level:
            outs = after_all(outs, up_sums[1].value)
        active, pre_grad, long_rows[level], up_rows[level] = outs[:4]
        up_mine, up_other, down_mine, down_other = call(
            here(lift_grad_kernel, plan),
            "lift_grad",
            [where]
            + low_two
            + down_grad
            + up_parts[level]
            + [active, pre_grad, up_rows[level], vectors[LAYERS + level]],
            [shape_of(chips, plan.part, chip_hidden + 2)] * 2
            + [shape_of(4, -(-hidden // 64) * 16, D)] * 2,
            [
                stacked,
                stacked_grad,
                up_room,
                pltpu.VMEM((plan.features, chip_hidden + 2), F32),
                pltpu.VMEM((chip_hidden, D), F32),
            ],
            True,
        )
        parts, (up_mine, up_other, down_mine, down_other) = beside(
            f"lift {level}", scatter(outs[4:]), [up_mine, up_other, down_mine, down_other]
        )
        middle_grad, piece = call(
            here(back_kernel, plan, len(parts), level),
            "middle_back",
            parts + [middle, norm2_gain, grad],
            [rows_f32, grad_like],
        )
        (middle_grad, piece, up_got, down_got), = beside(
            f"turn {level}", [middle_grad, piece, swap(up_other, 1), swap(down_other, 1)]
        )
        if level:
            down_sums[level] = CellSum(down_mine, down_got, "attend 1", "project 1", "lifted 0")
            up_sums[level] = CellSum(up_mine, up_got, "project 1", "lifted 0", "turn 0")
        else:
            down_sums[level] = CellSum(down_mine, down_got, "attend 0", "end 1", "end 2")
            up_sums[level] = CellSum(up_mine, up_got, "end 1", "end 2", "end 3")
        (pieces,) = beside(f"middle {level}", gather(piece))
        branch_grad = pieces
        outs = call(
            here(attend_back_kernel, plan),
            "attend_back",
            [where] + pieces + [windows[level], query, pair, other_pair, lse],
            [
                shape_of(plan.rows, plan.lanes),
                shape_of(plan.rows, plan.lanes),
                shape_of(plan.rows, plan.lanes),
                vector,
            ],
            [
                pltpu.VMEM((plan.prefix, D), F32),
                pltpu.VMEM((2 * plan.prefix, plan.lanes), F32),
                pltpu.VMEM((plan.rows, D), BF),
                pltpu.VMEM((2 * plan.rows, plan.lanes), BF),
                pltpu.VMEM((plan.rows, plan.lanes), BF),
                pltpu.VMEM((LANES, 2 * plan.rows), BF),
                pltpu.VMEM((2 * plan.rows, 2 * plan.gene_rows), F32),
                pltpu.VMEM((2 * plan.rows, 2 * plan.gene_rows), F32),
                pltpu.VMEM((2 * plan.rows, LANES), F32),
            ],
            True,
        )
        if level:
            (outs,) = beside("attend 1", outs)
        else:
            up_width, qkv_width = chip_hidden + 2, 3 * chip_cols + 2
            (outs,) = beside("attend 0", outs)
        query_grad, pair_mine, pair_other, long_rows[LAYERS + level] = outs
        outs = call(
            here(project_back_kernel, plan),
            "project_back",
            [where, query_grad, pair_mine, swap(pair_other, 1)] + qkv_parts[level] + choices,
            [shape_of(plan.rows, 3 * chip_cols), shape_of(1, 3 * chip_cols, dtype=F32)]
            + feature_blocks,
            [pltpu.VMEM((plan.prefix, plan.features), F32), own_room, window_room],
            True,
        )
        qkv_grad, qkv_bias = outs[:2]
        short_rows[level] = qkv_bias[:, :chip_cols]
        short_rows[LAYERS + level] = qkv_bias[:, 2 * chip_cols :]
        small = jnp.zeros((2, extra, D), F32)
        if not level:
            long_own = lax.dynamic_slice_in_dim(
                jnp.concatenate(long_rows, 0), chip * chip_cols, chip_cols, 1
            )
            small = [
                jnp.concatenate([vec.reshape(-1) for vec in vecs])
                for vecs in zip(
                    of_cores(long_own, cols, 1),
                    of_cores(jnp.concatenate(short_rows, 0), cols, 1),
                    of_cores(jnp.concatenate(up_rows, 0), hidden, 1),
                )
            ]
            small = jnp.stack(
                [jnp.pad(vec, (0, extra * D - vec.size)).reshape(extra, D) for vec in small]
            )
        width = 3 * chip_cols + 2
        made = call(
            here(attend_grad_kernel, plan, bool(level)),
            "attend_grad",
            [where]
            + low_one
            + branch_grad
            + qkv_parts[level]
            + out_choices
            + [mixed, qkv_grad, qkv_bias, vectors[level], small],
            [shape_of(chips, plan.part, width + (chip_cols if level else 0))] * 2
            + [shape_of(plan.part, D)] * (0 if level else 2),
            [
                pltpu.VMEM((plan.rows, plan.features), BF),
                pltpu.VMEM((plan.rows, D), BF),
                pltpu.VMEM((plan.prefix, plan.features), F32),
                pltpu.VMEM((plan.prefix, D), F32),
                own_room,
                window_room,
                pltpu.VMEM((plan.features, 3 * chip_cols + 2), F32),
                pltpu.VMEM((chip_cols, D), F32),
            ],
            True,
        )
        blocks = outs[2:]
        if level:
            parts = scatter(blocks)
            parts, (qkv_mine, qkv_other) = beside("project 1", parts, made)
            grad, piece = call(
                here(back_kernel, plan, len(parts), level),
                "rows_back",
                parts + [rows, norm1_gain, middle_grad],
                [rows_f32, grad_like],
            )
            grad, piece, qkv_got = together([grad, piece, swap(qkv_other, 1)])[0]
            qkv_sums[level] = CellSum(qkv_mine, qkv_got, "lift 0", "attend 0", "end 1")

    (made,) = together(made)
    qkv_mine, qkv_other, out_mine, out_other = made
    qkv_got, out_got = together([swap(qkv_other, 1), swap(out_other, 1)])[0]
    qkv_sums[0] = CellSum(qkv_mine, qkv_got, "end 2", "end 3", "end 4")
    beside("end 1", [qkv_sums[0].value])
    parts, _ = beside("end 2", scatter(after_all(blocks, qkv_sums[0].value)), [up_sums[0].value])
    ends = call(
        here(back_end_kernel, plan, len(parts), 0),
        "rows_back_end",
        parts + [rows, norm1_gain, middle_grad],
        ends_like,
    )
    out_sum = (after(out_mine, parts[0]).astype(F32) + out_got.astype(F32)).astype(BF)
    up_near = to_chips(after_all(messages_of(up_sums[1], up_width), *parts))
    parts, ends, up_near = beside(
        "end 3", scatter(after_all(last_blocks, *parts)), ends, up_near
    )
    result = call(
        here(finish_kernel, plan, len(parts), LAYERS - 1),
        "finish",
        parts + [last_middle, bias_down],
        ends_like,
    )
    near = to_chips(after_all(messages_of(qkv_sums[1], qkv_width), *parts))
    last_up = to_chips(after_all(messages_of(up_sums[0], up_width), *parts))
    def sum_near(value, away):
        if cells != 4:
            return lax.psum(value, "cell") if away == 1 else value
        got = lax.ppermute(value, "cell", [(at, at ^ away) for at in range(cells)])
        return (value.astype(F32) + got.astype(F32)).astype(BF)

    (g_down,) = call(
        here(join_down_kernel, plan),
        "join_down",
        after_all([item.value for item in down_sums], parts[0]),
        [shape_of(LAYERS, hidden, D, dtype=F32)],
    )
    near, last_up, result, (g_down,) = beside("end 4", near, last_up, result, [g_down])
    messages = after_all(messages_of(qkv_sums[0], qkv_width))
    last_near = to_chips(messages)
    (out_sum,) = after_all([out_sum], *messages)
    last_up, up_near = (after_all(values, *messages) for values in (last_up, up_near))
    up_parts = [last_up, up_near]
    def join(parts, blocks, width):
        whole, vectors = call(
            here(join_kernel, plan, blocks, width),
            "join",
            [where] + parts[0] + parts[1],
            [
                shape_of(cols, LAYERS, blocks * D if blocks > 1 else FF, dtype=F32),
                shape_of(LAYERS, 8, plan.part, dtype=F32),
            ],
            [pltpu.VMEM((chips, plan.part, width + 2), BF)],
            scalar=True,
        )
        return whole.transpose(1, 0, 2), vectors[:, 0, :cols], vectors[:, 1, :cols]

    ups = join(up_parts, 1, chip_hidden)
    last_near, (g_up, shift_two, gain_two), (out_sum,) = together(
        last_near, ups, [sum_near(out_sum, 1)]
    )
    out_sum = sum_near(out_sum, 2)
    qkv_parts = [last_near, near]
    g_qkv, shift_one, gain_one = join(qkv_parts, 3, 3 * chip_cols)
    riders = [qkv_sums[1].value[at, : plan.cols, qkv_width:] for at in range(chips)]
    out_sums = [out_sum[:cols], after(jnp.concatenate(riders, 1), last_up[0])]
    small = out_sum[cols : cols + extra].reshape(-1).astype(F32)
    size = LAYERS * cols
    b_down, b_out, b_q, b_v = (small[at * size : (at + 1) * size].reshape(LAYERS, cols) for at in range(4))
    b_up = small[4 * size : 4 * size + LAYERS * hidden].reshape(LAYERS, hidden)

    return (
        result[0].T[None],
        result[1][: plan.pre_rows][None],
        ends[0].T[None],
        ends[1][: plan.pre_rows][None],
        g_qkv,
        jnp.stack(out_sums).astype(F32),
        g_up,
        g_down,
        gain_one,
        shift_one,
        gain_two,
        shift_two,
        b_q,
        b_v,
        b_out,
        b_up,
        b_down,
    )


def solution(mesh):
    rows = P("cell", "gene", None)
    weight = P(None, "gene", None)
    vector = P(None, "gene")
    return jax.shard_map(
        body,
        mesh=mesh,
        in_specs=(rows, P("cell", None, None), rows, rows) + (weight,) * 4 + (P(),) * 9,
        out_specs=(rows,) * 4 + (weight,) * 4 + (vector,) * 9,
        check_vma=False,
    )
```
